128 devices in a mesh: grid: 8 (over x, core), cell: 16 (over z, y).
Axes of the slice: x: 4, y: 4, z: 4, core: 2. Of those that a mesh axis runs over, the one named last changes fastest.
Arguments:
- probes: float32 [16, 8, 524288], P(None, 'grid', 'cell'), may hold values from -180 to 180
- centre: float32 [8, 524288], P('grid', 'cell'), may hold values from 2.5 to 3.5
- lower_coef: float32 [8, 524288], P('grid', 'cell'), may hold values from 0.1 to 1
- upper_coef: float32 [8, 524288], P('grid', 'cell'), may hold values from 0.1 to 1
- donor_cells: int32 [8, 4, 98304], P('grid', None, 'cell'), may hold values from 0 to 32767
- receptor_cells: int32 [8, 98304], P('grid', 'cell'), may hold values from 0 to 32767
- weights: float32 [8, 4, 98304], P('grid', None, 'cell'), may hold values from 0.05 to 0.6
Outputs:
- basis: float32 [16, 8, 524288], P(None, 'grid', 'cell')
- factor: float32 [16, 16], replicated
The draws below stay inside these ranges and needn't reach their ends.
Inputs may be any that keep to these rules, and one draw needn't show every extreme that they name: `donor_cells`: indices within the donor block. `receptor_cells`: indices within the receptor block.
All inputs are finite; a program needn't handle non-finite values.
Results may differ from the reference program's by a relative error of at most 0.00005.
Values sent between devices are 32-bit elements; how exact they have to be, the bound alone decides.
No kernel may reach another device: no remote copies, remote signals or barrier semaphores. Data moves between devices by JAX's collectives and lax.ppermute only.
A program may use at most 320 MiB of HBM per device.

```python
import math
import jax
import jax.numpy as jnp
from jax import lax

PROBES = 16
CB = 32768
FRINGE = 1024
GRIDS = 8
CELLS = 524288
SLOTS = 6144
N_CELL = 16


def draw_probes(key, part):
    key = jax.random.fold_in(key, 11)
    key_base, key_cell, key_row = jax.random.split(key, 3)
    shape = (PROBES, GRIDS, CELLS)
    position = jnp.arange(GRIDS * CELLS, dtype=jnp.float32).reshape(1, GRIDS, CELLS) / jnp.float32(GRIDS * CELLS)
    cell_scale = jnp.exp(math.log(3.0) * position + math.log(10.0) * jax.random.uniform(key_cell, (1, GRIDS, CELLS), jnp.float32))
    row_scale = jnp.exp(math.log(10.0) * jax.random.uniform(key_row, (PROBES, 1, 1), jnp.float32))
    base = jnp.clip(jax.random.normal(key_base, shape, jnp.float32), -6.0, 6.0)
    return (base * cell_scale * row_scale / 10.0).astype(jnp.float32)


def with_ends(result, rng, smallest, largest):
    place = [jax.random.randint(jax.random.fold_in(rng, axis), (), 0, length) for axis, length in enumerate(result.shape)]
    main_axis = result.shape.index(max(result.shape))
    beside = place[:main_axis] + [(place[main_axis] + 1) % result.shape[main_axis]] + place[main_axis + 1:]
    return result.at[tuple(place)].set(smallest).at[tuple(beside)].set(largest)


def levels(stream_key, dims, pieces, least, largest):
    level, own = 1.0, jax.random.fold_in(stream_key, 6)
    for axis_at, parts in pieces:
        heights = jnp.exp(jax.random.uniform(jax.random.fold_in(own, axis_at), (parts,), jnp.float32, least / len(pieces), largest / len(pieces)))
        level = level * jnp.repeat(heights, dims[axis_at] // parts).reshape([-1 if axis == axis_at else 1 for axis in range(len(dims))])
    return level


def setup_inputs(seed: int = 0) -> dict:
    arg_keys = jax.random.split(jax.random.key(seed), 8)
    return {
        "probes": draw_probes(jax.random.fold_in(arg_keys[7], 71), 0),
        "centre": jnp.clip(2.5 + 1.0 * jax.random.uniform(arg_keys[1], (GRIDS, CELLS), jnp.float32) ** levels(arg_keys[1], (GRIDS, CELLS), ((0, 8), (1, 16)), -0.2, 0.2), 2.5, 3.5),
        "lower_coef": jnp.clip(0.1 + 0.9 * jax.random.uniform(arg_keys[2], (GRIDS, CELLS), jnp.float32) ** levels(arg_keys[2], (GRIDS, CELLS), ((0, 8), (1, 16)), -0.2, 0.2), 0.1, 1.0),
        "upper_coef": jnp.clip(0.1 + 0.9 * jax.random.uniform(arg_keys[3], (GRIDS, CELLS), jnp.float32) ** levels(arg_keys[3], (GRIDS, CELLS), ((0, 8), (1, 16)), -0.2, 0.2), 0.1, 1.0),
        "donor_cells": with_ends(jax.random.randint(arg_keys[4], (GRIDS, 4, N_CELL * SLOTS), 0, CB), jax.random.fold_in(arg_keys[4], 1), 0, CB - 1).astype(jnp.int32),
        "receptor_cells": with_ends(jax.random.randint(arg_keys[5], (GRIDS, N_CELL * SLOTS), 0, CB), jax.random.fold_in(arg_keys[5], 1), 0, CB - 1).astype(jnp.int32),
        "weights": jnp.clip(0.05 + 0.55 * jax.random.uniform(arg_keys[6], (GRIDS, 4, N_CELL * SLOTS), jnp.float32) ** levels(arg_keys[6], (GRIDS, 4, N_CELL * SLOTS), ((0, 8), (2, 16)), -0.2, 0.2), 0.05, 0.6),
    }


def forward_op(u, centre, lower_coef, upper_coef):
    padded = jnp.pad(u, ((0, 0), (1, 1)))
    return centre * u - lower_coef * padded[:, :-2] - upper_coef * padded[:, 2:]

def adjoint_op(z, centre, lower_coef, upper_coef):
    upper_pad = jnp.pad(upper_coef * z, ((0, 0), (1, 1)))
    lower_pad = jnp.pad(lower_coef * z, ((0, 0), (1, 1)))
    return centre * z - upper_pad[:, :-2] - lower_pad[:, 2:]

def reference(probes, centre, lower_coef, upper_coef, donor_cells, receptor_cells, weights):
    base = (jnp.arange(GRIDS, dtype=jnp.int32)[:, None] * CELLS + jnp.arange(N_CELL, dtype=jnp.int32)[None, :] * CB).astype(jnp.int32)
    donor_glob = donor_cells.reshape(GRIDS, 4, N_CELL, 2, 3, FRINGE) + base[:, None, :, None, None, None]
    donor_glob = jnp.transpose(donor_glob, (1, 0, 2, 3, 4, 5)).reshape(4, -1)
    recv_home = receptor_cells.reshape(GRIDS, N_CELL, 2, 3, FRINGE) + base[:, :, None, None, None]
    weight_home = weights.reshape(GRIDS, 4, N_CELL, 2, 3, FRINGE)
    recv_grid_rows = []
    weight_grid_rows = []
    for grid_step in (1, 2):
        recv_cols = []
        weight_cols = []
        for cell_step in (-1, 0, 1):
            recv_piece = recv_home[:, :, grid_step - 1, cell_step + 1]
            recv_cols.append(jnp.roll(jnp.roll(recv_piece, -grid_step, 0), -cell_step, 1))
            weight_piece = weight_home[:, :, :, grid_step - 1, cell_step + 1]
            weight_cols.append(jnp.roll(jnp.roll(weight_piece, -grid_step, 0), -cell_step, 2))
        recv_grid_rows.append(jnp.stack(recv_cols, axis=2))
        weight_grid_rows.append(jnp.stack(weight_cols, axis=3))
    recv_glob = jnp.stack(recv_grid_rows, axis=2).reshape(-1).astype(jnp.int32)
    weight_all = jnp.stack(weight_grid_rows, axis=3)
    weight_all = jnp.transpose(weight_all, (1, 0, 2, 3, 4, 5)).reshape(4, -1)

    def one_probe(flat):
        u = flat.reshape(GRIDS, CELLS)
        tangent = forward_op(u, centre, lower_coef, upper_coef).reshape(-1)
        coupled = jnp.sum(weight_all * flat[donor_glob], axis=0)
        tangent = tangent.at[recv_glob].add(coupled)
        adjoint = adjoint_op(tangent.reshape(GRIDS, CELLS), centre, lower_coef, upper_coef).reshape(-1)
        terms = weight_all * tangent[recv_glob][None, :]
        return adjoint.at[donor_glob].add(terms)
    adjoint_all = lax.map(one_probe, probes.reshape(PROBES, -1))
    gram = jnp.dot(adjoint_all, adjoint_all.T, precision=lax.Precision.HIGHEST) / jnp.float32(GRIDS * CELLS)
    factor = jnp.linalg.cholesky(gram)
    basis = jax.scipy.linalg.solve_triangular(factor, adjoint_all, lower=True)
    return (basis.reshape(PROBES, GRIDS, CELLS), factor)
```

```python
import functools

import jax
import jax.numpy as jnp
from jax import lax
from jax.experimental import pallas as pl
from jax.experimental.pallas import tpu as pltpu
from jax.sharding import PartitionSpec as P

f32 = jnp.float32
i32 = jnp.int32
bf16 = jnp.bfloat16

PROBES = 16
GROUPS = 8
ROWS = 4096
LANES = 128
PARTNERS = 6
FRINGE = 1024
SLOTS = PARTNERS * FRINGE
TILES = ROWS // LANES
WAYS = 8
UNROLL = 8

AXES = ("grid", "cell")
PARTNER_OFFSETS = [(d, e) for d in (1, 2) for e in (-1, 0, 1)]

VMEM = pl.BlockSpec(memory_space=pltpu.VMEM)
HBM = pl.BlockSpec(memory_space=pl.ANY)
PARAMS = pltpu.CompilerParams(vmem_limit_bytes=56 << 20)


def aligned(start, size):
    return pl.ds(pl.multiple_of(start, size), size)


def rows_of(start, size):
    return pl.ds(pl.multiple_of(start, 8), size)


def split(x):
    high = x.astype(bf16)
    return high, (x - high.astype(f32)).astype(bf16)


def start_index_copies(rows_hbm, parts, sem):
    count = parts[0].shape[0]
    copies = [
        pltpu.make_async_copy(rows_hbm.at[pl.ds(w * count, count)], parts[w], sem.at[w])
        for w in range(WAYS)
    ]
    for copy in copies:
        copy.start()
    return copies


def gather_rows(table, parts, staged):
    count = parts[0].shape[0]

    def step(j, carry):
        for u in range(UNROLL):
            q = j * UNROLL + u
            for w in range(WAYS):
                row = parts[w][q]
                staged[pl.ds(w * count + q, 1), :] = table[pl.ds(row, 1), :]
        return carry

    lax.fori_loop(0, count // UNROLL, step, 0)


def clear(sums):
    def step(j, carry):
        for total in sums:
            for u in range(4):
                total[rows_of(j * 32 + u * 8, 8), :] = jnp.zeros((8, LANES), f32)
        return carry

    lax.fori_loop(0, ROWS // 32, step, 0)


def add_rows(sums, parts, staged):
    count = parts[0].shape[0]

    def step(j, carry):
        for u in range(UNROLL):
            q = j * UNROLL + u
            for w in range(WAYS):
                row = parts[w][q]
                term = staged[pl.ds(w * count + q, 1), :]
                sums[w][pl.ds(row, 1), :] = sums[w][pl.ds(row, 1), :] + term
        return carry

    lax.fori_loop(0, count // UNROLL, step, 0)


def groups_of(cells, m, offset):
    return jnp.broadcast_to(cells[m : m + 1, aligned(offset, LANES)], (8, LANES)) >> 12


def select_fields(staged, cells, weights, out):
    many = cells.shape[0]
    for k in range(PARTNERS):

        def step(b, carry):
            local = aligned(b * LANES, LANES)
            offset = k * FRINGE + b * LANES
            total = [jnp.zeros((8, LANES), f32)] * 2
            for m in range(many):
                field = staged[aligned(m * SLOTS + offset, LANES), :].T
                group = groups_of(cells, m, offset)
                scale = 1.0 if weights is None else jnp.broadcast_to(weights[k][m : m + 1, local], (8, LANES))
                for g in range(GROUPS):
                    factor = jnp.where(group == g, scale, 0.0)
                    for h in range(2):
                        at = g * PROBES + h * 8
                        total[h] = total[h] + field[at : at + 8, :] * factor
            for h in range(2):
                out[k][h * 8 : h * 8 + 8, local] = total[h]
            return carry

        lax.fori_loop(0, FRINGE // LANES, step, 0)


def spread_fields(messages, cells, weights, staged):
    many = cells.shape[0]
    for k in range(PARTNERS):

        def step(b, carry):
            local = aligned(b * LANES, LANES)
            offset = k * FRINGE + b * LANES
            field = [messages[k][h * 8 : h * 8 + 8, local] for h in range(2)]
            for m in range(many):
                group = groups_of(cells, m, offset)
                scaled = field
                if weights is not None:
                    scale = jnp.broadcast_to(weights[k][m : m + 1, local], (8, LANES))
                    scaled = [part * scale for part in field]
                terms = [jnp.where(group == g, scaled[h], 0.0) for g in range(GROUPS) for h in range(2)]
                staged[aligned(m * SLOTS + offset, LANES), :] = jnp.concatenate(terms, axis=0).T
            return carry

        lax.fori_loop(0, FRINGE // LANES, step, 0)


def fill_ends(padded, low, high):
    lane = lax.broadcasted_iota(i32, (1, LANES), 1)
    before = pltpu.roll(padded[ROWS : ROWS + 8, :], PROBES, 1)[7:8, :]
    after = pltpu.roll(padded[8:16, :], LANES - PROBES, 1)[0:1, :]
    padded[7:8, :] = jnp.where(lane < PROBES, low, before)
    padded[ROWS + 8 : ROWS + 9, :] = jnp.where(lane >= LANES - PROBES, high, after)


def pack_kernel(probes, centre, lower, upper, low, high, table, tangent, c_out, l_out, u_out, padded):
    def packed(ref, height, tile):
        parts = []
        for g in range(GROUPS):
            part = ref[:, aligned(g * ROWS + tile * LANES, LANES)]
            parts.append(part if height == PROBES else jnp.broadcast_to(part, (PROBES, LANES)))
        return jnp.concatenate(parts, axis=0).T

    def step(tile, carry):
        at = aligned(tile * LANES, LANES)
        block = packed(probes, PROBES, tile)
        table[at, :] = block
        padded[rows_of(tile * LANES + 8, LANES), :] = block
        c_out[at, :] = packed(centre, 1, tile)
        l_out[at, :] = packed(lower, 1, tile)
        u_out[at, :] = packed(upper, 1, tile)
        return carry

    lax.fori_loop(0, TILES, step, 0)
    ends = [jnp.broadcast_to(low[...], (PROBES, LANES)), jnp.zeros((96, LANES), f32)]
    ends.append(jnp.broadcast_to(high[...], (PROBES, LANES)))
    ends = jnp.concatenate(ends, axis=0).T[0:1, :]
    fill_ends(padded, ends, ends)

    def stencil(j, carry):
        for u in range(4):
            start = j * 32 + u * 8
            at = rows_of(start, 8)
            tangent[at, :] = (
                c_out[at, :] * padded[rows_of(start + 8, 8), :]
                - l_out[at, :] * padded[pl.ds(start + 7, 8), :]
                - u_out[at, :] * padded[pl.ds(start + 9, 8), :]
            )
        return carry

    lax.fori_loop(0, ROWS // 32, stencil, 0)


def field(height=ROWS):
    return jax.ShapeDtypeStruct((height, LANES), f32)


def pack(probes, centre, lower, upper, low, high):
    return pl.pallas_call(
        pack_kernel,
        out_shape=[field()] * 5,
        in_specs=[VMEM] * 6,
        out_specs=[VMEM] * 5,
        scratch_shapes=[pltpu.VMEM((ROWS + 16, LANES), f32)],
        compiler_params=PARAMS,
        name="pack",
    )(probes, centre, lower, upper, low, high)


def index_scratch(count):
    return [pltpu.SemaphoreType.DMA((WAYS,))] + [pltpu.SMEM((count // WAYS,), i32)] * WAYS


def send_kernel(*refs):
    table, cells, rows_hbm = refs[:3]
    weights = refs[3:9]
    out = refs[9:15]
    staged, sem = refs[15:17]
    parts = refs[17:]
    copies = start_index_copies(rows_hbm, parts, sem)
    for copy in copies:
        copy.wait()
    gather_rows(table, parts, staged)
    select_fields(staged, cells, weights, out)


MESSAGE = jax.ShapeDtypeStruct((PROBES, FRINGE), f32)


def send(table, cells, rows, weights):
    count = 4 * SLOTS
    return pl.pallas_call(
        send_kernel,
        out_shape=[MESSAGE] * PARTNERS,
        in_specs=[VMEM, VMEM, HBM] + [VMEM] * PARTNERS,
        out_specs=[VMEM] * PARTNERS,
        scratch_shapes=[pltpu.VMEM((count, LANES), f32)] + index_scratch(count),
        compiler_params=PARAMS,
        name="send",
    )(table, cells, rows, *weights)


def couple_kernel(*refs):
    base, lower, upper, cells, rows_hbm = refs[:5]
    messages = refs[5:11]
    tangent = refs[11]
    out = refs[12:18]
    first, last = refs[18:20]
    staged, sem = refs[20:22]
    parts = refs[22 : 22 + WAYS]
    sums = refs[22 + WAYS :]
    copies = start_index_copies(rows_hbm, parts, sem)
    clear(sums)
    spread_fields(messages, cells, None, staged)
    for copy in copies:
        copy.wait()
    add_rows(sums, parts, staged)

    def total(j, carry):
        for u in range(4):
            at = rows_of(j * 32 + u * 8, 8)
            value = base[at, :]
            for part in sums:
                value = value + part[at, :]
            tangent[at, :] = value
        return carry

    lax.fori_loop(0, ROWS // 32, total, 0)
    first[...] = lower[0:8, :] * tangent[0:8, :]
    last[...] = upper[ROWS - 8 : ROWS, :] * tangent[ROWS - 8 : ROWS, :]
    gather_rows(tangent, parts, staged)
    select_fields(staged, cells, None, out)


def couple(base, lower, upper, cells, rows, messages):
    return pl.pallas_call(
        couple_kernel,
        out_shape=[field()] + [MESSAGE] * PARTNERS + [field(8)] * 2,
        in_specs=[VMEM] * 4 + [HBM] + [VMEM] * PARTNERS,
        out_specs=[VMEM] * (PARTNERS + 3),
        scratch_shapes=[pltpu.VMEM((SLOTS, LANES), f32)]
        + index_scratch(SLOTS)
        + [pltpu.VMEM((ROWS, LANES), f32)] * WAYS,
        compiler_params=PARAMS,
        name="couple",
    )(base, lower, upper, cells, rows, *messages)


def adjoint_kernel(*refs):
    tangent, centre, lower, upper, low, high, cells, rows_hbm = refs[:8]
    weights = refs[8:14]
    messages = refs[14:20]
    adjoint, gram = refs[20:22]
    staged, sem = refs[22:24]
    parts = refs[24 : 24 + WAYS]
    sums = refs[24 + WAYS : 24 + 2 * WAYS]
    raised, lowered = refs[24 + 2 * WAYS :]
    copies = start_index_copies(rows_hbm, parts, sem)
    clear(sums)
    spread_fields(messages, cells, weights, staged)

    def products(j, carry):
        for u in range(4):
            start = j * 32 + u * 8
            at = rows_of(start, 8)
            value = tangent[at, :]
            raised[rows_of(start + 8, 8), :] = upper[at, :] * value
            lowered[rows_of(start + 8, 8), :] = lower[at, :] * value
        return carry

    lax.fori_loop(0, ROWS // 32, products, 0)
    low_row = pltpu.roll(low[...], PROBES, 1)[7:8, :]
    high_row = pltpu.roll(high[...], LANES - PROBES, 1)[0:1, :]
    fill_ends(raised, low_row, jnp.zeros((1, LANES), f32))
    fill_ends(lowered, jnp.zeros((1, LANES), f32), high_row)
    for copy in copies:
        copy.wait()
    add_rows(sums, parts, staged)
    gram[...] = jnp.zeros((LANES, LANES), f32)

    def total(tile, carry):
        for u in range(LANES // 8):
            start = tile * LANES + u * 8
            at = rows_of(start, 8)
            value = centre[at, :] * tangent[at, :] - raised[pl.ds(start + 7, 8), :] - lowered[pl.ds(start + 9, 8), :]
            for part in sums:
                value = value + part[at, :]
            adjoint[at, :] = value
        block = adjoint[aligned(tile * LANES, LANES), :]
        gram[...] += jnp.dot(block.T, block, precision=lax.Precision.HIGHEST, preferred_element_type=f32)
        return carry

    lax.fori_loop(0, TILES, total, 0)


def adjoint_of(tangent, centre, lower, upper, low, high, cells, rows, weights, messages):
    count = 4 * SLOTS
    return pl.pallas_call(
        adjoint_kernel,
        out_shape=[field(), field(LANES)],
        in_specs=[VMEM] * 7 + [HBM] + [VMEM] * (2 * PARTNERS),
        out_specs=[VMEM] * 2,
        scratch_shapes=[pltpu.VMEM((count, LANES), f32)]
        + index_scratch(count)
        + [pltpu.VMEM((ROWS, LANES), f32)] * WAYS
        + [pltpu.VMEM((ROWS + 16, LANES), f32)] * 2,
        compiler_params=PARAMS,
        name="adjoint",
    )(tangent, centre, lower, upper, low, high, cells, rows, *weights, *messages)


def basis_kernel(gram, adjoint, basis, factor):
    row = lax.broadcasted_iota(i32, (PROBES, 1), 0)
    lane = lax.broadcasted_iota(i32, (PROBES, LANES), 1)
    left = gram[...]
    right = jnp.where(lax.broadcasted_iota(i32, (PROBES, LANES), 0) == lane % PROBES, 1.0, 0.0)
    for j in range(PROBES):
        pivot = left[j : j + 1, j : j + 1]
        ratio = jnp.where(row > j, left[:, j : j + 1] / pivot, 0.0)
        root = jnp.sqrt(pivot)
        left_row, right_row = left[j : j + 1, :], right[j : j + 1, :]
        left = jnp.where(row == j, left_row / root, left - ratio * left_row)
        right = jnp.where(row == j, right_row / root, right - ratio * right_row)
    across = lax.broadcasted_iota(i32, (PROBES, PROBES), 1)
    down = lax.broadcasted_iota(i32, (PROBES, PROBES), 0)
    factor[...] = jnp.where(across >= down, left, 0.0).T
    inverse = jnp.concatenate([right] * GROUPS, axis=0)
    same = lax.broadcasted_iota(i32, (LANES, LANES), 0) // PROBES
    same = same == lax.broadcasted_iota(i32, (LANES, LANES), 1) // PROBES
    high, low = split(jnp.where(same, inverse, 0.0))
    left_side = jnp.concatenate([high, high, low], axis=1)

    def step(tile, carry):
        high, low = split(adjoint[aligned(tile * LANES, LANES), :])
        right_side = jnp.concatenate([high, low, high], axis=1)
        block = lax.dot_general(left_side, right_side, (((1,), (1,)), ((), ())), preferred_element_type=f32)
        for g in range(GROUPS):
            basis[:, aligned(g * ROWS + tile * LANES, LANES)] = block[g * PROBES : (g + 1) * PROBES, :]
        return carry

    lax.fori_loop(0, TILES, step, 0)


def basis_of(gram, adjoint):
    return pl.pallas_call(
        basis_kernel,
        out_shape=[
            jax.ShapeDtypeStruct((PROBES, GROUPS * ROWS), f32),
            jax.ShapeDtypeStruct((PROBES, PROBES), f32),
        ],
        in_specs=[VMEM] * 2,
        out_specs=[VMEM] * 2,
        compiler_params=PARAMS,
        name="basis",
    )(gram, adjoint)


def moved(value, place):
    grids, columns = (lax.axis_size(axis) for axis in AXES)
    route = []
    for g in range(grids):
        for c in range(columns):
            to_g, to_c = place(g, c)
            if 0 <= to_c < columns:
                route.append((g * columns + c, (to_g % grids) * columns + to_c))
    return lax.ppermute(value, AXES, route)


def to_receptors(messages):
    columns = lax.axis_size("cell")
    return [
        moved(message, lambda g, c, d=d, e=e: (g + d, (c + e) % columns))
        for message, (d, e) in zip(messages, PARTNER_OFFSETS)
    ]


def to_donors(messages):
    columns = lax.axis_size("cell")
    return [
        moved(message, lambda g, c, d=d, e=e: (g - d, (c - e) % columns))
        for message, (d, e) in zip(messages, PARTNER_OFFSETS)
    ]


def to_next(value):
    return moved(value, lambda g, c: (g, c + 1))


def to_previous(value):
    return moved(value, lambda g, c: (g, c - 1))


def summed(value):
    value = value + moved(value, lambda g, c: (g ^ 1, c))
    value = value + moved(value, lambda g, c: (g ^ 2, c))
    value = value + moved(value, lambda g, c: ((6 - (g & 6)) | (g & 1), c))
    value = value + moved(value, lambda g, c: (g, c ^ 1))
    value = value + moved(value, lambda g, c: (g, (c & 12) | (3 - (c & 3))))
    value = value + moved(value, lambda g, c: (g, c ^ 4))
    value = value + moved(value, lambda g, c: (g, (12 - (c & 12)) | (c & 3)))
    return value


def body(probes, centre, lower_coef, upper_coef, donor_cells, receptor_cells, weights):
    state = probes[:, 0, :]
    width = state.shape[1]
    donors = donor_cells[0]
    donor_rows = (donors & (ROWS - 1)).reshape(-1)
    receptor_rows = (receptor_cells & (ROWS - 1)).reshape(-1)
    donor_weights = to_donors([weights[0, :, k * FRINGE : (k + 1) * FRINGE] for k in range(PARTNERS)])
    low = to_next(state[:, width - 1 :])
    high = to_previous(state[:, :1])
    table, base, c, l, u = pack(state, centre, lower_coef, upper_coef, low, high)
    messages = to_receptors(send(table, donors, donor_rows, donor_weights))
    outs = couple(base, l, u, receptor_cells, receptor_rows, messages)
    tangent = outs[0]
    messages = to_donors(outs[1:7])
    high = to_previous(outs[7])
    low = to_next(outs[8])
    adjoint, gram = adjoint_of(tangent, c, l, u, low, high, donors, donor_rows, donor_weights, messages)
    gram = sum(gram[g * PROBES : (g + 1) * PROBES, g * PROBES : (g + 1) * PROBES] for g in range(GROUPS))
    cells = lax.axis_size("grid") * lax.axis_size("cell") * width
    gram = summed(gram) / f32(cells)
    basis, factor = basis_of(gram, adjoint)
    return (basis[:, None, :], factor)


def solution(mesh):
    in_specs = (
        P(None, "grid", "cell"),
        P("grid", "cell"),
        P("grid", "cell"),
        P("grid", "cell"),
        P("grid", None, "cell"),
        P("grid", "cell"),
        P("grid", None, "cell"),
    )
    out_specs = (P(None, "grid", "cell"), P())
    return jax.shard_map(body, mesh=mesh, in_specs=in_specs, out_specs=out_specs, check_vma=False)
```

```python
import functools

import jax
import jax.numpy as jnp
from jax import lax
from jax.experimental import pallas as pl
from jax.experimental.pallas import tpu as pltpu
from jax.sharding import PartitionSpec as P

f32 = jnp.float32
i32 = jnp.int32
bf16 = jnp.bfloat16

PROBES = 16
GROUPS = 8
ROWS = 4096
LANES = 128
PARTNERS = 6
FRINGE = 1024
HALF = 3 * FRINGE
SLOTS = PARTNERS * FRINGE
TILES = ROWS // LANES
WAYS = 8
UNROLL = 8

AXES = ("grid", "cell")

VMEM = pl.BlockSpec(memory_space=pltpu.VMEM)
HBM = pl.BlockSpec(memory_space=pl.ANY)


def aligned(start, size):
    return pl.ds(pl.multiple_of(start, size), size)


def rows_of(start, size):
    return pl.ds(pl.multiple_of(start, 8), size)


def split(x):
    high = x.astype(bf16)
    return high, (x - high.astype(f32)).astype(bf16)


def params(limit_mib):
    return pltpu.CompilerParams(vmem_limit_bytes=limit_mib << 20)


def cost(microseconds):
    return pl.CostEstimate(flops=0, transcendentals=0, bytes_accessed=microseconds * 3_000_000)


def resident(*shape):
    return pltpu.VMEM(shape, f32)


def index_scratch(count):
    return [pltpu.SMEM((count // WAYS,), i32)] * WAYS + [pltpu.SemaphoreType.DMA((WAYS,))]


def index_copies(rows_hbm, many, half, parts, sem):
    size = parts[0].shape[0]
    each = WAYS // many
    copies = []
    for w in range(WAYS):
        start = (w // each) * SLOTS + half * HALF + (w % each) * size
        copies.append(pltpu.make_async_copy(rows_hbm.at[pl.ds(start, size)], parts[w], sem.at[w]))
    for copy in copies:
        copy.start()
    return copies


def finish(copies):
    for copy in copies:
        copy.wait()


def gather_rows(table, parts, staged):
    count = parts[0].shape[0]

    def step(j, carry):
        for u in range(UNROLL):
            q = j * UNROLL + u
            for w in range(WAYS):
                row = parts[w][q]
                staged[pl.ds(w * count + q, 1), :] = table[pl.ds(row, 1), :]
        return carry

    lax.fori_loop(0, count // UNROLL, step, 0)


def clear(sums):
    def step(j, carry):
        for total in sums:
            for u in range(4):
                total[rows_of(j * 32 + u * 8, 8), :] = jnp.zeros((8, LANES), f32)
        return carry

    lax.fori_loop(0, ROWS // 32, step, 0)


def add_rows(sums, parts, staged):
    count = parts[0].shape[0]

    def step(j, carry):
        for u in range(UNROLL):
            q = j * UNROLL + u
            for w in range(WAYS):
                row = parts[w][q]
                term = staged[pl.ds(w * count + q, 1), :]
                sums[w][pl.ds(row, 1), :] = sums[w][pl.ds(row, 1), :] + term
        return carry

    lax.fori_loop(0, count // UNROLL, step, 0)


def groups_of(cells, m, offset):
    return jnp.broadcast_to(cells[m : m + 1, aligned(offset, LANES)], (8, LANES)) >> 12


def select_fields(staged, cells, half, weights, out):
    many = cells.shape[0]
    for k in range(3):

        def step(b, carry):
            local = aligned(b * LANES, LANES)
            offset = k * FRINGE + b * LANES
            total = [jnp.zeros((8, LANES), f32)] * 2
            for m in range(many):
                field = staged[aligned(m * HALF + offset, LANES), :].T
                group = groups_of(cells, m, half * HALF + offset)
                scale = 1.0 if weights is None else jnp.broadcast_to(weights[k][m : m + 1, local], (8, LANES))
                for g in range(GROUPS):
                    factor = jnp.where(group == g, scale, 0.0)
                    for h in range(2):
                        at = g * PROBES + h * 8
                        total[h] = total[h] + field[at : at + 8, :] * factor
            for h in range(2):
                out[k][h * 8 : h * 8 + 8, local] = total[h]
            return carry

        lax.fori_loop(0, FRINGE // LANES, step, 0)


def spread_fields(messages, cells, half, weights, staged):
    many = cells.shape[0]
    for k in range(3):

        def step(b, carry):
            local = aligned(b * LANES, LANES)
            offset = k * FRINGE + b * LANES
            field = [messages[k][h * 8 : h * 8 + 8, local] for h in range(2)]
            for m in range(many):
                group = groups_of(cells, m, half * HALF + offset)
                scaled = field
                if weights is not None:
                    scale = jnp.broadcast_to(weights[k][m : m + 1, local], (8, LANES))
                    scaled = [part * scale for part in field]
                terms = [jnp.where(group == g, scaled[h], 0.0) for g in range(GROUPS) for h in range(2)]
                staged[aligned(m * HALF + offset, LANES), :] = jnp.concatenate(terms, axis=0).T
            return carry

        lax.fori_loop(0, FRINGE // LANES, step, 0)


def lanes(shape):
    return lax.broadcasted_iota(i32, shape, len(shape) - 1)


def fill_ends(padded, low, high):
    lane = lanes((1, LANES))
    before = pltpu.roll(padded[ROWS : ROWS + 8, :], PROBES, 1)[7:8, :]
    after = pltpu.roll(padded[8:16, :], LANES - PROBES, 1)[0:1, :]
    padded[7:8, :] = jnp.where(lane < PROBES, low, before)
    padded[ROWS + 8 : ROWS + 9, :] = jnp.where(lane >= LANES - PROBES, high, after)


def each_row_block(step):
    def outer(j, carry):
        for u in range(4):
            step(j * 32 + u * 8)
        return carry

    lax.fori_loop(0, ROWS // 32, outer, 0)


def table_kernel(probes, table, natural, sem):
    copies = [
        pltpu.make_async_copy(probes.at[p], natural.at[pl.ds(p, 1), :], sem.at[p]) for p in range(PROBES)
    ]
    for copy in copies:
        copy.start()
    finish(copies)

    def step(tile, carry):
        parts = [natural[:, aligned(g * ROWS + tile * LANES, LANES)] for g in range(GROUPS)]
        table[aligned(tile * LANES, LANES), :] = jnp.concatenate(parts, axis=0).T
        return carry

    lax.fori_loop(0, TILES, step, 0)


def table_of(probes):
    return pl.pallas_call(
        table_kernel,
        out_shape=resident(ROWS, LANES),
        in_specs=[HBM],
        out_specs=VMEM,
        scratch_shapes=[pltpu.VMEM((PROBES, GROUPS * ROWS), f32), pltpu.SemaphoreType.DMA((PROBES,))],
        compiler_params=params(8),
        cost_estimate=cost(3),
        name="table",
    )(probes)


def rows_kernel(half, table, rows_hbm, staged, *rest):
    parts, sem = rest[:WAYS], rest[WAYS]
    finish(index_copies(rows_hbm, 4, half, parts, sem))
    gather_rows(table, parts, staged)


def rows_at_donors(half, table, rows):
    count = 4 * HALF
    return pl.pallas_call(
        functools.partial(rows_kernel, half),
        out_shape=resident(count, LANES),
        in_specs=[VMEM, HBM],
        out_specs=VMEM,
        scratch_shapes=index_scratch(count),
        compiler_params=params(8),
        cost_estimate=cost(9),
        name="donor_rows",
    )(table, rows)


MESSAGE = jax.ShapeDtypeStruct((PROBES, FRINGE), f32)


def select_kernel(half, staged, cells, *rest):
    select_fields(staged, cells, half, rest[:3], rest[3:6])


def weighted_sums(half, staged, cells, weights):
    return pl.pallas_call(
        functools.partial(select_kernel, half),
        out_shape=[MESSAGE] * 3,
        in_specs=[VMEM] * 5,
        out_specs=[VMEM] * 3,
        compiler_params=params(8),
        cost_estimate=cost(3),
        name="weighted_sums",
    )(staged, cells, *weights)


def forward_kernel(table, centre, lower, upper, low, high, c_out, l_out, u_out, *rest):
    sums, padded = rest[:WAYS], rest[WAYS]

    def step(tile, carry):
        at = aligned(tile * LANES, LANES)
        padded[rows_of(tile * LANES + 8, LANES), :] = table[at, :]
        for ref, out in ((centre, c_out), (lower, l_out), (upper, u_out)):
            parts = [
                jnp.broadcast_to(ref[:, aligned(g * ROWS + tile * LANES, LANES)], (PROBES, LANES))
                for g in range(GROUPS)
            ]
            out[at, :] = jnp.concatenate(parts, axis=0).T
        return carry

    lax.fori_loop(0, TILES, step, 0)
    ends = [jnp.broadcast_to(low[...], (PROBES, LANES)), jnp.zeros((96, LANES), f32)]
    ends.append(jnp.broadcast_to(high[...], (PROBES, LANES)))
    ends = jnp.concatenate(ends, axis=0).T[0:1, :]
    fill_ends(padded, ends, ends)

    def stencil(start):
        at = rows_of(start, 8)
        sums[0][at, :] = (
            c_out[at, :] * padded[rows_of(start + 8, 8), :]
            - l_out[at, :] * padded[pl.ds(start + 7, 8), :]
            - u_out[at, :] * padded[pl.ds(start + 9, 8), :]
        )

    each_row_block(stencil)
    clear(sums[1:])


def forward(table, centre, lower, upper, low, high):
    return pl.pallas_call(
        forward_kernel,
        out_shape=[resident(ROWS, LANES)] * (3 + WAYS),
        in_specs=[VMEM] * 6,
        out_specs=[VMEM] * (3 + WAYS),
        scratch_shapes=[pltpu.VMEM((ROWS + 16, LANES), f32)],
        compiler_params=params(8),
        cost_estimate=cost(7),
        name="forward",
    )(table, centre, lower, upper, low, high)


def couple_kernel(*refs):
    lower, upper, cells, rows_hbm = refs[:4]
    messages = refs[4:10]
    tangent = refs[10 + WAYS]
    out = refs[11 + WAYS : 14 + WAYS]
    first, last = refs[14 + WAYS : 16 + WAYS]
    sums = refs[16 + WAYS : 16 + 2 * WAYS]
    staged = refs[16 + 2 * WAYS : 18 + 2 * WAYS]
    parts = refs[18 + 2 * WAYS :]
    parts, sems = (parts[:WAYS], parts[WAYS + 1 : 2 * WAYS + 1]), (parts[WAYS], parts[2 * WAYS + 1])
    copies = [index_copies(rows_hbm, 1, half, parts[half], sems[half]) for half in range(2)]
    for half in range(2):
        spread_fields(messages[half * 3 : half * 3 + 3], cells, half, None, staged[half])
    for half in range(2):
        finish(copies[half])
        add_rows(sums, parts[half], staged[half])

    def total(start):
        at = rows_of(start, 8)
        value = sums[0][at, :]
        for part in sums[1:]:
            value = value + part[at, :]
        tangent[at, :] = value

    each_row_block(total)
    first[...] = lower[0:8, :] * tangent[0:8, :]
    last[...] = upper[ROWS - 8 : ROWS, :] * tangent[ROWS - 8 : ROWS, :]
    gather_rows(tangent, parts[1], staged[1])
    select_fields(staged[1], cells, 1, None, out)


def couple(lower, upper, cells, rows, messages, sums):
    edge = jax.ShapeDtypeStruct((8, LANES), f32)
    outs = pl.pallas_call(
        couple_kernel,
        out_shape=[resident(ROWS, LANES)] + [MESSAGE] * 3 + [edge] * 2 + [resident(ROWS, LANES)] * WAYS,
        in_specs=[VMEM] * 3 + [HBM] + [VMEM] * (PARTNERS + WAYS),
        out_specs=[VMEM] * (6 + WAYS),
        scratch_shapes=[pltpu.VMEM((HALF, LANES), f32)] * 2 + index_scratch(HALF) * 2,
        input_output_aliases={10 + w: 6 + w for w in range(WAYS)},
        compiler_params=params(8),
        cost_estimate=cost(11),
        name="couple",
    )(lower, upper, cells, rows, *messages, *sums)
    return outs[0], outs[1:4], outs[4], outs[5]


def receptor_kernel(tangent, cells, rows_hbm, *rest):
    out, staged, parts, sem = rest[:3], rest[3], rest[4 : 4 + WAYS], rest[4 + WAYS]
    finish(index_copies(rows_hbm, 1, 0, parts, sem))
    gather_rows(tangent, parts, staged)
    select_fields(staged, cells, 0, None, out)


def at_receptors(tangent, cells, rows):
    return pl.pallas_call(
        receptor_kernel,
        out_shape=[MESSAGE] * 3,
        in_specs=[VMEM, VMEM, HBM],
        out_specs=[VMEM] * 3,
        scratch_shapes=[pltpu.VMEM((HALF, LANES), f32)] + index_scratch(HALF),
        compiler_params=params(8),
        cost_estimate=cost(3),
        name="at_receptors",
    )(tangent, cells, rows)


def transposed_kernel(tangent, centre, lower, upper, *rest):
    sums, raised, lowered = rest[:WAYS], rest[WAYS], rest[WAYS + 1]

    def products(start):
        at = rows_of(start, 8)
        value = tangent[at, :]
        raised[rows_of(start + 8, 8), :] = upper[at, :] * value
        lowered[rows_of(start + 8, 8), :] = lower[at, :] * value

    each_row_block(products)
    nothing = jnp.zeros((1, LANES), f32)
    fill_ends(raised, nothing, nothing)
    fill_ends(lowered, nothing, nothing)

    def stencil(start):
        at = rows_of(start, 8)
        sums[0][at, :] = (
            centre[at, :] * tangent[at, :] - raised[pl.ds(start + 7, 8), :] - lowered[pl.ds(start + 9, 8), :]
        )

    each_row_block(stencil)
    clear(sums[1:])


def transposed(tangent, centre, lower, upper):
    return pl.pallas_call(
        transposed_kernel,
        out_shape=[resident(ROWS, LANES)] * WAYS,
        in_specs=[VMEM] * 4,
        out_specs=[VMEM] * WAYS,
        scratch_shapes=[pltpu.VMEM((ROWS + 16, LANES), f32)] * 2,
        compiler_params=params(8),
        cost_estimate=cost(4),
        name="transposed",
    )(tangent, centre, lower, upper)


def donor_kernel(half, last, *refs):
    cells, rows_hbm = refs[:2]
    weights, messages = refs[2:5], refs[5:8]
    refs = refs[8:]
    if last:
        low, high = refs[:2]
        refs = refs[2:]
    refs = refs[WAYS:]
    if last:
        adjoint, gram = refs[:2]
        refs = refs[2:]
    sums, staged, parts, sem = refs[:WAYS], refs[WAYS], refs[WAYS + 1 : 1 + 2 * WAYS], refs[1 + 2 * WAYS]
    copies = index_copies(rows_hbm, 4, half, parts, sem)
    spread_fields(messages, cells, half, weights, staged)
    finish(copies)
    add_rows(sums, parts, staged)
    if not last:
        return
    lane = lanes((1, LANES))
    low_row = pltpu.roll(low[...], PROBES, 1)[7:8, :]
    high_row = pltpu.roll(high[...], LANES - PROBES, 1)[0:1, :]
    sums[0][0:1, :] = sums[0][0:1, :] - jnp.where(lane < PROBES, low_row, 0.0)
    end = sums[0][ROWS - 1 : ROWS, :]
    sums[0][ROWS - 1 : ROWS, :] = end - jnp.where(lane >= LANES - PROBES, high_row, 0.0)

    def total(tile, product):
        for u in range(LANES // 8):
            at = rows_of(tile * LANES + u * 8, 8)
            value = sums[0][at, :]
            for part in sums[1:]:
                value = value + part[at, :]
            adjoint[at, :] = value
        block = adjoint[aligned(tile * LANES, LANES), :]
        high, low = split(block)
        high_t, low_t = split(block.T)
        left_side = jnp.concatenate([high_t, high_t, low_t], axis=1)
        right_side = jnp.concatenate([high, low, high], axis=0)
        return product + jnp.dot(left_side, right_side, preferred_element_type=f32)

    product = lax.fori_loop(0, TILES, total, jnp.zeros((LANES, LANES), f32))
    group = lanes((PROBES, LANES)) // PROBES
    folded = jnp.zeros((PROBES, LANES), f32)
    for g in range(GROUPS):
        folded = folded + jnp.where(group == g, product[g * PROBES : (g + 1) * PROBES, :], 0.0)
    for shift in (64, 32, 16):
        folded = folded + pltpu.roll(folded, shift, 1)
    gram[...] = folded[:, :PROBES]


def add_at_donors(half, cells, rows, weights, messages, sums, ends=None):
    last = ends is not None
    count = 4 * HALF
    ends = list(ends) if last else []
    out_shape = [resident(ROWS, LANES)] * WAYS
    first_sum = 8 + len(ends)
    if last:
        out_shape = [resident(ROWS, LANES), jax.ShapeDtypeStruct((PROBES, PROBES), f32)] + out_shape
    skip = len(out_shape) - WAYS
    outs = pl.pallas_call(
        functools.partial(donor_kernel, half, last),
        out_shape=out_shape,
        in_specs=[VMEM, HBM] + [VMEM] * (6 + len(ends) + WAYS),
        out_specs=[VMEM] * len(out_shape),
        scratch_shapes=[pltpu.VMEM((count, LANES), f32)] + index_scratch(count),
        input_output_aliases={first_sum + w: skip + w for w in range(WAYS)},
        compiler_params=params(12),
        cost_estimate=cost(12),
        name="add_at_donors",
    )(cells, rows, *weights, *messages, *ends, *sums)
    return outs[:2] if last else outs


def basis_kernel(total_cells, gram, adjoint, basis, factor, natural, sem):
    row = lax.broadcasted_iota(i32, (PROBES, 1), 0)
    left = gram[...] / f32(total_cells)
    right = jnp.where(lax.broadcasted_iota(i32, (PROBES, LANES), 0) == lanes((PROBES, LANES)) % PROBES, 1.0, 0.0)
    for j in range(PROBES):
        pivot = left[j : j + 1, j : j + 1]
        ratio = jnp.where(row > j, left[:, j : j + 1] / pivot, 0.0)
        root = jnp.sqrt(pivot)
        left_row, right_row = left[j : j + 1, :], right[j : j + 1, :]
        left = jnp.where(row == j, left_row / root, left - ratio * left_row)
        right = jnp.where(row == j, right_row / root, right - ratio * right_row)
    down = lax.broadcasted_iota(i32, (PROBES, PROBES), 0)
    factor[...] = jnp.where(lanes((PROBES, PROBES)) >= down, left, 0.0).T
    inverse = jnp.concatenate([right] * GROUPS, axis=0)
    same = lax.broadcasted_iota(i32, (LANES, LANES), 0) // PROBES == lanes((LANES, LANES)) // PROBES
    high, low = split(jnp.where(same, inverse, 0.0))
    left_side = jnp.concatenate([high, high, low], axis=1)

    def step(j, carry):
        for u in range(2):
            tile = j * 2 + u
            high, low = split(adjoint[aligned(tile * LANES, LANES), :])
            right_side = jnp.concatenate([high, low, high], axis=1)
            block = lax.dot_general(left_side, right_side, (((1,), (1,)), ((), ())), preferred_element_type=f32)
            for g in range(GROUPS):
                natural[:, aligned(g * ROWS + tile * LANES, LANES)] = block[g * PROBES : (g + 1) * PROBES, :]
        return carry

    lax.fori_loop(0, TILES // 2, step, 0)
    copies = [
        pltpu.make_async_copy(natural.at[pl.ds(p, 1), :], basis.at[p], sem.at[p]) for p in range(PROBES)
    ]
    for copy in copies:
        copy.start()
    finish(copies)


def basis_of(total_cells, gram, adjoint):
    return pl.pallas_call(
        functools.partial(basis_kernel, total_cells),
        out_shape=[
            jax.ShapeDtypeStruct((PROBES, 1, GROUPS * ROWS), f32),
            jax.ShapeDtypeStruct((PROBES, PROBES), f32),
        ],
        in_specs=[VMEM] * 2,
        out_specs=[HBM, VMEM],
        scratch_shapes=[pltpu.VMEM((PROBES, GROUPS * ROWS), f32), pltpu.SemaphoreType.DMA((PROBES,))],
        compiler_params=params(8),
        cost_estimate=cost(6),
        name="basis",
    )(gram, adjoint)


def moved(value, place):
    grids, columns = (lax.axis_size(axis) for axis in AXES)
    route = []
    for g in range(grids):
        for c in range(columns):
            to_g, to_c = place(g, c)
            if 0 <= to_c < columns:
                route.append((g * columns + c, (to_g % grids) * columns + to_c))
    return lax.ppermute(value, AXES, route)


def to_receptors(half, messages):
    columns = lax.axis_size("cell")
    d = half + 1
    return [
        moved(message, lambda g, c, e=e: (g + d, (c + e) % columns)) for message, e in zip(messages, (-1, 0, 1))
    ]


def to_donors(half, messages):
    columns = lax.axis_size("cell")
    d = half + 1
    return [
        moved(message, lambda g, c, e=e: (g - d, (c - e) % columns)) for message, e in zip(messages, (-1, 0, 1))
    ]


def to_next(value):
    return moved(value, lambda g, c: (g, c + 1))


def to_previous(value):
    return moved(value, lambda g, c: (g, c - 1))


def summed(value):
    value = value + moved(value, lambda g, c: (g ^ 1, c))
    value = value + moved(value, lambda g, c: (g ^ 2, c))
    value = value + moved(value, lambda g, c: ((6 - (g & 6)) | (g & 1), c))
    value = value + moved(value, lambda g, c: (g, c ^ 1))
    value = value + moved(value, lambda g, c: (g, (c & 12) | (3 - (c & 3))))
    value = value + moved(value, lambda g, c: (g, c ^ 4))
    value = value + moved(value, lambda g, c: (g, (12 - (c & 12)) | (c & 3)))
    return value


def body(probes, centre, lower_coef, upper_coef, donor_cells, receptor_cells, weights):
    width = probes.shape[2]
    donors = donor_cells[0]
    donor_rows = (donors & (ROWS - 1)).reshape(-1)
    receptor_rows = (receptor_cells & (ROWS - 1)).reshape(-1)
    donor_weights = [None, None]
    for half in (1, 0):
        pieces = [weights[0, :, (half * 3 + k) * FRINGE : (half * 3 + k + 1) * FRINGE] for k in range(3)]
        donor_weights[half] = to_donors(half, pieces)
    low = to_next(probes[:, 0, width - 1 :])
    high = to_previous(probes[:, 0, :1])
    table = table_of(probes)
    messages = [None, None]
    for half in (1, 0):
        staged = rows_at_donors(half, table, donor_rows)
        messages[half] = to_receptors(half, weighted_sums(half, staged, donors, donor_weights[half]))
    c, l, u, *sums = forward(table, centre, lower_coef, upper_coef, low, high)
    tangent, returned, first, last = couple(l, u, receptor_cells, receptor_rows, messages[0] + messages[1], sums)
    far = to_donors(1, returned)
    near = to_donors(0, at_receptors(tangent, receptor_cells, receptor_rows))
    high = to_previous(first)
    low = to_next(last)
    sums = transposed(tangent, c, l, u)
    sums = add_at_donors(1, donors, donor_rows, donor_weights[1], far, sums)
    adjoint, gram = add_at_donors(0, donors, donor_rows, donor_weights[0], near, sums, (low, high))
    total_cells = lax.axis_size("grid") * lax.axis_size("cell") * width
    basis, factor = basis_of(total_cells, summed(gram), adjoint)
    return (basis, factor)


def solution(mesh):
    in_specs = (
        P(None, "grid", "cell"),
        P("grid", "cell"),
        P("grid", "cell"),
        P("grid", "cell"),
        P("grid", None, "cell"),
        P("grid", "cell"),
        P("grid", None, "cell"),
    )
    out_specs = (P(None, "grid", "cell"), P())
    return jax.shard_map(body, mesh=mesh, in_specs=in_specs, out_specs=out_specs, check_vma=False)
```

```python
import functools

import jax
import jax.numpy as jnp
from jax import lax
from jax.experimental import pallas as pl
from jax.experimental.pallas import tpu as pltpu
from jax.sharding import PartitionSpec as P

f32 = jnp.float32
i32 = jnp.int32
bf16 = jnp.bfloat16

PROBES = 16
GROUPS = 8
ROWS = 4096
LANES = 128
PARTNERS = 6
FRINGE = 1024
HALF = 3 * FRINGE
SLOTS = PARTNERS * FRINGE
TILES = ROWS // LANES
WAYS = 8
UNROLL = 8

AXES = ("grid", "cell")

VMEM = pl.BlockSpec(memory_space=pltpu.VMEM)
HBM = pl.BlockSpec(memory_space=pl.ANY)
FIXED = pl.BlockSpec(memory_space=pltpu.HBM)


def aligned(start, size):
    return pl.ds(pl.multiple_of(start, size), size)


def rows_of(start, size):
    return pl.ds(pl.multiple_of(start, 8), size)


def split(x):
    high = x.astype(bf16)
    return high, (x - high.astype(f32)).astype(bf16)


def params(limit_mib):
    return pltpu.CompilerParams(vmem_limit_bytes=limit_mib << 20)


def cost(microseconds):
    return pl.CostEstimate(flops=0, transcendentals=0, bytes_accessed=microseconds * 3_000_000)


def resident(*shape):
    return pltpu.VMEM(shape, f32)


HEAD = 128


def segments(many, partners):
    return [(m, k) for m in range(many) for k in partners]


def index_scratch(segs):
    size = len(segs) * FRINGE // WAYS
    return [pltpu.SMEM((size,), i32)] * WAYS + [pltpu.SemaphoreType.DMA((3 * WAYS,))]


def index_copies(rows_hbm, segs, parts, sem):
    size = parts[0].shape[0]
    cuts = sorted({0, HEAD, size} | set(range(0, size, FRINGE)))
    phases = [[], []]
    for c in range(len(cuts) - 1):
        low, high = cuts[c], cuts[c + 1]
        for w in range(WAYS):
            seg, offset = divmod(w * size + low, FRINGE)
            start = segs[seg][0] * SLOTS + segs[seg][1] * FRINGE + offset
            copy = pltpu.make_async_copy(
                rows_hbm.at[pl.ds(start, high - low)], parts[w].at[pl.ds(low, high - low)], sem.at[c * WAYS + w]
            )
            copy.start()
            phases[min(c, 1)].append(copy)
    return phases


def finish(copies):
    for copy in copies:
        copy.wait()


def row_steps(parts, low, high, step):
    def outer(j, carry):
        for n in range(UNROLL):
            q = low + j * UNROLL + n
            for w in range(WAYS):
                step(w, q, parts[w][q])
        return carry

    lax.fori_loop(0, (high - low) // UNROLL, outer, 0)


def gather_rows(table, parts, staged, phases):
    count = parts[0].shape[0]

    def step(w, q, row):
        staged[pl.ds(w * count + q, 1), :] = table[pl.ds(row, 1), :]

    finish(phases[0])
    row_steps(parts, 0, HEAD, step)
    finish(phases[1])
    row_steps(parts, HEAD, count, step)


def clear(sums):
    def step(j, carry):
        for total in sums:
            for n in range(4):
                total[rows_of(j * 32 + n * 8, 8), :] = jnp.zeros((8, LANES), f32)
        return carry

    lax.fori_loop(0, ROWS // 32, step, 0)


def add_rows(sums, parts, staged):
    count = parts[0].shape[0]

    def step(w, q, row):
        term = staged[pl.ds(w * count + q, 1), :]
        sums[w][pl.ds(row, 1), :] = sums[w][pl.ds(row, 1), :] + term

    row_steps(parts, 0, count, step)


def groups_of(cells, m, offset):
    return jnp.broadcast_to(cells[m : m + 1, aligned(offset, LANES)], (8, LANES)) >> 12


def each_block(many, step):
    unroll = 8 // many

    def outer(j, carry):
        for n in range(unroll):
            step(j * unroll + n)
        return carry

    lax.fori_loop(0, FRINGE // LANES // unroll, outer, 0)


def select_fields(staged, cells, partners, weights, out):
    many = cells.shape[0]
    for n, k in enumerate(partners):

        def step(b):
            total = [jnp.zeros((8, LANES), f32)] * 2
            for m in range(many):
                field = staged[aligned((m * len(partners) + n) * FRINGE + b * LANES, LANES), :].T
                group = groups_of(cells, m, k * FRINGE + b * LANES)
                scale = 1.0
                if weights is not None:
                    ref, row, column = weights[k]
                    scale = ref[row + m : row + m + 1, aligned(column + b * LANES, LANES)]
                    scale = jnp.broadcast_to(scale, (8, LANES))
                for g in range(GROUPS):
                    factor = jnp.where(group == g, scale, 0.0)
                    for h in range(2):
                        at = g * PROBES + h * 8
                        total[h] = total[h] + field[at : at + 8, :] * factor
            ref, row, column = out[k]
            for h in range(2):
                ref[row + h * 8 : row + h * 8 + 8, aligned(column + b * LANES, LANES)] = total[h]

        each_block(many, step)


def spread_fields(messages, cells, partners, weights, staged):
    many = cells.shape[0]
    for n, k in enumerate(partners):

        def step(b):
            ref, row, column = messages[k]
            field = [ref[row + h * 8 : row + h * 8 + 8, aligned(column + b * LANES, LANES)] for h in range(2)]
            for m in range(many):
                group = groups_of(cells, m, k * FRINGE + b * LANES)
                scaled = field
                if weights is not None:
                    ref, row, column = weights[k]
                    scale = ref[row + m : row + m + 1, aligned(column + b * LANES, LANES)]
                    scaled = [part * jnp.broadcast_to(scale, (8, LANES)) for part in field]
                terms = [jnp.where(group == g, scaled[h], 0.0) for g in range(GROUPS) for h in range(2)]
                at = aligned((m * len(partners) + n) * FRINGE + b * LANES, LANES)
                staged[at, :] = jnp.concatenate(terms, axis=0).T

        each_block(many, step)


def lanes(shape):
    return lax.broadcasted_iota(i32, shape, len(shape) - 1)


def fill_ends(padded, low, high):
    lane = lanes((1, LANES))
    before = pltpu.roll(padded[ROWS : ROWS + 8, :], PROBES, 1)[7:8, :]
    after = pltpu.roll(padded[8:16, :], LANES - PROBES, 1)[0:1, :]
    padded[7:8, :] = jnp.where(lane < PROBES, low, before)
    padded[ROWS + 8 : ROWS + 9, :] = jnp.where(lane >= LANES - PROBES, high, after)


def each_row_block(step):
    def outer(j, carry):
        for u in range(4):
            step(j * 32 + u * 8)
        return carry

    lax.fori_loop(0, ROWS // 32, outer, 0)


def table_kernel(probes, table, natural, sem):
    copies = [
        pltpu.make_async_copy(probes.at[p], natural.at[pl.ds(p, 1), :], sem.at[p]) for p in range(PROBES)
    ]
    for copy in copies:
        copy.start()
    finish(copies)

    def step(j, carry):
        for n in range(4):
            tile = j * 4 + n
            parts = [natural[:, aligned(g * ROWS + tile * LANES, LANES)] for g in range(GROUPS)]
            table[aligned(tile * LANES, LANES), :] = jnp.concatenate(parts, axis=0).T
        return carry

    lax.fori_loop(0, TILES // 4, step, 0)


def table_of(probes):
    return pl.pallas_call(
        table_kernel,
        out_shape=resident(ROWS, LANES),
        in_specs=[FIXED],
        out_specs=VMEM,
        scratch_shapes=[pltpu.VMEM((PROBES, GROUPS * ROWS), f32), pltpu.SemaphoreType.DMA((PROBES,))],
        compiler_params=params(8),
        cost_estimate=cost(3),
        name="table",
    )(probes)


BEFORE, SAME, AFTER = (0, 3), (1, 4), (2, 5)
SIDES = BEFORE + AFTER
NEAR, FAR = (0, 1, 2), (3, 4, 5)
EDGE = slice(FRINGE, FRINGE + LANES)


def weight_places(before, same, after):
    return {
        0: (before, 0, 0),
        3: (before, 4, 0),
        1: (same[0], 0, FRINGE),
        4: (same[1], 0, 4 * FRINGE),
        2: (after, 0, 0),
        5: (after, 4, 0),
    }


def pair_places(pair, ref):
    return {pair[0]: (ref, 0, 0), pair[1]: (ref, PROBES, 0)}


def grid_places(near, far):
    places = {k: (near, n * PROBES, 0) for n, k in enumerate(NEAR)}
    places.update({k: (far, n * PROBES, 0) for n, k in enumerate(FAR)})
    return places


def simple_call(kernel, out_shape, operands, name):
    return pl.pallas_call(
        kernel,
        out_shape=out_shape,
        in_specs=[VMEM] * len(operands),
        out_specs=[VMEM] * len(out_shape),
        compiler_params=params(8),
        cost_estimate=cost(1),
        name=name,
    )(*operands)


def weight_relay_kernel(near, far, table, up, down):
    for pair, out, rows in ((BEFORE, up, slice(ROWS - 8, ROWS)), (AFTER, down, slice(0, 8))):
        for n, ref in enumerate((near, far)):
            start = pair[n] * FRINGE
            out[n * 4 : n * 4 + 4, 0:FRINGE] = ref[:, start : start + FRINGE]
        out[:, EDGE] = table[rows, :]


def weight_relay(near, far, table):
    shape = jax.ShapeDtypeStruct((8, FRINGE + LANES), f32)
    return simple_call(weight_relay_kernel, [shape] * 2, (near, far, table), "weight_relay")


def rows_kernel(table, rows_hbm, staged, *rest):
    parts, sem = rest[:WAYS], rest[WAYS]
    gather_rows(table, parts, staged, index_copies(rows_hbm, segments(4, SIDES), parts, sem))


def rows_at_sides(table, rows):
    segs = segments(4, SIDES)
    return pl.pallas_call(
        rows_kernel,
        out_shape=resident(len(segs) * FRINGE, LANES),
        in_specs=[VMEM, HBM],
        out_specs=VMEM,
        scratch_shapes=index_scratch(segs),
        compiler_params=params(8),
        cost_estimate=cost(11),
        name="rows_at_sides",
    )(table, rows)


PAIR = jax.ShapeDtypeStruct((2 * PROBES, FRINGE), f32)
TRIPLE = jax.ShapeDtypeStruct((3 * PROBES, FRINGE), f32)


def side_sums_kernel(staged, cells, before, after, up, down):
    places = {**pair_places(AFTER, up), **pair_places(BEFORE, down)}
    select_fields(staged, cells, SIDES, weight_places(before, (None, None), after), places)


def side_sums(staged, cells, before, after):
    return simple_call(side_sums_kernel, [PAIR] * 2, (staged, cells, before, after), "side_sums")


def same_sums_kernel(table, cells, rows_hbm, near, far, out, staged, *rest):
    parts, sem = rest[:WAYS], rest[WAYS]
    gather_rows(table, parts, staged, index_copies(rows_hbm, segments(4, SAME), parts, sem))
    select_fields(staged, cells, SAME, weight_places(None, (near, far), None), pair_places(SAME, out))


def same_sums(table, cells, rows, near, far):
    segs = segments(4, SAME)
    return pl.pallas_call(
        same_sums_kernel,
        out_shape=PAIR,
        in_specs=[VMEM, VMEM, HBM, VMEM, VMEM],
        out_specs=VMEM,
        scratch_shapes=[pltpu.VMEM((len(segs) * FRINGE, LANES), f32)] + index_scratch(segs),
        compiler_params=params(8),
        cost_estimate=cost(8),
        name="same_sums",
    )(table, cells, rows, near, far)


def message_relay_kernel(before, same, after, near, far):
    for n, out in enumerate((near, far)):
        for i, ref in enumerate((before, same, after)):
            out[i * PROBES : (i + 1) * PROBES, :] = ref[n * PROBES : (n + 1) * PROBES, :]


def message_relay(before, same, after):
    return simple_call(message_relay_kernel, [TRIPLE] * 2, (before, same, after), "message_relay")


def end_flags():
    column = lax.axis_index("cell")
    return (column > 0).astype(f32), (column < lax.axis_size("cell") - 1).astype(f32)


def outer_rows(before, after):
    has_low, has_high = end_flags()
    low = pltpu.roll(before[0:8, EDGE], PROBES, 1)[7:8, :] * has_low
    high = pltpu.roll(after[0:8, EDGE], LANES - PROBES, 1)[0:1, :] * has_high
    return low, high


def forward_kernel(table, centre, lower, upper, before, after, c_out, l_out, u_out, *rest):
    sums, padded = rest[:WAYS], rest[WAYS]

    def step(j, carry):
        for n in range(2):
            tile = j * 2 + n
            at = aligned(tile * LANES, LANES)
            padded[rows_of(tile * LANES + 8, LANES), :] = table[at, :]
            for ref, out in ((centre, c_out), (lower, l_out), (upper, u_out)):
                parts = [
                    jnp.broadcast_to(ref[:, aligned(g * ROWS + tile * LANES, LANES)], (PROBES, LANES))
                    for g in range(GROUPS)
                ]
                out[at, :] = jnp.concatenate(parts, axis=0).T
        return carry

    lax.fori_loop(0, TILES // 2, step, 0)
    fill_ends(padded, *outer_rows(before, after))

    def stencil(start):
        at = rows_of(start, 8)
        sums[0][at, :] = (
            c_out[at, :] * padded[rows_of(start + 8, 8), :]
            - l_out[at, :] * padded[pl.ds(start + 7, 8), :]
            - u_out[at, :] * padded[pl.ds(start + 9, 8), :]
        )

    each_row_block(stencil)
    clear(sums[1:])


def forward(table, centre, lower, upper, before, after):
    return pl.pallas_call(
        forward_kernel,
        out_shape=[resident(ROWS, LANES)] * (3 + WAYS),
        in_specs=[VMEM] * 6,
        out_specs=[VMEM] * (3 + WAYS),
        scratch_shapes=[pltpu.VMEM((ROWS + 16, LANES), f32)],
        compiler_params=params(8),
        cost_estimate=cost(7),
        name="forward",
    )(table, centre, lower, upper, before, after)


def couple_kernel(cells, rows_hbm, near, far, *refs):
    refs = refs[WAYS:]
    tangent, out, sums = refs[0], refs[1], refs[2 : 2 + WAYS]
    staged, staged_far = refs[2 + WAYS : 4 + WAYS]
    refs = refs[4 + WAYS :]
    parts, sem, parts_far, sem_far = refs[:WAYS], refs[WAYS], refs[WAYS + 1 : 2 * WAYS + 1], refs[2 * WAYS + 1]
    every = NEAR + FAR
    phases = index_copies(rows_hbm, segments(1, every), parts, sem)
    phases_far = index_copies(rows_hbm, segments(1, FAR), parts_far, sem_far)
    spread_fields(grid_places(near, far), cells, every, None, staged)
    finish(phases[0] + phases[1])
    add_rows(sums, parts, staged)

    def total(start):
        at = rows_of(start, 8)
        value = sums[0][at, :]
        for part in sums[1:]:
            value = value + part[at, :]
        tangent[at, :] = value

    each_row_block(total)
    gather_rows(tangent, parts_far, staged_far, phases_far)
    select_fields(staged_far, cells, FAR, None, grid_places(None, out))


def couple(cells, rows, near, far, sums):
    every, some = segments(1, NEAR + FAR), segments(1, FAR)
    outs = pl.pallas_call(
        couple_kernel,
        out_shape=[resident(ROWS, LANES), TRIPLE] + [resident(ROWS, LANES)] * WAYS,
        in_specs=[VMEM, HBM] + [VMEM] * (2 + WAYS),
        out_specs=[VMEM] * (2 + WAYS),
        scratch_shapes=[pltpu.VMEM((SLOTS, LANES), f32), pltpu.VMEM((SLOTS // 2, LANES), f32)]
        + index_scratch(every)
        + index_scratch(some),
        input_output_aliases={4 + w: 2 + w for w in range(WAYS)},
        compiler_params=params(8),
        cost_estimate=cost(11),
        name="couple",
    )(cells, rows, near, far, *sums)
    return outs[0], outs[1]


def receptor_kernel(tangent, cells, rows_hbm, out, staged, *rest):
    parts, sem = rest[:WAYS], rest[WAYS]
    gather_rows(tangent, parts, staged, index_copies(rows_hbm, segments(1, NEAR), parts, sem))
    select_fields(staged, cells, NEAR, None, grid_places(out, None))


def at_receptors(tangent, cells, rows):
    segs = segments(1, NEAR)
    return pl.pallas_call(
        receptor_kernel,
        out_shape=TRIPLE,
        in_specs=[VMEM, VMEM, HBM],
        out_specs=VMEM,
        scratch_shapes=[pltpu.VMEM((len(segs) * FRINGE, LANES), f32)] + index_scratch(segs),
        compiler_params=params(8),
        cost_estimate=cost(3),
        name="at_receptors",
    )(tangent, cells, rows)


def return_relay_kernel(near, far, tangent, lower, upper, up, down):
    for n, ref in enumerate((near, far)):
        at = slice(n * PROBES, (n + 1) * PROBES)
        up[at, 0:FRINGE] = ref[0:PROBES, :]
        down[at, 0:FRINGE] = ref[2 * PROBES : 3 * PROBES, :]
    end = slice(ROWS - 8, ROWS)
    up[0:8, EDGE] = upper[end, :] * tangent[end, :]
    down[0:8, EDGE] = lower[0:8, :] * tangent[0:8, :]


def return_relay(near, far, tangent, lower, upper):
    shape = jax.ShapeDtypeStruct((2 * PROBES, FRINGE + LANES), f32)
    return simple_call(return_relay_kernel, [shape] * 2, (near, far, tangent, lower, upper), "return_relay")


def transposed_kernel(tangent, centre, lower, upper, *rest):
    sums, raised, lowered = rest[:WAYS], rest[WAYS], rest[WAYS + 1]

    def products(start):
        at = rows_of(start, 8)
        value = tangent[at, :]
        raised[rows_of(start + 8, 8), :] = upper[at, :] * value
        lowered[rows_of(start + 8, 8), :] = lower[at, :] * value

    each_row_block(products)
    nothing = jnp.zeros((1, LANES), f32)
    fill_ends(raised, nothing, nothing)
    fill_ends(lowered, nothing, nothing)

    def stencil(start):
        at = rows_of(start, 8)
        sums[0][at, :] = (
            centre[at, :] * tangent[at, :] - raised[pl.ds(start + 7, 8), :] - lowered[pl.ds(start + 9, 8), :]
        )

    each_row_block(stencil)
    clear(sums[1:])


def transposed(tangent, centre, lower, upper):
    return pl.pallas_call(
        transposed_kernel,
        out_shape=[resident(ROWS, LANES)] * WAYS,
        in_specs=[VMEM] * 4,
        out_specs=[VMEM] * WAYS,
        scratch_shapes=[pltpu.VMEM((ROWS + 16, LANES), f32)] * 2,
        compiler_params=params(8),
        cost_estimate=cost(4),
        name="transposed",
    )(tangent, centre, lower, upper)


def donor_same_kernel(cells, rows_hbm, near_weights, far_weights, near, far, *refs):
    refs = refs[WAYS:]
    sums, staged, parts, sem = refs[:WAYS], refs[WAYS], refs[WAYS + 1 : 2 * WAYS + 1], refs[2 * WAYS + 1]
    phases = index_copies(rows_hbm, segments(4, SAME), parts, sem)
    weights = weight_places(None, (near_weights, far_weights), None)
    spread_fields(grid_places(near, far), cells, SAME, weights, staged)
    finish(phases[0] + phases[1])
    add_rows(sums, parts, staged)


def add_same(cells, rows, near_weights, far_weights, near, far, sums):
    segs = segments(4, SAME)
    return pl.pallas_call(
        donor_same_kernel,
        out_shape=[resident(ROWS, LANES)] * WAYS,
        in_specs=[VMEM, HBM] + [VMEM] * (4 + WAYS),
        out_specs=[VMEM] * WAYS,
        scratch_shapes=[pltpu.VMEM((len(segs) * FRINGE, LANES), f32)] + index_scratch(segs),
        input_output_aliases={6 + w: w for w in range(WAYS)},
        compiler_params=params(8),
        cost_estimate=cost(9),
        name="add_same",
    )(cells, rows, near_weights, far_weights, near, far, *sums)


def donor_sides_kernel(cells, rows_hbm, before_weights, after_weights, before, after, *refs):
    refs = refs[WAYS:]
    adjoint, gram, sums, staged = refs[0], refs[1], refs[2 : 2 + WAYS], refs[2 + WAYS]
    parts, sem = refs[3 + WAYS : 3 + 2 * WAYS], refs[3 + 2 * WAYS]
    phases = index_copies(rows_hbm, segments(4, SIDES), parts, sem)
    weights = weight_places(before_weights, (None, None), after_weights)
    spread_fields({**pair_places(BEFORE, before), **pair_places(AFTER, after)}, cells, SIDES, weights, staged)
    finish(phases[0] + phases[1])
    add_rows(sums, parts, staged)
    lane = lanes((1, LANES))
    low, high = outer_rows(before, after)
    sums[0][0:1, :] = sums[0][0:1, :] - jnp.where(lane < PROBES, low, 0.0)
    end = sums[0][ROWS - 1 : ROWS, :]
    sums[0][ROWS - 1 : ROWS, :] = end - jnp.where(lane >= LANES - PROBES, high, 0.0)

    def total(start):
        at = rows_of(start, 8)
        value = sums[0][at, :]
        for part in sums[1:]:
            value = value + part[at, :]
        adjoint[at, :] = value

    each_row_block(total)

    def multiply(j, product):
        left_side, right_side = [], []
        for n in range(4):
            block = adjoint[aligned((j * 4 + n) * LANES, LANES), :]
            high, low = split(block)
            high_t, low_t = split(block.T)
            left_side += [high_t, high_t, low_t]
            right_side += [high, low, high]
        left_side = jnp.concatenate(left_side, axis=1)
        right_side = jnp.concatenate(right_side, axis=0)
        return product + jnp.dot(left_side, right_side, preferred_element_type=f32)

    product = lax.fori_loop(0, TILES // 4, multiply, jnp.zeros((LANES, LANES), f32))
    group = lanes((PROBES, LANES)) // PROBES
    folded = jnp.zeros((PROBES, LANES), f32)
    for g in range(GROUPS):
        folded = folded + jnp.where(group == g, product[g * PROBES : (g + 1) * PROBES, :], 0.0)
    for shift in (64, 32, 16):
        folded = folded + pltpu.roll(folded, shift, 1)
    gram[...] = folded[:, :PROBES]


def add_sides(cells, rows, before_weights, after_weights, before, after, sums):
    segs = segments(4, SIDES)
    outs = pl.pallas_call(
        donor_sides_kernel,
        out_shape=[resident(ROWS, LANES), jax.ShapeDtypeStruct((PROBES, PROBES), f32)]
        + [resident(ROWS, LANES)] * WAYS,
        in_specs=[VMEM, HBM] + [VMEM] * (4 + WAYS),
        out_specs=[VMEM] * (2 + WAYS),
        scratch_shapes=[pltpu.VMEM((len(segs) * FRINGE, LANES), f32)] + index_scratch(segs),
        input_output_aliases={6 + w: 2 + w for w in range(WAYS)},
        compiler_params=params(12),
        cost_estimate=cost(18),
        name="add_sides",
    )(cells, rows, before_weights, after_weights, before, after, *sums)
    return outs[0], outs[1]


def basis_kernel(total_cells, gram, adjoint, basis, factor, natural, sem):
    row = lax.broadcasted_iota(i32, (PROBES, 1), 0)
    left = gram[...] / f32(total_cells)
    right = jnp.where(lax.broadcasted_iota(i32, (PROBES, LANES), 0) == lanes((PROBES, LANES)) % PROBES, 1.0, 0.0)
    for j in range(PROBES):
        pivot = left[j : j + 1, j : j + 1]
        ratio = jnp.where(row > j, left[:, j : j + 1] / pivot, 0.0)
        root = jnp.sqrt(pivot)
        left_row, right_row = left[j : j + 1, :], right[j : j + 1, :]
        left = jnp.where(row == j, left_row / root, left - ratio * left_row)
        right = jnp.where(row == j, right_row / root, right - ratio * right_row)
    down = lax.broadcasted_iota(i32, (PROBES, PROBES), 0)
    factor[...] = jnp.where(lanes((PROBES, PROBES)) >= down, left, 0.0).T
    inverse = jnp.concatenate([right] * GROUPS, axis=0)
    same = lax.broadcasted_iota(i32, (LANES, LANES), 0) // PROBES == lanes((LANES, LANES)) // PROBES
    high, low = split(jnp.where(same, inverse, 0.0))
    left_side = jnp.concatenate([high, high, low], axis=1)

    def step(j, carry):
        for n in range(4):
            tile = j * 4 + n
            high, low = split(adjoint[aligned(tile * LANES, LANES), :])
            right_side = jnp.concatenate([high, low, high], axis=1)
            block = lax.dot_general(left_side, right_side, (((1,), (1,)), ((), ())), preferred_element_type=f32)
            for g in range(GROUPS):
                natural[:, aligned(g * ROWS + tile * LANES, LANES)] = block[g * PROBES : (g + 1) * PROBES, :]
        return carry

    lax.fori_loop(0, TILES // 4, step, 0)
    copies = [
        pltpu.make_async_copy(natural.at[pl.ds(p, 1), :], basis.at[p], sem.at[p]) for p in range(PROBES)
    ]
    for copy in copies:
        copy.start()
    finish(copies)


def basis_of(total_cells, gram, adjoint):
    return pl.pallas_call(
        functools.partial(basis_kernel, total_cells),
        out_shape=[
            jax.ShapeDtypeStruct((PROBES, 1, GROUPS * ROWS), f32),
            jax.ShapeDtypeStruct((PROBES, PROBES), f32),
        ],
        in_specs=[VMEM] * 2,
        out_specs=[FIXED, VMEM],
        scratch_shapes=[pltpu.VMEM((PROBES, GROUPS * ROWS), f32), pltpu.SemaphoreType.DMA((PROBES,))],
        compiler_params=params(8),
        cost_estimate=cost(6),
        name="basis",
    )(gram, adjoint)


def moved(value, place):
    grids, columns = (lax.axis_size(axis) for axis in AXES)
    route = []
    for g in range(grids):
        for c in range(columns):
            to_g, to_c = place(g, c)
            route.append((g * columns + c, (to_g % grids) * columns + to_c % columns))
    return lax.ppermute(value, AXES, route)


def along_grid(value, distance):
    return moved(value, lambda g, c: (g + distance, c))


def along_cell(value, distance):
    return moved(value, lambda g, c: (g, c + distance))


def summed(value):
    value = value + moved(value, lambda g, c: (g ^ 1, c))
    value = value + moved(value, lambda g, c: (g ^ 2, c))
    value = value + moved(value, lambda g, c: ((6 - (g & 6)) | (g & 1), c))
    value = value + moved(value, lambda g, c: (g, c ^ 1))
    value = value + moved(value, lambda g, c: (g, (c & 12) | (3 - (c & 3))))
    value = value + moved(value, lambda g, c: (g, c ^ 4))
    value = value + moved(value, lambda g, c: (g, (12 - (c & 12)) | (c & 3)))
    return value


def body(probes, centre, lower_coef, upper_coef, donor_cells, receptor_cells, weights):
    donors = donor_cells[0]
    donor_rows = (donors & (ROWS - 1)).reshape(-1)
    receptor_rows = (receptor_cells & (ROWS - 1)).reshape(-1)
    near_weights, far_weights = along_grid(weights, -1)[0], along_grid(weights, -2)[0]
    table = table_of(probes)
    up, down = weight_relay(near_weights, far_weights, table)
    before_weights, after_weights = along_cell(up, 1), along_cell(down, -1)
    staged = rows_at_sides(table, donor_rows)
    up, down = side_sums(staged, donors, before_weights, after_weights)
    after, before = along_cell(up, 1), along_cell(down, -1)
    same = same_sums(table, donors, donor_rows, near_weights, far_weights)
    near, far = message_relay(before, same, after)
    near, far = along_grid(near, 1), along_grid(far, 2)
    c, l, u, *sums = forward(table, centre, lower_coef, upper_coef, before_weights, after_weights)
    tangent, far = couple(receptor_cells, receptor_rows, near, far, sums)
    far = along_grid(far, -2)
    near = along_grid(at_receptors(tangent, receptor_cells, receptor_rows), -1)
    sums = transposed(tangent, c, l, u)
    up, down = return_relay(near, far, tangent, l, u)
    before, after = along_cell(up, 1), along_cell(down, -1)
    sums = add_same(donors, donor_rows, near_weights, far_weights, near, far, sums)
    adjoint, gram = add_sides(donors, donor_rows, before_weights, after_weights, before, after, sums)
    total_cells = lax.axis_size("grid") * lax.axis_size("cell") * probes.shape[2]
    basis, factor = basis_of(total_cells, summed(gram), adjoint)
    return (basis, factor)


def solution(mesh):
    in_specs = (
        P(None, "grid", "cell"),
        P("grid", "cell"),
        P("grid", "cell"),
        P("grid", "cell"),
        P("grid", None, "cell"),
        P("grid", "cell"),
        P("grid", None, "cell"),
    )
    out_specs = (P(None, "grid", "cell"), P())
    return jax.shard_map(body, mesh=mesh, in_specs=in_specs, out_specs=out_specs, check_vma=False)
```

```python
import functools

import jax
import jax.numpy as jnp
from jax import lax
from jax.experimental import pallas as pl
from jax.experimental.pallas import tpu as pltpu
from jax.sharding import PartitionSpec as P

f32 = jnp.float32
i32 = jnp.int32
bf16 = jnp.bfloat16

PROBES = 16
GROUPS = 8
ROWS = 4096
LANES = 128
PARTNERS = 6
FRINGE = 1024
HALF = 3 * FRINGE
SLOTS = PARTNERS * FRINGE
TILES = ROWS // LANES
WAYS = 8
SUMS = 16
UNROLL = 8

AXES = ("grid", "cell")

VMEM = pl.BlockSpec(memory_space=pltpu.VMEM)
HBM = pl.BlockSpec(memory_space=pl.ANY)
FIXED = pl.BlockSpec(memory_space=pltpu.HBM)


def aligned(start, size):
    return pl.ds(pl.multiple_of(start, size), size)


def rows_of(start, size):
    return pl.ds(pl.multiple_of(start, 8), size)


def split(x):
    high = x.astype(bf16)
    return high, (x - high.astype(f32)).astype(bf16)


def params(limit_mib):
    return pltpu.CompilerParams(vmem_limit_bytes=limit_mib << 20)


def cost(microseconds):
    return pl.CostEstimate(flops=0, transcendentals=0, bytes_accessed=microseconds * 3_000_000)


def resident(*shape):
    return pltpu.VMEM(shape, f32)


HEAD = 128


def segments(many, partners):
    return [(m, k) for m in range(many) for k in partners]


def index_scratch(segs):
    size = len(segs) * FRINGE // WAYS
    return [pltpu.SMEM((size,), i32)] * WAYS + [pltpu.SemaphoreType.DMA((3 * WAYS,))]


def index_copies(rows_hbm, segs, parts, sem):
    size = parts[0].shape[0]
    cuts = sorted({0, HEAD, size} | set(range(0, size, FRINGE)))
    phases = [[], []]
    for c in range(len(cuts) - 1):
        low, high = cuts[c], cuts[c + 1]
        for w in range(WAYS):
            seg, offset = divmod(w * size + low, FRINGE)
            start = segs[seg][0] * SLOTS + segs[seg][1] * FRINGE + offset
            copy = pltpu.make_async_copy(
                rows_hbm.at[pl.ds(start, high - low)], parts[w].at[pl.ds(low, high - low)], sem.at[c * WAYS + w]
            )
            copy.start()
            phases[min(c, 1)].append(copy)
    return phases


def finish(copies):
    for copy in copies:
        copy.wait()


def row_steps(parts, low, high, step):
    def outer(j, carry):
        for n in range(UNROLL):
            q = low + j * UNROLL + n
            for w in range(WAYS):
                step(w, n, q, parts[w][q])
        return carry

    lax.fori_loop(0, (high - low) // UNROLL, outer, 0)


def gather_rows(table, parts, staged, phases):
    count = parts[0].shape[0]

    def step(w, n, q, row):
        staged[pl.ds(w * count + q, 1), :] = table[pl.ds(row, 1), :]

    finish(phases[0])
    row_steps(parts, 0, HEAD, step)
    finish(phases[1])
    row_steps(parts, HEAD, count, step)


def clear(sums):
    def step(j, carry):
        for total in sums:
            for n in range(4):
                total[rows_of(j * 32 + n * 8, 8), :] = jnp.zeros((8, LANES), f32)
        return carry

    lax.fori_loop(0, ROWS // 32, step, 0)


def add_rows(sums, parts, staged):
    count = parts[0].shape[0]

    def step(w, n, q, row):
        term = staged[pl.ds(w * count + q, 1), :]
        total = sums[w + n % (SUMS // WAYS) * WAYS]
        total[pl.ds(row, 1), :] = total[pl.ds(row, 1), :] + term

    row_steps(parts, 0, count, step)


def groups_of(cells, m, offset):
    return jnp.broadcast_to(cells[m : m + 1, aligned(offset, LANES)], (8, LANES)) >> 12


def each_block(many, step):
    unroll = 8 // many

    def outer(j, carry):
        for n in range(unroll):
            step(j * unroll + n)
        return carry

    lax.fori_loop(0, FRINGE // LANES // unroll, outer, 0)


def select_fields(staged, cells, partners, weights, out):
    many = cells.shape[0]
    for n, k in enumerate(partners):

        def step(b):
            total = [jnp.zeros((8, LANES), f32)] * 2
            for m in range(many):
                field = staged[aligned((m * len(partners) + n) * FRINGE + b * LANES, LANES), :].T
                group = groups_of(cells, m, k * FRINGE + b * LANES)
                scale = 1.0
                if weights is not None:
                    ref, row, column = weights[k]
                    scale = ref[row + m : row + m + 1, aligned(column + b * LANES, LANES)]
                    scale = jnp.broadcast_to(scale, (8, LANES))
                for g in range(GROUPS):
                    factor = jnp.where(group == g, scale, 0.0)
                    for h in range(2):
                        at = g * PROBES + h * 8
                        total[h] = total[h] + field[at : at + 8, :] * factor
            ref, row, column = out[k]
            for h in range(2):
                ref[row + h * 8 : row + h * 8 + 8, aligned(column + b * LANES, LANES)] = total[h]

        each_block(many, step)


def spread_fields(messages, cells, partners, weights, staged):
    many = cells.shape[0]
    for n, k in enumerate(partners):

        def step(b):
            ref, row, column = messages[k]
            field = [ref[row + h * 8 : row + h * 8 + 8, aligned(column + b * LANES, LANES)] for h in range(2)]
            for m in range(many):
                group = groups_of(cells, m, k * FRINGE + b * LANES)
                scaled = field
                if weights is not None:
                    ref, row, column = weights[k]
                    scale = ref[row + m : row + m + 1, aligned(column + b * LANES, LANES)]
                    scaled = [part * jnp.broadcast_to(scale, (8, LANES)) for part in field]
                terms = [jnp.where(group == g, scaled[h], 0.0) for g in range(GROUPS) for h in range(2)]
                at = aligned((m * len(partners) + n) * FRINGE + b * LANES, LANES)
                staged[at, :] = jnp.concatenate(terms, axis=0).T

        each_block(many, step)


def lanes(shape):
    return lax.broadcasted_iota(i32, shape, len(shape) - 1)


def fill_ends(padded, low, high):
    lane = lanes((1, LANES))
    before = pltpu.roll(padded[ROWS : ROWS + 8, :], PROBES, 1)[7:8, :]
    after = pltpu.roll(padded[8:16, :], LANES - PROBES, 1)[0:1, :]
    padded[7:8, :] = jnp.where(lane < PROBES, low, before)
    padded[ROWS + 8 : ROWS + 9, :] = jnp.where(lane >= LANES - PROBES, high, after)


def each_row_block(step):
    def outer(j, carry):
        for u in range(4):
            step(j * 32 + u * 8)
        return carry

    lax.fori_loop(0, ROWS // 32, outer, 0)


def table_kernel(probes, table, natural, sem):
    copies = [
        pltpu.make_async_copy(probes.at[p], natural.at[pl.ds(p, 1), :], sem.at[p]) for p in range(PROBES)
    ]
    for copy in copies:
        copy.start()
    finish(copies)

    def step(j, carry):
        for n in range(4):
            tile = j * 4 + n
            parts = [natural[:, aligned(g * ROWS + tile * LANES, LANES)] for g in range(GROUPS)]
            table[aligned(tile * LANES, LANES), :] = jnp.concatenate(parts, axis=0).T
        return carry

    lax.fori_loop(0, TILES // 4, step, 0)


def table_of(probes):
    return pl.pallas_call(
        table_kernel,
        out_shape=resident(ROWS, LANES),
        in_specs=[FIXED],
        out_specs=VMEM,
        scratch_shapes=[pltpu.VMEM((PROBES, GROUPS * ROWS), f32), pltpu.SemaphoreType.DMA((PROBES,))],
        compiler_params=params(8),
        cost_estimate=cost(3),
        name="table",
    )(probes)


BEFORE, SAME, AFTER = (0, 3), (1, 4), (2, 5)
SIDES = BEFORE + AFTER
NEAR, FAR = (0, 1, 2), (3, 4, 5)
EDGE = slice(FRINGE, FRINGE + LANES)


def weight_places(before, same, after):
    return {
        0: (before, 0, 0),
        3: (before, 4, 0),
        1: (same[0], 0, FRINGE),
        4: (same[1], 0, 4 * FRINGE),
        2: (after, 0, 0),
        5: (after, 4, 0),
    }


def pair_places(pair, ref):
    return {pair[0]: (ref, 0, 0), pair[1]: (ref, PROBES, 0)}


def grid_places(near, far):
    places = {k: (near, n * PROBES, 0) for n, k in enumerate(NEAR)}
    places.update({k: (far, n * PROBES, 0) for n, k in enumerate(FAR)})
    return places


def simple_call(kernel, out_shape, operands, name):
    return pl.pallas_call(
        kernel,
        out_shape=out_shape,
        in_specs=[VMEM] * len(operands),
        out_specs=[VMEM] * len(out_shape),
        compiler_params=params(8),
        cost_estimate=cost(1),
        name=name,
    )(*operands)


def weight_relay_kernel(near, far, table, up, down):
    for pair, out, rows in ((BEFORE, up, slice(ROWS - 8, ROWS)), (AFTER, down, slice(0, 8))):
        for n, ref in enumerate((near, far)):
            start = pair[n] * FRINGE
            out[n * 4 : n * 4 + 4, 0:FRINGE] = ref[:, start : start + FRINGE]
        out[:, EDGE] = table[rows, :]


def weight_relay(near, far, table):
    shape = jax.ShapeDtypeStruct((8, FRINGE + LANES), f32)
    return simple_call(weight_relay_kernel, [shape] * 2, (near, far, table), "weight_relay")


def rows_kernel(table, rows_hbm, staged, *rest):
    parts, sem = rest[:WAYS], rest[WAYS]
    gather_rows(table, parts, staged, index_copies(rows_hbm, segments(4, SIDES), parts, sem))


def rows_at_sides(table, rows):
    segs = segments(4, SIDES)
    return pl.pallas_call(
        rows_kernel,
        out_shape=resident(len(segs) * FRINGE, LANES),
        in_specs=[VMEM, HBM],
        out_specs=VMEM,
        scratch_shapes=index_scratch(segs),
        compiler_params=params(8),
        cost_estimate=cost(11),
        name="rows_at_sides",
    )(table, rows)


PAIR = jax.ShapeDtypeStruct((2 * PROBES, FRINGE), f32)
TRIPLE = jax.ShapeDtypeStruct((3 * PROBES, FRINGE), f32)


def side_sums_kernel(staged, cells, before, after, up, down):
    places = {**pair_places(AFTER, up), **pair_places(BEFORE, down)}
    select_fields(staged, cells, SIDES, weight_places(before, (None, None), after), places)


def side_sums(staged, cells, before, after):
    return simple_call(side_sums_kernel, [PAIR] * 2, (staged, cells, before, after), "side_sums")


def same_sums_kernel(table, cells, rows_hbm, near, far, out, staged, *rest):
    parts, sem = rest[:WAYS], rest[WAYS]
    gather_rows(table, parts, staged, index_copies(rows_hbm, segments(4, SAME), parts, sem))
    select_fields(staged, cells, SAME, weight_places(None, (near, far), None), pair_places(SAME, out))


def same_sums(table, cells, rows, near, far):
    segs = segments(4, SAME)
    return pl.pallas_call(
        same_sums_kernel,
        out_shape=PAIR,
        in_specs=[VMEM, VMEM, HBM, VMEM, VMEM],
        out_specs=VMEM,
        scratch_shapes=[pltpu.VMEM((len(segs) * FRINGE, LANES), f32)] + index_scratch(segs),
        compiler_params=params(8),
        cost_estimate=cost(8),
        name="same_sums",
    )(table, cells, rows, near, far)


def message_relay_kernel(before, same, after, near, far):
    for n, out in enumerate((near, far)):
        for i, ref in enumerate((before, same, after)):
            out[i * PROBES : (i + 1) * PROBES, :] = ref[n * PROBES : (n + 1) * PROBES, :]


def message_relay(before, same, after):
    return simple_call(message_relay_kernel, [TRIPLE] * 2, (before, same, after), "message_relay")


def end_flags():
    column = lax.axis_index("cell")
    return (column > 0).astype(f32), (column < lax.axis_size("cell") - 1).astype(f32)


def outer_rows(before, after):
    has_low, has_high = end_flags()
    low = pltpu.roll(before[0:8, EDGE], PROBES, 1)[7:8, :] * has_low
    high = pltpu.roll(after[0:8, EDGE], LANES - PROBES, 1)[0:1, :] * has_high
    return low, high


def forward_kernel(table, centre, lower, upper, before, after, c_out, l_out, u_out, *rest):
    sums, padded = rest[:SUMS], rest[SUMS]

    def step(j, carry):
        for n in range(2):
            tile = j * 2 + n
            at = aligned(tile * LANES, LANES)
            padded[rows_of(tile * LANES + 8, LANES), :] = table[at, :]
            for ref, out in ((centre, c_out), (lower, l_out), (upper, u_out)):
                parts = [
                    jnp.broadcast_to(ref[:, aligned(g * ROWS + tile * LANES, LANES)], (PROBES, LANES))
                    for g in range(GROUPS)
                ]
                out[at, :] = jnp.concatenate(parts, axis=0).T
        return carry

    lax.fori_loop(0, TILES // 2, step, 0)
    fill_ends(padded, *outer_rows(before, after))

    def stencil(start):
        at = rows_of(start, 8)
        sums[0][at, :] = (
            c_out[at, :] * padded[rows_of(start + 8, 8), :]
            - l_out[at, :] * padded[pl.ds(start + 7, 8), :]
            - u_out[at, :] * padded[pl.ds(start + 9, 8), :]
        )

    each_row_block(stencil)
    clear(sums[1:])


def forward(table, centre, lower, upper, before, after):
    return pl.pallas_call(
        forward_kernel,
        out_shape=[resident(ROWS, LANES)] * (3 + SUMS),
        in_specs=[VMEM] * 6,
        out_specs=[VMEM] * (3 + SUMS),
        scratch_shapes=[pltpu.VMEM((ROWS + 16, LANES), f32)],
        compiler_params=params(8),
        cost_estimate=cost(7),
        name="forward",
    )(table, centre, lower, upper, before, after)


def couple_kernel(cells, rows_hbm, near, far, *refs):
    refs = refs[SUMS:]
    tangent, out, sums = refs[0], refs[1], refs[2 : 2 + SUMS]
    staged, staged_far = refs[2 + SUMS : 4 + SUMS]
    refs = refs[4 + SUMS :]
    parts, sem, parts_far, sem_far = refs[:WAYS], refs[WAYS], refs[WAYS + 1 : 2 * WAYS + 1], refs[2 * WAYS + 1]
    every = NEAR + FAR
    phases = index_copies(rows_hbm, segments(1, every), parts, sem)
    phases_far = index_copies(rows_hbm, segments(1, FAR), parts_far, sem_far)
    spread_fields(grid_places(near, far), cells, every, None, staged)
    finish(phases[0] + phases[1])
    add_rows(sums, parts, staged)

    def total(start):
        at = rows_of(start, 8)
        value = sums[0][at, :]
        for part in sums[1:]:
            value = value + part[at, :]
        tangent[at, :] = value

    each_row_block(total)
    gather_rows(tangent, parts_far, staged_far, phases_far)
    select_fields(staged_far, cells, FAR, None, grid_places(None, out))


def couple(cells, rows, near, far, sums):
    every, some = segments(1, NEAR + FAR), segments(1, FAR)
    outs = pl.pallas_call(
        couple_kernel,
        out_shape=[resident(ROWS, LANES), TRIPLE] + [resident(ROWS, LANES)] * SUMS,
        in_specs=[VMEM, HBM] + [VMEM] * (2 + SUMS),
        out_specs=[VMEM] * (2 + SUMS),
        scratch_shapes=[pltpu.VMEM((SLOTS, LANES), f32), pltpu.VMEM((SLOTS // 2, LANES), f32)]
        + index_scratch(every)
        + index_scratch(some),
        input_output_aliases={4 + w: 2 + w for w in range(SUMS)},
        compiler_params=params(8),
        cost_estimate=cost(11),
        name="couple",
    )(cells, rows, near, far, *sums)
    return outs[0], outs[1]


def receptor_kernel(tangent, cells, rows_hbm, out, staged, *rest):
    parts, sem = rest[:WAYS], rest[WAYS]
    gather_rows(tangent, parts, staged, index_copies(rows_hbm, segments(1, NEAR), parts, sem))
    select_fields(staged, cells, NEAR, None, grid_places(out, None))


def at_receptors(tangent, cells, rows):
    segs = segments(1, NEAR)
    return pl.pallas_call(
        receptor_kernel,
        out_shape=TRIPLE,
        in_specs=[VMEM, VMEM, HBM],
        out_specs=VMEM,
        scratch_shapes=[pltpu.VMEM((len(segs) * FRINGE, LANES), f32)] + index_scratch(segs),
        compiler_params=params(8),
        cost_estimate=cost(3),
        name="at_receptors",
    )(tangent, cells, rows)


def return_relay_kernel(near, far, tangent, lower, upper, ready, up, down):
    for n, ref in enumerate((near, far)):
        at = slice(n * PROBES, (n + 1) * PROBES)
        up[at, 0:FRINGE] = ref[0:PROBES, :]
        down[at, 0:FRINGE] = ref[2 * PROBES : 3 * PROBES, :]
    end = slice(ROWS - 8, ROWS)
    up[0:8, EDGE] = upper[end, :] * tangent[end, :]
    down[0:8, EDGE] = lower[0:8, :] * tangent[0:8, :]


def return_relay(near, far, tangent, lower, upper, ready):
    shape = jax.ShapeDtypeStruct((2 * PROBES, FRINGE + LANES), f32)
    return simple_call(return_relay_kernel, [shape] * 2, (near, far, tangent, lower, upper, ready), "return_relay")


def transposed_kernel(tangent, centre, lower, upper, *rest):
    sums, raised, lowered = rest[:SUMS], rest[SUMS], rest[SUMS + 1]

    def products(start):
        at = rows_of(start, 8)
        value = tangent[at, :]
        raised[rows_of(start + 8, 8), :] = upper[at, :] * value
        lowered[rows_of(start + 8, 8), :] = lower[at, :] * value

    each_row_block(products)
    nothing = jnp.zeros((1, LANES), f32)
    fill_ends(raised, nothing, nothing)
    fill_ends(lowered, nothing, nothing)

    def stencil(start):
        at = rows_of(start, 8)
        sums[0][at, :] = (
            centre[at, :] * tangent[at, :] - raised[pl.ds(start + 7, 8), :] - lowered[pl.ds(start + 9, 8), :]
        )

    each_row_block(stencil)
    clear(sums[1:])


def transposed(tangent, centre, lower, upper):
    return pl.pallas_call(
        transposed_kernel,
        out_shape=[resident(ROWS, LANES)] * SUMS,
        in_specs=[VMEM] * 4,
        out_specs=[VMEM] * SUMS,
        scratch_shapes=[pltpu.VMEM((ROWS + 16, LANES), f32)] * 2,
        compiler_params=params(8),
        cost_estimate=cost(4),
        name="transposed",
    )(tangent, centre, lower, upper)


def donor_same_kernel(cells, rows_hbm, near_weights, far_weights, near, far, *refs):
    refs = refs[SUMS:]
    sums, staged, parts, sem = refs[:SUMS], refs[SUMS], refs[SUMS + 1 : SUMS + WAYS + 1], refs[SUMS + WAYS + 1]
    phases = index_copies(rows_hbm, segments(4, SAME), parts, sem)
    weights = weight_places(None, (near_weights, far_weights), None)
    spread_fields(grid_places(near, far), cells, SAME, weights, staged)
    finish(phases[0] + phases[1])
    add_rows(sums, parts, staged)


def add_same(cells, rows, near_weights, far_weights, near, far, sums):
    segs = segments(4, SAME)
    return pl.pallas_call(
        donor_same_kernel,
        out_shape=[resident(ROWS, LANES)] * SUMS,
        in_specs=[VMEM, HBM] + [VMEM] * (4 + SUMS),
        out_specs=[VMEM] * SUMS,
        scratch_shapes=[pltpu.VMEM((len(segs) * FRINGE, LANES), f32)] + index_scratch(segs),
        input_output_aliases={6 + w: w for w in range(SUMS)},
        compiler_params=params(8),
        cost_estimate=cost(9),
        name="add_same",
    )(cells, rows, near_weights, far_weights, near, far, *sums)


def donor_sides_kernel(cells, rows_hbm, before_weights, after_weights, before, after, *refs):
    refs = refs[SUMS:]
    adjoint, gram, sums, staged = refs[0], refs[1], refs[2 : 2 + SUMS], refs[2 + SUMS]
    parts, sem = refs[3 + SUMS : 3 + SUMS + WAYS], refs[3 + SUMS + WAYS]
    phases = index_copies(rows_hbm, segments(4, SIDES), parts, sem)
    weights = weight_places(before_weights, (None, None), after_weights)
    spread_fields({**pair_places(BEFORE, before), **pair_places(AFTER, after)}, cells, SIDES, weights, staged)
    finish(phases[0] + phases[1])
    add_rows(sums, parts, staged)
    lane = lanes((1, LANES))
    low, high = outer_rows(before, after)
    sums[0][0:1, :] = sums[0][0:1, :] - jnp.where(lane < PROBES, low, 0.0)
    end = sums[0][ROWS - 1 : ROWS, :]
    sums[0][ROWS - 1 : ROWS, :] = end - jnp.where(lane >= LANES - PROBES, high, 0.0)

    def total(start):
        at = rows_of(start, 8)
        value = sums[0][at, :]
        for part in sums[1:]:
            value = value + part[at, :]
        adjoint[at, :] = value

    each_row_block(total)

    def multiply(j, product):
        left_side, right_side = [], []
        for n in range(4):
            block = adjoint[aligned((j * 4 + n) * LANES, LANES), :]
            high, low = split(block)
            high_t, low_t = split(block.T)
            left_side += [high_t, high_t, low_t]
            right_side += [high, low, high]
        left_side = jnp.concatenate(left_side, axis=1)
        right_side = jnp.concatenate(right_side, axis=0)
        return product + jnp.dot(left_side, right_side, preferred_element_type=f32)

    product = lax.fori_loop(0, TILES // 4, multiply, jnp.zeros((LANES, LANES), f32))
    group = lanes((PROBES, LANES)) // PROBES
    folded = jnp.zeros((PROBES, LANES), f32)
    for g in range(GROUPS):
        folded = folded + jnp.where(group == g, product[g * PROBES : (g + 1) * PROBES, :], 0.0)
    for shift in (64, 32, 16):
        folded = folded + pltpu.roll(folded, shift, 1)
    gram[...] = folded[:, :PROBES]


def add_sides(cells, rows, before_weights, after_weights, before, after, sums):
    segs = segments(4, SIDES)
    outs = pl.pallas_call(
        donor_sides_kernel,
        out_shape=[resident(ROWS, LANES), jax.ShapeDtypeStruct((PROBES, PROBES), f32)]
        + [resident(ROWS, LANES)] * SUMS,
        in_specs=[VMEM, HBM] + [VMEM] * (4 + SUMS),
        out_specs=[VMEM] * (2 + SUMS),
        scratch_shapes=[pltpu.VMEM((len(segs) * FRINGE, LANES), f32)] + index_scratch(segs),
        input_output_aliases={6 + w: 2 + w for w in range(SUMS)},
        compiler_params=params(12),
        cost_estimate=cost(18),
        name="add_sides",
    )(cells, rows, before_weights, after_weights, before, after, *sums)
    return outs[0], outs[1]


def basis_kernel(total_cells, gram, adjoint, basis, factor, natural, sem):
    row = lax.broadcasted_iota(i32, (PROBES, 1), 0)
    left = gram[...] / f32(total_cells)
    right = jnp.where(lax.broadcasted_iota(i32, (PROBES, LANES), 0) == lanes((PROBES, LANES)) % PROBES, 1.0, 0.0)
    for j in range(PROBES):
        pivot = left[j : j + 1, j : j + 1]
        ratio = jnp.where(row > j, left[:, j : j + 1] / pivot, 0.0)
        root = jnp.sqrt(pivot)
        left_row, right_row = left[j : j + 1, :], right[j : j + 1, :]
        left = jnp.where(row == j, left_row / root, left - ratio * left_row)
        right = jnp.where(row == j, right_row / root, right - ratio * right_row)
    down = lax.broadcasted_iota(i32, (PROBES, PROBES), 0)
    factor[...] = jnp.where(lanes((PROBES, PROBES)) >= down, left, 0.0).T
    inverse = jnp.concatenate([right] * GROUPS, axis=0)
    same = lax.broadcasted_iota(i32, (LANES, LANES), 0) // PROBES == lanes((LANES, LANES)) // PROBES
    high, low = split(jnp.where(same, inverse, 0.0))
    left_side = jnp.concatenate([high, high, low], axis=1)

    def step(j, carry):
        for n in range(4):
            tile = j * 4 + n
            high, low = split(adjoint[aligned(tile * LANES, LANES), :])
            right_side = jnp.concatenate([high, low, high], axis=1)
            block = lax.dot_general(left_side, right_side, (((1,), (1,)), ((), ())), preferred_element_type=f32)
            for g in range(GROUPS):
                natural[:, aligned(g * ROWS + tile * LANES, LANES)] = block[g * PROBES : (g + 1) * PROBES, :]
        return carry

    lax.fori_loop(0, TILES // 4, step, 0)
    copies = [
        pltpu.make_async_copy(natural.at[pl.ds(p, 1), :], basis.at[p], sem.at[p]) for p in range(PROBES)
    ]
    for copy in copies:
        copy.start()
    finish(copies)


def basis_of(total_cells, gram, adjoint):
    return pl.pallas_call(
        functools.partial(basis_kernel, total_cells),
        out_shape=[
            jax.ShapeDtypeStruct((PROBES, 1, GROUPS * ROWS), f32),
            jax.ShapeDtypeStruct((PROBES, PROBES), f32),
        ],
        in_specs=[VMEM] * 2,
        out_specs=[FIXED, VMEM],
        scratch_shapes=[pltpu.VMEM((PROBES, GROUPS * ROWS), f32), pltpu.SemaphoreType.DMA((PROBES,))],
        compiler_params=params(8),
        cost_estimate=cost(6),
        name="basis",
    )(gram, adjoint)


def moved(value, place):
    grids, columns = (lax.axis_size(axis) for axis in AXES)
    route = []
    for g in range(grids):
        for c in range(columns):
            to_g, to_c = place(g, c)
            route.append((g * columns + c, (to_g % grids) * columns + to_c % columns))
    return lax.ppermute(value, AXES, route)


def along_grid(value, distance):
    return moved(value, lambda g, c: (g + distance, c))


def along_cell(value, distance):
    return moved(value, lambda g, c: (g, c + distance))


def ring_sum(value, step):
    after, across, before = (moved(value, lambda g, c, n=n: step(g, c, n)) for n in (1, 2, 3))
    return (value + across) + (before + after)


def summed(value):
    value = value + moved(value, lambda g, c: (g ^ 1, c))
    value = ring_sum(value, lambda g, c, n: (g + 2 * n, c))
    value = ring_sum(value, lambda g, c, n: (g, (c & 12) | ((c + n) & 3)))
    return ring_sum(value, lambda g, c, n: (g, c + 4 * n))


def body(probes, centre, lower_coef, upper_coef, donor_cells, receptor_cells, weights):
    donors = donor_cells[0]
    donor_rows = (donors & (ROWS - 1)).reshape(-1)
    receptor_rows = (receptor_cells & (ROWS - 1)).reshape(-1)
    near_weights, far_weights = along_grid(weights, -1)[0], along_grid(weights, -2)[0]
    table = table_of(probes)
    up, down = weight_relay(near_weights, far_weights, table)
    before_weights, after_weights = along_cell(up, 1), along_cell(down, -1)
    staged = rows_at_sides(table, donor_rows)
    up, down = side_sums(staged, donors, before_weights, after_weights)
    after, before = along_cell(up, 1), along_cell(down, -1)
    same = same_sums(table, donors, donor_rows, near_weights, far_weights)
    near, far = message_relay(before, same, after)
    near, far = along_grid(near, 1), along_grid(far, 2)
    c, l, u, *sums = forward(table, centre, lower_coef, upper_coef, before_weights, after_weights)
    tangent, far = couple(receptor_cells, receptor_rows, near, far, sums)
    far = along_grid(far, -2)
    near = along_grid(at_receptors(tangent, receptor_cells, receptor_rows), -1)
    sums = transposed(tangent, c, l, u)
    up, down = return_relay(near, far, tangent, l, u, sums[-1])
    before, after = along_cell(up, 1), along_cell(down, -1)
    sums = add_same(donors, donor_rows, near_weights, far_weights, near, far, sums)
    adjoint, gram = add_sides(donors, donor_rows, before_weights, after_weights, before, after, sums)
    total_cells = lax.axis_size("grid") * lax.axis_size("cell") * probes.shape[2]
    basis, factor = basis_of(total_cells, summed(gram), adjoint)
    return (basis, factor)


def solution(mesh):
    in_specs = (
        P(None, "grid", "cell"),
        P("grid", "cell"),
        P("grid", "cell"),
        P("grid", "cell"),
        P("grid", None, "cell"),
        P("grid", "cell"),
        P("grid", None, "cell"),
    )
    out_specs = (P(None, "grid", "cell"), P())
    return jax.shard_map(body, mesh=mesh, in_specs=in_specs, out_specs=out_specs, check_vma=False)
```

```python
import functools

import jax
import jax.numpy as jnp
from jax import lax
from jax.experimental import pallas as pl
from jax.experimental.pallas import tpu as pltpu
from jax.sharding import PartitionSpec as P

f32 = jnp.float32
i32 = jnp.int32
bf16 = jnp.bfloat16

PROBES = 16
GROUPS = 8
ROWS = 4096
LANES = 128
PARTNERS = 6
FRINGE = 1024
HALF = 3 * FRINGE
SLOTS = PARTNERS * FRINGE
TILES = ROWS // LANES
WAYS = 8
SUMS = 4
QUARTER = SLOTS // 4
UNROLL = 8

AXES = ("grid", "cell")

VMEM = pl.BlockSpec(memory_space=pltpu.VMEM)
HBM = pl.BlockSpec(memory_space=pl.ANY)
FIXED = pl.BlockSpec(memory_space=pltpu.HBM)


def aligned(start, size):
    return pl.ds(pl.multiple_of(start, size), size)


def rows_of(start, size):
    return pl.ds(pl.multiple_of(start, 8), size)


def split(x):
    high = x.astype(bf16)
    return high, (x - high.astype(f32)).astype(bf16)


def params(limit_mib):
    return pltpu.CompilerParams(vmem_limit_bytes=limit_mib << 20)


def cost(microseconds):
    return pl.CostEstimate(flops=0, transcendentals=0, bytes_accessed=microseconds * 3_000_000)


def resident(*shape):
    return pltpu.VMEM(shape, f32)


HEAD = 128


def segments(many, partners):
    return [(m, k) for m in range(many) for k in partners]


def index_scratch(segs):
    size = len(segs) * FRINGE // WAYS
    return [pltpu.SMEM((size,), i32)] * WAYS + [pltpu.SemaphoreType.DMA((3 * WAYS,))]


def index_copies(rows_hbm, segs, parts, sem):
    size = parts[0].shape[0]
    cuts = sorted({0, HEAD, size} | set(range(0, size, FRINGE)))
    phases = [[], []]
    for c in range(len(cuts) - 1):
        low, high = cuts[c], cuts[c + 1]
        for w in range(WAYS):
            seg, offset = divmod(w * size + low, FRINGE)
            start = segs[seg][0] * SLOTS + segs[seg][1] * FRINGE + offset
            copy = pltpu.make_async_copy(
                rows_hbm.at[pl.ds(start, high - low)], parts[w].at[pl.ds(low, high - low)], sem.at[c * WAYS + w]
            )
            copy.start()
            phases[min(c, 1)].append(copy)
    return phases


def finish(copies):
    for copy in copies:
        copy.wait()


def row_steps(parts, low, high, step):
    def outer(j, carry):
        for n in range(UNROLL):
            q = low + j * UNROLL + n
            for w in range(WAYS):
                step(w, q, parts[w][q])
        return carry

    lax.fori_loop(0, (high - low) // UNROLL, outer, 0)


def gather_rows(table, parts, staged, phases):
    count = parts[0].shape[0]

    def step(w, q, row):
        staged[pl.ds(w * count + q, 1), :] = table[pl.ds(row, 1), :]

    finish(phases[0])
    row_steps(parts, 0, HEAD, step)
    finish(phases[1])
    row_steps(parts, HEAD, count, step)


def clear(sums):
    def step(j, carry):
        for total in sums:
            for n in range(4):
                total[rows_of(j * 32 + n * 8, 8), :] = jnp.zeros((8, LANES), f32)
        return carry

    lax.fori_loop(0, ROWS // 32, step, 0)


def add_rows(sums, parts, staged):
    count = parts[0].shape[0]

    def outer(j, carry):
        for n in range(UNROLL):
            q = j * UNROLL + n
            for half in range(2):
                total = sums[half + n % 2 * 2]
                lists = [2 * m + half for m in range(4)]
                rows = [parts[w][q] for w in lists]
                old = [total[pl.ds(row, 1), :] for row in rows]
                new = [value + staged[pl.ds(w * count + q, 1), :] for value, w in zip(old, lists)]
                for row, value in zip(rows, new):
                    total[pl.ds(row, 1), :] = value
        return carry

    lax.fori_loop(0, count // UNROLL, outer, 0)


def groups_of(cells, m, offset):
    return jnp.broadcast_to(cells[m : m + 1, aligned(offset, LANES)], (8, LANES)) >> 12


def each_block(many, step):
    unroll = 8 // many

    def outer(j, carry):
        for n in range(unroll):
            step(j * unroll + n)
        return carry

    lax.fori_loop(0, FRINGE // LANES // unroll, outer, 0)


def select_fields(staged, cells, partners, weights, out):
    many = cells.shape[0]
    for n, k in enumerate(partners):

        def step(b):
            total = [jnp.zeros((8, LANES), f32)] * 2
            for m in range(many):
                field = staged[aligned((m * len(partners) + n) * FRINGE + b * LANES, LANES), :].T
                group = groups_of(cells, m, k * FRINGE + b * LANES)
                scale = 1.0
                if weights is not None:
                    ref, row, column = weights[k]
                    scale = ref[row + m : row + m + 1, aligned(column + b * LANES, LANES)]
                    scale = jnp.broadcast_to(scale, (8, LANES))
                for g in range(GROUPS):
                    factor = jnp.where(group == g, scale, 0.0)
                    for h in range(2):
                        at = g * PROBES + h * 8
                        total[h] = total[h] + field[at : at + 8, :] * factor
            ref, row, column = out[k]
            for h in range(2):
                ref[row + h * 8 : row + h * 8 + 8, aligned(column + b * LANES, LANES)] = total[h]

        each_block(many, step)


def spread_group(fields, cells, outs):
    group = [value >> 12 for value in cells]
    row = [value & (ROWS - 1) for value in cells]
    terms = [[jnp.where(group[m] == g, fields[m][h], 0.0) for g in range(GROUPS) for h in range(2)] for m in range(4)]
    for m in range(4):
        same = [row[m] == row[i] for i in range(m)]
        block = []
        for v in range(2 * GROUPS):
            value = terms[m][v]
            for i in range(m):
                value = value + jnp.where(same[i], terms[i][v], 0.0)
            block.append(value)
        ref, at = outs[m]
        ref[aligned(at, LANES), :] = jnp.concatenate(block, axis=0).T


def block_of(ref, row, column):
    return jnp.broadcast_to(ref[row : row + 1, aligned(column, LANES)], (8, LANES))


def field_of(place, b):
    ref, row, column = place
    return [ref[row + h * 8 : row + h * 8 + 8, aligned(column + b * LANES, LANES)] for h in range(2)]


def spread_at_donors(messages, cells, partners, weights, staged):
    for n, k in enumerate(partners):

        def step(b):
            field = field_of(messages[k], b)
            ref, row, column = weights[k]
            scale = [block_of(ref, row + m, column + b * LANES) for m in range(4)]
            fields = [[part * scale[m] for part in field] for m in range(4)]
            blocks = [block_of(cells, m, k * FRINGE + b * LANES) for m in range(4)]
            spread_group(fields, blocks, [(staged, (m * len(partners) + n) * FRINGE + b * LANES) for m in range(4)])

        each_block(4, step)


def spread_at_receptors(messages, cells, staged):
    for part in range(3):

        def step(j, carry):
            fields, blocks, outs = [], [], []
            for m in range(4):
                k, shift = divmod(m * QUARTER + part * 4 * LANES, FRINGE)
                fields.append(field_of(messages[k], j + shift // LANES))
                at = m * QUARTER + (part * 4 + j) * LANES
                blocks.append(block_of(cells, 0, at))
                outs.append((staged, at))
            spread_group(fields, blocks, outs)
            return carry

        lax.fori_loop(0, 4, step, 0, unroll=2)


def lanes(shape):
    return lax.broadcasted_iota(i32, shape, len(shape) - 1)


def fill_ends(padded, low, high):
    lane = lanes((1, LANES))
    before = pltpu.roll(padded[ROWS : ROWS + 8, :], PROBES, 1)[7:8, :]
    after = pltpu.roll(padded[8:16, :], LANES - PROBES, 1)[0:1, :]
    padded[7:8, :] = jnp.where(lane < PROBES, low, before)
    padded[ROWS + 8 : ROWS + 9, :] = jnp.where(lane >= LANES - PROBES, high, after)


def each_row_block(step):
    def outer(j, carry):
        for u in range(4):
            step(j * 32 + u * 8)
        return carry

    lax.fori_loop(0, ROWS // 32, outer, 0)


def table_kernel(probes, table, natural, sem):
    copies = [
        pltpu.make_async_copy(probes.at[p], natural.at[pl.ds(p, 1), :], sem.at[p]) for p in range(PROBES)
    ]
    for copy in copies:
        copy.start()
    finish(copies)

    def step(j, carry):
        for n in range(4):
            tile = j * 4 + n
            parts = [natural[:, aligned(g * ROWS + tile * LANES, LANES)] for g in range(GROUPS)]
            table[aligned(tile * LANES, LANES), :] = jnp.concatenate(parts, axis=0).T
        return carry

    lax.fori_loop(0, TILES // 4, step, 0)


def table_of(probes):
    return pl.pallas_call(
        table_kernel,
        out_shape=resident(ROWS, LANES),
        in_specs=[FIXED],
        out_specs=VMEM,
        scratch_shapes=[pltpu.VMEM((PROBES, GROUPS * ROWS), f32), pltpu.SemaphoreType.DMA((PROBES,))],
        compiler_params=params(8),
        cost_estimate=cost(3),
        name="table",
    )(probes)


BEFORE, SAME, AFTER = (0, 3), (1, 4), (2, 5)
SIDES = BEFORE + AFTER
NEAR, FAR = (0, 1, 2), (3, 4, 5)
EDGE = slice(FRINGE, FRINGE + LANES)


def weight_places(before, same, after):
    return {
        0: (before, 0, 0),
        3: (before, 4, 0),
        1: (same[0], 0, FRINGE),
        4: (same[1], 0, 4 * FRINGE),
        2: (after, 0, 0),
        5: (after, 4, 0),
    }


def pair_places(pair, ref):
    return {pair[0]: (ref, 0, 0), pair[1]: (ref, PROBES, 0)}


def grid_places(near, far):
    places = {k: (near, n * PROBES, 0) for n, k in enumerate(NEAR)}
    places.update({k: (far, n * PROBES, 0) for n, k in enumerate(FAR)})
    return places


def simple_call(kernel, out_shape, operands, name):
    return pl.pallas_call(
        kernel,
        out_shape=out_shape,
        in_specs=[VMEM] * len(operands),
        out_specs=[VMEM] * len(out_shape),
        compiler_params=params(8),
        cost_estimate=cost(1),
        name=name,
    )(*operands)


def weight_relay_kernel(near, far, table, up, down):
    for pair, out, rows in ((BEFORE, up, slice(ROWS - 8, ROWS)), (AFTER, down, slice(0, 8))):
        for n, ref in enumerate((near, far)):
            start = pair[n] * FRINGE
            out[n * 4 : n * 4 + 4, 0:FRINGE] = ref[:, start : start + FRINGE]
        out[:, EDGE] = table[rows, :]


def weight_relay(near, far, table):
    shape = jax.ShapeDtypeStruct((8, FRINGE + LANES), f32)
    return simple_call(weight_relay_kernel, [shape] * 2, (near, far, table), "weight_relay")


def rows_kernel(table, rows_hbm, staged, *rest):
    parts, sem = rest[:WAYS], rest[WAYS]
    gather_rows(table, parts, staged, index_copies(rows_hbm, segments(4, SIDES), parts, sem))


def rows_at_sides(table, rows):
    segs = segments(4, SIDES)
    return pl.pallas_call(
        rows_kernel,
        out_shape=resident(len(segs) * FRINGE, LANES),
        in_specs=[VMEM, HBM],
        out_specs=VMEM,
        scratch_shapes=index_scratch(segs),
        compiler_params=params(8),
        cost_estimate=cost(11),
        name="rows_at_sides",
    )(table, rows)


PAIR = jax.ShapeDtypeStruct((2 * PROBES, FRINGE), f32)
TRIPLE = jax.ShapeDtypeStruct((3 * PROBES, FRINGE), f32)


def side_sums_kernel(staged, cells, before, after, up, down):
    places = {**pair_places(AFTER, up), **pair_places(BEFORE, down)}
    select_fields(staged, cells, SIDES, weight_places(before, (None, None), after), places)


def side_sums(staged, cells, before, after):
    return simple_call(side_sums_kernel, [PAIR] * 2, (staged, cells, before, after), "side_sums")


def same_sums_kernel(table, cells, rows_hbm, near, far, out, staged, *rest):
    parts, sem = rest[:WAYS], rest[WAYS]
    gather_rows(table, parts, staged, index_copies(rows_hbm, segments(4, SAME), parts, sem))
    select_fields(staged, cells, SAME, weight_places(None, (near, far), None), pair_places(SAME, out))


def same_sums(table, cells, rows, near, far):
    segs = segments(4, SAME)
    return pl.pallas_call(
        same_sums_kernel,
        out_shape=PAIR,
        in_specs=[VMEM, VMEM, HBM, VMEM, VMEM],
        out_specs=VMEM,
        scratch_shapes=[pltpu.VMEM((len(segs) * FRINGE, LANES), f32)] + index_scratch(segs),
        compiler_params=params(8),
        cost_estimate=cost(8),
        name="same_sums",
    )(table, cells, rows, near, far)


def message_relay_kernel(before, same, after, near, far):
    for n, out in enumerate((near, far)):
        for i, ref in enumerate((before, same, after)):
            out[i * PROBES : (i + 1) * PROBES, :] = ref[n * PROBES : (n + 1) * PROBES, :]


def message_relay(before, same, after):
    return simple_call(message_relay_kernel, [TRIPLE] * 2, (before, same, after), "message_relay")


def end_flags():
    column = lax.axis_index("cell")
    return (column > 0).astype(f32), (column < lax.axis_size("cell") - 1).astype(f32)


def outer_rows(before, after):
    has_low, has_high = end_flags()
    low = pltpu.roll(before[0:8, EDGE], PROBES, 1)[7:8, :] * has_low
    high = pltpu.roll(after[0:8, EDGE], LANES - PROBES, 1)[0:1, :] * has_high
    return low, high


def forward_kernel(table, centre, lower, upper, before, after, c_out, l_out, u_out, *rest):
    sums, padded = rest[:SUMS], rest[SUMS]

    def step(j, carry):
        for n in range(2):
            tile = j * 2 + n
            at = aligned(tile * LANES, LANES)
            padded[rows_of(tile * LANES + 8, LANES), :] = table[at, :]
            for ref, out in ((centre, c_out), (lower, l_out), (upper, u_out)):
                parts = [
                    jnp.broadcast_to(ref[:, aligned(g * ROWS + tile * LANES, LANES)], (PROBES, LANES))
                    for g in range(GROUPS)
                ]
                out[at, :] = jnp.concatenate(parts, axis=0).T
        return carry

    lax.fori_loop(0, TILES // 2, step, 0)
    fill_ends(padded, *outer_rows(before, after))

    def stencil(start):
        at = rows_of(start, 8)
        sums[0][at, :] = (
            c_out[at, :] * padded[rows_of(start + 8, 8), :]
            - l_out[at, :] * padded[pl.ds(start + 7, 8), :]
            - u_out[at, :] * padded[pl.ds(start + 9, 8), :]
        )

    each_row_block(stencil)
    clear(sums[1:])


def forward(table, centre, lower, upper, before, after):
    return pl.pallas_call(
        forward_kernel,
        out_shape=[resident(ROWS, LANES)] * (3 + SUMS),
        in_specs=[VMEM] * 6,
        out_specs=[VMEM] * (3 + SUMS),
        scratch_shapes=[pltpu.VMEM((ROWS + 16, LANES), f32)],
        compiler_params=params(8),
        cost_estimate=cost(7),
        name="forward",
    )(table, centre, lower, upper, before, after)


def couple_kernel(cells, rows_hbm, near, far, *refs):
    refs = refs[SUMS:]
    tangent, out, sums = refs[0], refs[1], refs[2 : 2 + SUMS]
    staged, staged_far = refs[2 + SUMS : 4 + SUMS]
    refs = refs[4 + SUMS :]
    parts, sem, parts_far, sem_far = refs[:WAYS], refs[WAYS], refs[WAYS + 1 : 2 * WAYS + 1], refs[2 * WAYS + 1]
    every = NEAR + FAR
    phases = index_copies(rows_hbm, segments(1, every), parts, sem)
    phases_far = index_copies(rows_hbm, segments(1, FAR), parts_far, sem_far)
    spread_at_receptors(grid_places(near, far), cells, staged)
    finish(phases[0] + phases[1])
    add_rows(sums, parts, staged)

    def total(start):
        at = rows_of(start, 8)
        value = sums[0][at, :]
        for part in sums[1:]:
            value = value + part[at, :]
        tangent[at, :] = value

    each_row_block(total)
    gather_rows(tangent, parts_far, staged_far, phases_far)
    select_fields(staged_far, cells, FAR, None, grid_places(None, out))


def couple(cells, rows, near, far, sums):
    every, some = segments(1, NEAR + FAR), segments(1, FAR)
    outs = pl.pallas_call(
        couple_kernel,
        out_shape=[resident(ROWS, LANES), TRIPLE] + [resident(ROWS, LANES)] * SUMS,
        in_specs=[VMEM, HBM] + [VMEM] * (2 + SUMS),
        out_specs=[VMEM] * (2 + SUMS),
        scratch_shapes=[pltpu.VMEM((SLOTS, LANES), f32), pltpu.VMEM((SLOTS // 2, LANES), f32)]
        + index_scratch(every)
        + index_scratch(some),
        input_output_aliases={4 + w: 2 + w for w in range(SUMS)},
        compiler_params=params(8),
        cost_estimate=cost(11),
        name="couple",
    )(cells, rows, near, far, *sums)
    return outs[0], outs[1]


def receptor_kernel(tangent, cells, rows_hbm, out, staged, *rest):
    parts, sem = rest[:WAYS], rest[WAYS]
    gather_rows(tangent, parts, staged, index_copies(rows_hbm, segments(1, NEAR), parts, sem))
    select_fields(staged, cells, NEAR, None, grid_places(out, None))


def at_receptors(tangent, cells, rows):
    segs = segments(1, NEAR)
    return pl.pallas_call(
        receptor_kernel,
        out_shape=TRIPLE,
        in_specs=[VMEM, VMEM, HBM],
        out_specs=VMEM,
        scratch_shapes=[pltpu.VMEM((len(segs) * FRINGE, LANES), f32)] + index_scratch(segs),
        compiler_params=params(8),
        cost_estimate=cost(3),
        name="at_receptors",
    )(tangent, cells, rows)


def return_relay_kernel(near, far, tangent, lower, upper, ready, up, down):
    for n, ref in enumerate((near, far)):
        at = slice(n * PROBES, (n + 1) * PROBES)
        up[at, 0:FRINGE] = ref[0:PROBES, :]
        down[at, 0:FRINGE] = ref[2 * PROBES : 3 * PROBES, :]
    end = slice(ROWS - 8, ROWS)
    up[0:8, EDGE] = upper[end, :] * tangent[end, :]
    down[0:8, EDGE] = lower[0:8, :] * tangent[0:8, :]


def return_relay(near, far, tangent, lower, upper, ready):
    shape = jax.ShapeDtypeStruct((2 * PROBES, FRINGE + LANES), f32)
    return simple_call(return_relay_kernel, [shape] * 2, (near, far, tangent, lower, upper, ready), "return_relay")


def transposed_kernel(tangent, centre, lower, upper, *rest):
    sums, raised, lowered = rest[:SUMS], rest[SUMS], rest[SUMS + 1]

    def products(start):
        at = rows_of(start, 8)
        value = tangent[at, :]
        raised[rows_of(start + 8, 8), :] = upper[at, :] * value
        lowered[rows_of(start + 8, 8), :] = lower[at, :] * value

    each_row_block(products)
    nothing = jnp.zeros((1, LANES), f32)
    fill_ends(raised, nothing, nothing)
    fill_ends(lowered, nothing, nothing)

    def stencil(start):
        at = rows_of(start, 8)
        sums[0][at, :] = (
            centre[at, :] * tangent[at, :] - raised[pl.ds(start + 7, 8), :] - lowered[pl.ds(start + 9, 8), :]
        )

    each_row_block(stencil)
    clear(sums[1:])


def transposed(tangent, centre, lower, upper):
    return pl.pallas_call(
        transposed_kernel,
        out_shape=[resident(ROWS, LANES)] * SUMS,
        in_specs=[VMEM] * 4,
        out_specs=[VMEM] * SUMS,
        scratch_shapes=[pltpu.VMEM((ROWS + 16, LANES), f32)] * 2,
        compiler_params=params(8),
        cost_estimate=cost(4),
        name="transposed",
    )(tangent, centre, lower, upper)


def donor_same_kernel(cells, rows_hbm, near_weights, far_weights, near, far, *refs):
    refs = refs[SUMS:]
    sums, staged, parts, sem = refs[:SUMS], refs[SUMS], refs[SUMS + 1 : SUMS + WAYS + 1], refs[SUMS + WAYS + 1]
    phases = index_copies(rows_hbm, segments(4, SAME), parts, sem)
    weights = weight_places(None, (near_weights, far_weights), None)
    spread_at_donors(grid_places(near, far), cells, SAME, weights, staged)
    finish(phases[0] + phases[1])
    add_rows(sums, parts, staged)


def add_same(cells, rows, near_weights, far_weights, near, far, sums):
    segs = segments(4, SAME)
    return pl.pallas_call(
        donor_same_kernel,
        out_shape=[resident(ROWS, LANES)] * SUMS,
        in_specs=[VMEM, HBM] + [VMEM] * (4 + SUMS),
        out_specs=[VMEM] * SUMS,
        scratch_shapes=[pltpu.VMEM((len(segs) * FRINGE, LANES), f32)] + index_scratch(segs),
        input_output_aliases={6 + w: w for w in range(SUMS)},
        compiler_params=params(8),
        cost_estimate=cost(9),
        name="add_same",
    )(cells, rows, near_weights, far_weights, near, far, *sums)


def donor_sides_kernel(cells, rows_hbm, before_weights, after_weights, before, after, *refs):
    refs = refs[SUMS:]
    adjoint, gram, sums, staged = refs[0], refs[1], refs[2 : 2 + SUMS], refs[2 + SUMS]
    parts, sem = refs[3 + SUMS : 3 + SUMS + WAYS], refs[3 + SUMS + WAYS]
    phases = index_copies(rows_hbm, segments(4, SIDES), parts, sem)
    weights = weight_places(before_weights, (None, None), after_weights)
    spread_at_donors({**pair_places(BEFORE, before), **pair_places(AFTER, after)}, cells, SIDES, weights, staged)
    finish(phases[0] + phases[1])
    add_rows(sums, parts, staged)
    lane = lanes((1, LANES))
    low, high = outer_rows(before, after)
    sums[0][0:1, :] = sums[0][0:1, :] - jnp.where(lane < PROBES, low, 0.0)
    end = sums[0][ROWS - 1 : ROWS, :]
    sums[0][ROWS - 1 : ROWS, :] = end - jnp.where(lane >= LANES - PROBES, high, 0.0)

    def total(start):
        at = rows_of(start, 8)
        value = sums[0][at, :]
        for part in sums[1:]:
            value = value + part[at, :]
        adjoint[at, :] = value

    each_row_block(total)

    def multiply(j, product):
        left_side, right_side = [], []
        for n in range(4):
            block = adjoint[aligned((j * 4 + n) * LANES, LANES), :]
            high, low = split(block)
            high_t, low_t = split(block.T)
            left_side += [high_t, high_t, low_t]
            right_side += [high, low, high]
        left_side = jnp.concatenate(left_side, axis=1)
        right_side = jnp.concatenate(right_side, axis=0)
        return product + jnp.dot(left_side, right_side, preferred_element_type=f32)

    product = lax.fori_loop(0, TILES // 4, multiply, jnp.zeros((LANES, LANES), f32))
    group = lanes((PROBES, LANES)) // PROBES
    folded = jnp.zeros((PROBES, LANES), f32)
    for g in range(GROUPS):
        folded = folded + jnp.where(group == g, product[g * PROBES : (g + 1) * PROBES, :], 0.0)
    for shift in (64, 32, 16):
        folded = folded + pltpu.roll(folded, shift, 1)
    gram[...] = folded[:, :PROBES]


def add_sides(cells, rows, before_weights, after_weights, before, after, sums):
    segs = segments(4, SIDES)
    outs = pl.pallas_call(
        donor_sides_kernel,
        out_shape=[resident(ROWS, LANES), jax.ShapeDtypeStruct((PROBES, PROBES), f32)]
        + [resident(ROWS, LANES)] * SUMS,
        in_specs=[VMEM, HBM] + [VMEM] * (4 + SUMS),
        out_specs=[VMEM] * (2 + SUMS),
        scratch_shapes=[pltpu.VMEM((len(segs) * FRINGE, LANES), f32)] + index_scratch(segs),
        input_output_aliases={6 + w: 2 + w for w in range(SUMS)},
        compiler_params=params(12),
        cost_estimate=cost(18),
        name="add_sides",
    )(cells, rows, before_weights, after_weights, before, after, *sums)
    return outs[0], outs[1]


def basis_kernel(total_cells, gram, adjoint, basis, factor, natural, sem):
    row = lax.broadcasted_iota(i32, (PROBES, 1), 0)
    left = gram[...] / f32(total_cells)
    right = jnp.where(lax.broadcasted_iota(i32, (PROBES, LANES), 0) == lanes((PROBES, LANES)) % PROBES, 1.0, 0.0)
    for j in range(PROBES):
        pivot = left[j : j + 1, j : j + 1]
        ratio = jnp.where(row > j, left[:, j : j + 1] / pivot, 0.0)
        root = jnp.sqrt(pivot)
        left_row, right_row = left[j : j + 1, :], right[j : j + 1, :]
        left = jnp.where(row == j, left_row / root, left - ratio * left_row)
        right = jnp.where(row == j, right_row / root, right - ratio * right_row)
    down = lax.broadcasted_iota(i32, (PROBES, PROBES), 0)
    factor[...] = jnp.where(lanes((PROBES, PROBES)) >= down, left, 0.0).T
    inverse = jnp.concatenate([right] * GROUPS, axis=0)
    same = lax.broadcasted_iota(i32, (LANES, LANES), 0) // PROBES == lanes((LANES, LANES)) // PROBES
    high, low = split(jnp.where(same, inverse, 0.0))
    left_side = jnp.concatenate([high, high, low], axis=1)

    def step(j, carry):
        for n in range(4):
            tile = j * 4 + n
            high, low = split(adjoint[aligned(tile * LANES, LANES), :])
            right_side = jnp.concatenate([high, low, high], axis=1)
            block = lax.dot_general(left_side, right_side, (((1,), (1,)), ((), ())), preferred_element_type=f32)
            for g in range(GROUPS):
                natural[:, aligned(g * ROWS + tile * LANES, LANES)] = block[g * PROBES : (g + 1) * PROBES, :]
        return carry

    lax.fori_loop(0, TILES // 4, step, 0)
    copies = [
        pltpu.make_async_copy(natural.at[pl.ds(p, 1), :], basis.at[p], sem.at[p]) for p in range(PROBES)
    ]
    for copy in copies:
        copy.start()
    finish(copies)


def basis_of(total_cells, gram, adjoint):
    return pl.pallas_call(
        functools.partial(basis_kernel, total_cells),
        out_shape=[
            jax.ShapeDtypeStruct((PROBES, 1, GROUPS * ROWS), f32),
            jax.ShapeDtypeStruct((PROBES, PROBES), f32),
        ],
        in_specs=[VMEM] * 2,
        out_specs=[FIXED, VMEM],
        scratch_shapes=[pltpu.VMEM((PROBES, GROUPS * ROWS), f32), pltpu.SemaphoreType.DMA((PROBES,))],
        compiler_params=params(8),
        cost_estimate=cost(6),
        name="basis",
    )(gram, adjoint)


def moved(value, place):
    grids, columns = (lax.axis_size(axis) for axis in AXES)
    route = []
    for g in range(grids):
        for c in range(columns):
            to_g, to_c = place(g, c)
            route.append((g * columns + c, (to_g % grids) * columns + to_c % columns))
    return lax.ppermute(value, AXES, route)


def along_grid(value, distance):
    return moved(value, lambda g, c: (g + distance, c))


def along_cell(value, distance):
    return moved(value, lambda g, c: (g, c + distance))


def ring_sum(value, step):
    after, across, before = (moved(value, lambda g, c, n=n: step(g, c, n)) for n in (1, 2, 3))
    return (value + across) + (before + after)


def summed(value):
    value = value + moved(value, lambda g, c: (g ^ 1, c))
    value = ring_sum(value, lambda g, c, n: (g + 2 * n, c))
    value = ring_sum(value, lambda g, c, n: (g, (c & 12) | ((c + n) & 3)))
    return ring_sum(value, lambda g, c, n: (g, c + 4 * n))


def body(probes, centre, lower_coef, upper_coef, donor_cells, receptor_cells, weights):
    donors = donor_cells[0]
    donor_rows = (donors & (ROWS - 1)).reshape(-1)
    receptor_rows = (receptor_cells & (ROWS - 1)).reshape(-1)
    near_weights, far_weights = along_grid(weights, -1)[0], along_grid(weights, -2)[0]
    table = table_of(probes)
    up, down = weight_relay(near_weights, far_weights, table)
    before_weights, after_weights = along_cell(up, 1), along_cell(down, -1)
    staged = rows_at_sides(table, donor_rows)
    up, down = side_sums(staged, donors, before_weights, after_weights)
    after, before = along_cell(up, 1), along_cell(down, -1)
    same = same_sums(table, donors, donor_rows, near_weights, far_weights)
    near, far = message_relay(before, same, after)
    near, far = along_grid(near, 1), along_grid(far, 2)
    c, l, u, *sums = forward(table, centre, lower_coef, upper_coef, before_weights, after_weights)
    tangent, far = couple(receptor_cells, receptor_rows, near, far, sums)
    far = along_grid(far, -2)
    near = along_grid(at_receptors(tangent, receptor_cells, receptor_rows), -1)
    sums = transposed(tangent, c, l, u)
    up, down = return_relay(near, far, tangent, l, u, sums[-1])
    before, after = along_cell(up, 1), along_cell(down, -1)
    sums = add_same(donors, donor_rows, near_weights, far_weights, near, far, sums)
    adjoint, gram = add_sides(donors, donor_rows, before_weights, after_weights, before, after, sums)
    total_cells = lax.axis_size("grid") * lax.axis_size("cell") * probes.shape[2]
    basis, factor = basis_of(total_cells, summed(gram), adjoint)
    return (basis, factor)


def solution(mesh):
    in_specs = (
        P(None, "grid", "cell"),
        P("grid", "cell"),
        P("grid", "cell"),
        P("grid", "cell"),
        P("grid", None, "cell"),
        P("grid", "cell"),
        P("grid", None, "cell"),
    )
    out_specs = (P(None, "grid", "cell"), P())
    return jax.shard_map(body, mesh=mesh, in_specs=in_specs, out_specs=out_specs, check_vma=False)
```

```python
import functools

import jax
import jax.numpy as jnp
from jax import lax
from jax.experimental import pallas as pl
from jax.experimental.pallas import tpu as pltpu
from jax.sharding import PartitionSpec as P

f32 = jnp.float32
i32 = jnp.int32
bf16 = jnp.bfloat16

PROBES = 16
GROUPS = 8
ROWS = 4096
LANES = 128
PARTNERS = 6
FRINGE = 1024
HALF = 3 * FRINGE
SLOTS = PARTNERS * FRINGE
TILES = ROWS // LANES
WAYS = 8
SUMS = 4
QUARTER = SLOTS // 4
UNROLL = 8

AXES = ("grid", "cell")

VMEM = pl.BlockSpec(memory_space=pltpu.VMEM)
HBM = pl.BlockSpec(memory_space=pl.ANY)
FIXED = pl.BlockSpec(memory_space=pltpu.HBM)


def aligned(start, size):
    return pl.ds(pl.multiple_of(start, size), size)


def rows_of(start, size):
    return pl.ds(pl.multiple_of(start, 8), size)


def split(x):
    high = x.astype(bf16)
    return high, (x - high.astype(f32)).astype(bf16)


def params(limit_mib):
    return pltpu.CompilerParams(vmem_limit_bytes=limit_mib << 20)


def cost(microseconds):
    return pl.CostEstimate(flops=0, transcendentals=0, bytes_accessed=microseconds * 3_000_000)


def resident(*shape):
    return pltpu.VMEM(shape, f32)


HEAD = 128


def segments(many, partners):
    return [(m, k) for m in range(many) for k in partners]


def index_scratch(segs):
    size = len(segs) * FRINGE // WAYS
    return [pltpu.SMEM((size,), i32)] * WAYS + [pltpu.SemaphoreType.DMA((3 * WAYS,))]


def index_copies(rows_hbm, segs, parts, sem):
    size = parts[0].shape[0]
    cuts = sorted({0, HEAD, size} | set(range(0, size, FRINGE)))
    phases = [[], []]
    for c in range(len(cuts) - 1):
        low, high = cuts[c], cuts[c + 1]
        for w in range(WAYS):
            seg, offset = divmod(w * size + low, FRINGE)
            start = segs[seg][0] * SLOTS + segs[seg][1] * FRINGE + offset
            copy = pltpu.make_async_copy(
                rows_hbm.at[pl.ds(start, high - low)], parts[w].at[pl.ds(low, high - low)], sem.at[c * WAYS + w]
            )
            copy.start()
            phases[min(c, 1)].append(copy)
    return phases


def finish(copies):
    for copy in copies:
        copy.wait()


def row_steps(parts, low, high, step):
    def outer(j, carry):
        for n in range(UNROLL):
            q = low + j * UNROLL + n
            for w in range(WAYS):
                step(w, q, parts[w][q])
        return carry

    lax.fori_loop(0, (high - low) // UNROLL, outer, 0)


def gather_rows(table, parts, staged, phases):
    count = parts[0].shape[0]

    def step(w, q, row):
        staged[pl.ds(w * count + q, 1), :] = table[pl.ds(row, 1), :]

    finish(phases[0])
    row_steps(parts, 0, HEAD, step)
    finish(phases[1])
    row_steps(parts, HEAD, count, step)


def clear(sums):
    def step(j, carry):
        for total in sums:
            for n in range(4):
                total[rows_of(j * 32 + n * 8, 8), :] = jnp.zeros((8, LANES), f32)
        return carry

    lax.fori_loop(0, ROWS // 32, step, 0)


def add_rows(sums, parts, staged):
    count = parts[0].shape[0]

    def outer(j, carry):
        for n in range(UNROLL):
            q = j * UNROLL + n
            for half in range(2):
                total = sums[half + n % 2 * 2]
                lists = [2 * m + half for m in range(4)]
                rows = [parts[w][q] for w in lists]
                old = [total[pl.ds(row, 1), :] for row in rows]
                new = [value + staged[pl.ds(w * count + q, 1), :] for value, w in zip(old, lists)]
                for row, value in zip(rows, new):
                    total[pl.ds(row, 1), :] = value
        return carry

    lax.fori_loop(0, count // UNROLL, outer, 0)


def groups_of(cells, m, offset):
    return jnp.broadcast_to(cells[m : m + 1, aligned(offset, LANES)], (8, LANES)) >> 12


def each_block(many, step):
    unroll = 8 // many

    def outer(j, carry):
        for n in range(unroll):
            step(j * unroll + n)
        return carry

    lax.fori_loop(0, FRINGE // LANES // unroll, outer, 0)


def select_fields(staged, cells, partners, weights, out):
    many = cells.shape[0]
    for n, k in enumerate(partners):

        def step(b):
            total = [jnp.zeros((8, LANES), f32)] * 2
            for m in range(many):
                field = staged[aligned((m * len(partners) + n) * FRINGE + b * LANES, LANES), :].T
                group = groups_of(cells, m, k * FRINGE + b * LANES)
                scale = 1.0
                if weights is not None:
                    ref, row, column = weights[k]
                    scale = ref[row + m : row + m + 1, aligned(column + b * LANES, LANES)]
                    scale = jnp.broadcast_to(scale, (8, LANES))
                for g in range(GROUPS):
                    factor = jnp.where(group == g, scale, 0.0)
                    for h in range(2):
                        at = g * PROBES + h * 8
                        total[h] = total[h] + field[at : at + 8, :] * factor
            ref, row, column = out[k]
            for h in range(2):
                ref[row + h * 8 : row + h * 8 + 8, aligned(column + b * LANES, LANES)] = total[h]

        each_block(many, step)


def spread_group(fields, cells, outs):
    group = [value >> 12 for value in cells]
    row = [value & (ROWS - 1) for value in cells]
    terms = [[jnp.where(group[m] == g, fields[m][h], 0.0) for g in range(GROUPS) for h in range(2)] for m in range(4)]
    for m in range(4):
        same = [row[m] == row[i] for i in range(m)]
        block = []
        for v in range(2 * GROUPS):
            value = terms[m][v]
            for i in range(m):
                value = value + jnp.where(same[i], terms[i][v], 0.0)
            block.append(value)
        ref, at = outs[m]
        ref[aligned(at, LANES), :] = jnp.concatenate(block, axis=0).T


def block_of(ref, row, column):
    return jnp.broadcast_to(ref[row : row + 1, aligned(column, LANES)], (8, LANES))


def field_of(place, b):
    ref, row, column = place
    return [ref[row + h * 8 : row + h * 8 + 8, aligned(column + b * LANES, LANES)] for h in range(2)]


def spread_at_donors(messages, cells, partners, weights, staged):
    for n, k in enumerate(partners):

        def step(b):
            field = field_of(messages[k], b)
            ref, row, column = weights[k]
            scale = [block_of(ref, row + m, column + b * LANES) for m in range(4)]
            fields = [[part * scale[m] for part in field] for m in range(4)]
            blocks = [block_of(cells, m, k * FRINGE + b * LANES) for m in range(4)]
            spread_group(fields, blocks, [(staged, (m * len(partners) + n) * FRINGE + b * LANES) for m in range(4)])

        each_block(4, step)


def spread_at_receptors(messages, cells, staged):
    for part in range(3):

        def step(j, carry):
            fields, blocks, outs = [], [], []
            for m in range(4):
                k, shift = divmod(m * QUARTER + part * 4 * LANES, FRINGE)
                fields.append(field_of(messages[k], j + shift // LANES))
                at = m * QUARTER + (part * 4 + j) * LANES
                blocks.append(block_of(cells, 0, at))
                outs.append((staged, at))
            spread_group(fields, blocks, outs)
            return carry

        lax.fori_loop(0, 4, step, 0, unroll=2)


def lanes(shape):
    return lax.broadcasted_iota(i32, shape, len(shape) - 1)


def fill_ends(padded, low, high):
    lane = lanes((1, LANES))
    before = pltpu.roll(padded[ROWS : ROWS + 8, :], PROBES, 1)[7:8, :]
    after = pltpu.roll(padded[8:16, :], LANES - PROBES, 1)[0:1, :]
    padded[7:8, :] = jnp.where(lane < PROBES, low, before)
    padded[ROWS + 8 : ROWS + 9, :] = jnp.where(lane >= LANES - PROBES, high, after)


def each_row_block(step):
    def outer(j, carry):
        for u in range(4):
            step(j * 32 + u * 8)
        return carry

    lax.fori_loop(0, ROWS // 32, outer, 0)


def table_kernel(probes, table, natural, sem):
    copies = [
        pltpu.make_async_copy(probes.at[p], natural.at[pl.ds(p, 1), :], sem.at[p]) for p in range(PROBES)
    ]
    for copy in copies:
        copy.start()
    finish(copies)

    def step(j, carry):
        for n in range(4):
            tile = j * 4 + n
            parts = [natural[:, aligned(g * ROWS + tile * LANES, LANES)] for g in range(GROUPS)]
            table[aligned(tile * LANES, LANES), :] = jnp.concatenate(parts, axis=0).T
        return carry

    lax.fori_loop(0, TILES // 4, step, 0)


def table_of(probes):
    return pl.pallas_call(
        table_kernel,
        out_shape=resident(ROWS, LANES),
        in_specs=[FIXED],
        out_specs=VMEM,
        scratch_shapes=[pltpu.VMEM((PROBES, GROUPS * ROWS), f32), pltpu.SemaphoreType.DMA((PROBES,))],
        compiler_params=params(60),
        cost_estimate=cost(3),
        name="table",
    )(probes)


BEFORE, SAME, AFTER = (0, 3), (1, 4), (2, 5)
SIDES = BEFORE + AFTER
NEAR, FAR = (0, 1, 2), (3, 4, 5)
EDGE = slice(FRINGE, FRINGE + LANES)


def weight_places(before, same, after):
    return {
        0: (before, 0, 0),
        3: (before, 4, 0),
        1: (same[0], 0, FRINGE),
        4: (same[1], 0, 4 * FRINGE),
        2: (after, 0, 0),
        5: (after, 4, 0),
    }


def pair_places(pair, ref):
    return {pair[0]: (ref, 0, 0), pair[1]: (ref, PROBES, 0)}


def grid_places(near, far):
    places = {k: (near, n * PROBES, 0) for n, k in enumerate(NEAR)}
    places.update({k: (far, n * PROBES, 0) for n, k in enumerate(FAR)})
    return places


def simple_call(kernel, out_shape, operands, name):
    return pl.pallas_call(
        kernel,
        out_shape=out_shape,
        in_specs=[VMEM] * len(operands),
        out_specs=[VMEM] * len(out_shape),
        compiler_params=params(8),
        cost_estimate=cost(1),
        name=name,
    )(*operands)


def weight_relay_kernel(near, far, table, up, down):
    for pair, out, rows in ((BEFORE, up, slice(ROWS - 8, ROWS)), (AFTER, down, slice(0, 8))):
        for n, ref in enumerate((near, far)):
            start = pair[n] * FRINGE
            out[n * 4 : n * 4 + 4, 0:FRINGE] = ref[:, start : start + FRINGE]
        out[:, EDGE] = table[rows, :]


def weight_relay(near, far, table):
    shape = jax.ShapeDtypeStruct((8, FRINGE + LANES), f32)
    return simple_call(weight_relay_kernel, [shape] * 2, (near, far, table), "weight_relay")


def rows_kernel(table, rows_hbm, staged, *rest):
    parts, sem = rest[:WAYS], rest[WAYS]
    gather_rows(table, parts, staged, index_copies(rows_hbm, segments(4, SIDES), parts, sem))


def rows_at_sides(table, rows):
    segs = segments(4, SIDES)
    return pl.pallas_call(
        rows_kernel,
        out_shape=resident(len(segs) * FRINGE, LANES),
        in_specs=[VMEM, HBM],
        out_specs=VMEM,
        scratch_shapes=index_scratch(segs),
        compiler_params=params(8),
        cost_estimate=cost(11),
        name="rows_at_sides",
    )(table, rows)


PAIR = jax.ShapeDtypeStruct((2 * PROBES, FRINGE), f32)
TRIPLE = jax.ShapeDtypeStruct((3 * PROBES, FRINGE), f32)


def side_sums_kernel(staged, cells, before, after, up, down):
    places = {**pair_places(AFTER, up), **pair_places(BEFORE, down)}
    select_fields(staged, cells, SIDES, weight_places(before, (None, None), after), places)


def side_sums(staged, cells, before, after):
    return simple_call(side_sums_kernel, [PAIR] * 2, (staged, cells, before, after), "side_sums")


def same_sums_kernel(table, cells, rows_hbm, near, far, out, staged, *rest):
    parts, sem = rest[:WAYS], rest[WAYS]
    gather_rows(table, parts, staged, index_copies(rows_hbm, segments(4, SAME), parts, sem))
    select_fields(staged, cells, SAME, weight_places(None, (near, far), None), pair_places(SAME, out))


def same_sums(table, cells, rows, near, far):
    segs = segments(4, SAME)
    return pl.pallas_call(
        same_sums_kernel,
        out_shape=PAIR,
        in_specs=[VMEM, VMEM, HBM, VMEM, VMEM],
        out_specs=VMEM,
        scratch_shapes=[pltpu.VMEM((len(segs) * FRINGE, LANES), f32)] + index_scratch(segs),
        compiler_params=params(8),
        cost_estimate=cost(8),
        name="same_sums",
    )(table, cells, rows, near, far)


def message_relay_kernel(before, same, after, near, far):
    for n, out in enumerate((near, far)):
        for i, ref in enumerate((before, same, after)):
            out[i * PROBES : (i + 1) * PROBES, :] = ref[n * PROBES : (n + 1) * PROBES, :]


def message_relay(before, same, after):
    return simple_call(message_relay_kernel, [TRIPLE] * 2, (before, same, after), "message_relay")


def end_flags():
    column = lax.axis_index("cell")
    return (column > 0).astype(f32), (column < lax.axis_size("cell") - 1).astype(f32)


def outer_rows(before, after):
    has_low, has_high = end_flags()
    low = pltpu.roll(before[0:8, EDGE], PROBES, 1)[7:8, :] * has_low
    high = pltpu.roll(after[0:8, EDGE], LANES - PROBES, 1)[0:1, :] * has_high
    return low, high


def forward_kernel(table, centre, lower, upper, before, after, c_out, l_out, u_out, *rest):
    sums, padded = rest[:SUMS], rest[SUMS]

    def step(j, carry):
        for n in range(2):
            tile = j * 2 + n
            at = aligned(tile * LANES, LANES)
            padded[rows_of(tile * LANES + 8, LANES), :] = table[at, :]
            for ref, out in ((centre, c_out), (lower, l_out), (upper, u_out)):
                parts = [
                    jnp.broadcast_to(ref[:, aligned(g * ROWS + tile * LANES, LANES)], (PROBES, LANES))
                    for g in range(GROUPS)
                ]
                out[at, :] = jnp.concatenate(parts, axis=0).T
        return carry

    lax.fori_loop(0, TILES // 2, step, 0)
    fill_ends(padded, *outer_rows(before, after))

    def stencil(start):
        at = rows_of(start, 8)
        sums[0][at, :] = (
            c_out[at, :] * padded[rows_of(start + 8, 8), :]
            - l_out[at, :] * padded[pl.ds(start + 7, 8), :]
            - u_out[at, :] * padded[pl.ds(start + 9, 8), :]
        )

    each_row_block(stencil)
    clear(sums[1:])


def forward(table, centre, lower, upper, before, after):
    return pl.pallas_call(
        forward_kernel,
        out_shape=[resident(ROWS, LANES)] * (3 + SUMS),
        in_specs=[VMEM] * 6,
        out_specs=[VMEM] * (3 + SUMS),
        scratch_shapes=[pltpu.VMEM((ROWS + 16, LANES), f32)],
        compiler_params=params(8),
        cost_estimate=cost(7),
        name="forward",
    )(table, centre, lower, upper, before, after)


def couple_kernel(cells, rows_hbm, near, far, *refs):
    refs = refs[SUMS:]
    tangent, out, sums = refs[0], refs[1], refs[2 : 2 + SUMS]
    staged, staged_far = refs[2 + SUMS : 4 + SUMS]
    refs = refs[4 + SUMS :]
    parts, sem, parts_far, sem_far = refs[:WAYS], refs[WAYS], refs[WAYS + 1 : 2 * WAYS + 1], refs[2 * WAYS + 1]
    every = NEAR + FAR
    phases = index_copies(rows_hbm, segments(1, every), parts, sem)
    phases_far = index_copies(rows_hbm, segments(1, FAR), parts_far, sem_far)
    spread_at_receptors(grid_places(near, far), cells, staged)
    finish(phases[0] + phases[1])
    add_rows(sums, parts, staged)

    def total(start):
        at = rows_of(start, 8)
        value = sums[0][at, :]
        for part in sums[1:]:
            value = value + part[at, :]
        tangent[at, :] = value

    each_row_block(total)
    gather_rows(tangent, parts_far, staged_far, phases_far)
    select_fields(staged_far, cells, FAR, None, grid_places(None, out))


def couple(cells, rows, near, far, sums):
    every, some = segments(1, NEAR + FAR), segments(1, FAR)
    outs = pl.pallas_call(
        couple_kernel,
        out_shape=[resident(ROWS, LANES), TRIPLE] + [resident(ROWS, LANES)] * SUMS,
        in_specs=[VMEM, HBM] + [VMEM] * (2 + SUMS),
        out_specs=[VMEM] * (2 + SUMS),
        scratch_shapes=[pltpu.VMEM((SLOTS, LANES), f32), pltpu.VMEM((SLOTS // 2, LANES), f32)]
        + index_scratch(every)
        + index_scratch(some),
        input_output_aliases={4 + w: 2 + w for w in range(SUMS)},
        compiler_params=params(8),
        cost_estimate=cost(11),
        name="couple",
    )(cells, rows, near, far, *sums)
    return outs[0], outs[1]


def receptor_kernel(tangent, cells, rows_hbm, out, staged, *rest):
    parts, sem = rest[:WAYS], rest[WAYS]
    gather_rows(tangent, parts, staged, index_copies(rows_hbm, segments(1, NEAR), parts, sem))
    select_fields(staged, cells, NEAR, None, grid_places(out, None))


def at_receptors(tangent, cells, rows):
    segs = segments(1, NEAR)
    return pl.pallas_call(
        receptor_kernel,
        out_shape=TRIPLE,
        in_specs=[VMEM, VMEM, HBM],
        out_specs=VMEM,
        scratch_shapes=[pltpu.VMEM((len(segs) * FRINGE, LANES), f32)] + index_scratch(segs),
        compiler_params=params(8),
        cost_estimate=cost(3),
        name="at_receptors",
    )(tangent, cells, rows)


def return_relay_kernel(near, far, tangent, lower, upper, ready, up, down):
    for n, ref in enumerate((near, far)):
        at = slice(n * PROBES, (n + 1) * PROBES)
        up[at, 0:FRINGE] = ref[0:PROBES, :]
        down[at, 0:FRINGE] = ref[2 * PROBES : 3 * PROBES, :]
    end = slice(ROWS - 8, ROWS)
    up[0:8, EDGE] = upper[end, :] * tangent[end, :]
    down[0:8, EDGE] = lower[0:8, :] * tangent[0:8, :]


def return_relay(near, far, tangent, lower, upper, ready):
    shape = jax.ShapeDtypeStruct((2 * PROBES, FRINGE + LANES), f32)
    return simple_call(return_relay_kernel, [shape] * 2, (near, far, tangent, lower, upper, ready), "return_relay")


def transposed_kernel(tangent, centre, lower, upper, ready, *rest):
    sums, raised, lowered = rest[:SUMS], rest[SUMS], rest[SUMS + 1]

    def products(start):
        at = rows_of(start, 8)
        value = tangent[at, :]
        raised[rows_of(start + 8, 8), :] = upper[at, :] * value
        lowered[rows_of(start + 8, 8), :] = lower[at, :] * value

    each_row_block(products)
    nothing = jnp.zeros((1, LANES), f32)
    fill_ends(raised, nothing, nothing)
    fill_ends(lowered, nothing, nothing)

    def stencil(start):
        at = rows_of(start, 8)
        sums[0][at, :] = (
            centre[at, :] * tangent[at, :] - raised[pl.ds(start + 7, 8), :] - lowered[pl.ds(start + 9, 8), :]
        )

    each_row_block(stencil)
    clear(sums[1:])


def transposed(tangent, centre, lower, upper, ready):
    return pl.pallas_call(
        transposed_kernel,
        out_shape=[resident(ROWS, LANES)] * SUMS,
        in_specs=[VMEM] * 5,
        out_specs=[VMEM] * SUMS,
        scratch_shapes=[pltpu.VMEM((ROWS + 16, LANES), f32)] * 2,
        compiler_params=params(8),
        cost_estimate=cost(1),
        name="transposed",
    )(tangent, centre, lower, upper, ready)


def donor_same_kernel(cells, rows_hbm, near_weights, far_weights, near, far, *refs):
    refs = refs[SUMS:]
    sums, staged, parts, sem = refs[:SUMS], refs[SUMS], refs[SUMS + 1 : SUMS + WAYS + 1], refs[SUMS + WAYS + 1]
    phases = index_copies(rows_hbm, segments(4, SAME), parts, sem)
    weights = weight_places(None, (near_weights, far_weights), None)
    spread_at_donors(grid_places(near, far), cells, SAME, weights, staged)
    finish(phases[0] + phases[1])
    add_rows(sums, parts, staged)


def add_same(cells, rows, near_weights, far_weights, near, far, sums):
    segs = segments(4, SAME)
    return pl.pallas_call(
        donor_same_kernel,
        out_shape=[resident(ROWS, LANES)] * SUMS,
        in_specs=[VMEM, HBM] + [VMEM] * (4 + SUMS),
        out_specs=[VMEM] * SUMS,
        scratch_shapes=[pltpu.VMEM((len(segs) * FRINGE, LANES), f32)] + index_scratch(segs),
        input_output_aliases={6 + w: w for w in range(SUMS)},
        compiler_params=params(8),
        cost_estimate=cost(9),
        name="add_same",
    )(cells, rows, near_weights, far_weights, near, far, *sums)


def sum_of_groups(value):
    for shift in (64, 32, 16):
        value = value + pltpu.roll(value, shift, 1)
    return value


def own_group():
    return lanes((8, LANES)) // PROBES == lax.broadcasted_iota(i32, (8, LANES), 0)


def donor_sides_kernel(cells, rows_hbm, before_weights, after_weights, before, after, *refs):
    refs = refs[SUMS:]
    adjoint, gram, sums, staged = refs[0], refs[1], refs[2 : 2 + SUMS], refs[2 + SUMS]
    parts, sem = refs[3 + SUMS : 3 + SUMS + WAYS], refs[3 + SUMS + WAYS]
    phases = index_copies(rows_hbm, segments(4, SIDES), parts, sem)
    weights = weight_places(before_weights, (None, None), after_weights)
    spread_at_donors({**pair_places(BEFORE, before), **pair_places(AFTER, after)}, cells, SIDES, weights, staged)
    finish(phases[0] + phases[1])
    add_rows(sums, parts, staged)
    lane = lanes((1, LANES))
    low, high = outer_rows(before, after)
    sums[0][0:1, :] = sums[0][0:1, :] - jnp.where(lane < PROBES, low, 0.0)
    end = sums[0][ROWS - 1 : ROWS, :]
    sums[0][ROWS - 1 : ROWS, :] = end - jnp.where(lane >= LANES - PROBES, high, 0.0)

    def total(start):
        at = rows_of(start, 8)
        value = sums[0][at, :]
        for part in sums[1:]:
            value = value + part[at, :]
        adjoint[at, :] = value

    each_row_block(total)

    def multiply(j, product):
        left_side, right_side = [], []
        for n in range(4):
            block = adjoint[aligned((j * 4 + n) * LANES, LANES), :]
            high, low = split(block)
            high_t, low_t = split(block.T)
            left_side += [high_t, high_t, low_t]
            right_side += [high, low, high]
        left_side = jnp.concatenate(left_side, axis=1)
        right_side = jnp.concatenate(right_side, axis=0)
        return product + jnp.dot(left_side, right_side, preferred_element_type=f32)

    product = lax.fori_loop(0, TILES // 4, multiply, jnp.zeros((LANES, LANES), f32))
    group = lanes((PROBES, LANES)) // PROBES
    folded = jnp.zeros((PROBES, LANES), f32)
    for g in range(GROUPS):
        folded = folded + jnp.where(group == g, product[g * PROBES : (g + 1) * PROBES, :], 0.0)
    folded = sum_of_groups(folded)
    for n in range(2):
        gram[n : n + 1, :] = jnp.sum(jnp.where(own_group(), folded[n * 8 : n * 8 + 8, :], 0.0), axis=0, keepdims=True)


def add_sides(cells, rows, before_weights, after_weights, before, after, sums):
    segs = segments(4, SIDES)
    outs = pl.pallas_call(
        donor_sides_kernel,
        out_shape=[resident(ROWS, LANES), jax.ShapeDtypeStruct((2, LANES), f32)]
        + [resident(ROWS, LANES)] * SUMS,
        in_specs=[VMEM, HBM] + [VMEM] * (4 + SUMS),
        out_specs=[VMEM] * (2 + SUMS),
        scratch_shapes=[pltpu.VMEM((len(segs) * FRINGE, LANES), f32)] + index_scratch(segs),
        input_output_aliases={6 + w: 2 + w for w in range(SUMS)},
        compiler_params=params(12),
        cost_estimate=cost(18),
        name="add_sides",
    )(cells, rows, before_weights, after_weights, before, after, *sums)
    return outs[0], outs[1]


def basis_kernel(total_cells, gram, adjoint, basis, factor, natural, sem):
    row = lax.broadcasted_iota(i32, (PROBES, LANES), 0)
    lane = lanes((PROBES, LANES))
    whole = jnp.concatenate(
        [sum_of_groups(jnp.where(own_group(), jnp.broadcast_to(gram[n : n + 1, :], (8, LANES)), 0.0)) for n in range(2)],
        axis=0,
    ) / f32(total_cells)
    columns = [jnp.broadcast_to(whole[:, j : j + 1], (PROBES, LANES)) for j in range(PROBES)]
    right = jnp.where(row == lane % PROBES, 1.0, 0.0)
    result = jnp.zeros((PROBES, LANES), f32)
    for j in range(PROBES):
        pivot = columns[j][j : j + 1, :]
        root = jnp.sqrt(pivot)
        ratio = jnp.where(row > j, columns[j] / pivot, 0.0)
        result = jnp.where((lane == j) & (row >= j), columns[j] / root, result)
        right_row = right[j : j + 1, :]
        right = jnp.where(row == j, right_row / root, right - ratio * right_row)
        for n in range(j + 1, PROBES):
            columns[n] = columns[n] - ratio * columns[n][j : j + 1, :]
    factor[...] = result[:, :PROBES]
    inverse = jnp.concatenate([right] * GROUPS, axis=0)
    same = lax.broadcasted_iota(i32, (LANES, LANES), 0) // PROBES == lanes((LANES, LANES)) // PROBES
    high, low = split(jnp.where(same, inverse, 0.0))
    left_side = jnp.concatenate([high, high, low], axis=1)

    def step(j, carry):
        for n in range(4):
            tile = j * 4 + n
            high, low = split(adjoint[aligned(tile * LANES, LANES), :])
            right_side = jnp.concatenate([high, low, high], axis=1)
            block = lax.dot_general(left_side, right_side, (((1,), (1,)), ((), ())), preferred_element_type=f32)
            for g in range(GROUPS):
                natural[:, aligned(g * ROWS + tile * LANES, LANES)] = block[g * PROBES : (g + 1) * PROBES, :]
        return carry

    copies = []
    for quarter in range(4):
        lax.fori_loop(quarter * TILES // 16, (quarter + 1) * TILES // 16, step, 0)
        for g in range(GROUPS):
            at = pl.ds(g * ROWS + quarter * ROWS // 4, ROWS // 4)
            copies.append(pltpu.make_async_copy(natural.at[:, at], basis.at[:, 0, at], sem.at[len(copies)]))
            copies[-1].start()
    finish(copies)


def basis_of(total_cells, gram, adjoint):
    return pl.pallas_call(
        functools.partial(basis_kernel, total_cells),
        out_shape=[
            jax.ShapeDtypeStruct((PROBES, 1, GROUPS * ROWS), f32),
            jax.ShapeDtypeStruct((PROBES, PROBES), f32),
        ],
        in_specs=[VMEM] * 2,
        out_specs=[FIXED, VMEM],
        scratch_shapes=[pltpu.VMEM((PROBES, GROUPS * ROWS), f32), pltpu.SemaphoreType.DMA((4 * GROUPS,))],
        compiler_params=params(8),
        cost_estimate=cost(6),
        name="basis",
    )(gram, adjoint)


def moved(value, place):
    grids, columns = (lax.axis_size(axis) for axis in AXES)
    route = []
    for g in range(grids):
        for c in range(columns):
            to_g, to_c = place(g, c)
            route.append((g * columns + c, (to_g % grids) * columns + to_c % columns))
    return lax.ppermute(value, AXES, route)


def along_grid(value, distance):
    return moved(value, lambda g, c: (g + distance, c))


def along_cell(value, distance):
    return moved(value, lambda g, c: (g, c + distance))


def axis_sum(value, axis):
    copies = jnp.broadcast_to(value, (lax.axis_size(axis),) + value.shape)
    return jnp.sum(lax.all_to_all(copies, axis, 0, 0), axis=0)


def body(probes, centre, lower_coef, upper_coef, donor_cells, receptor_cells, weights):
    donors = donor_cells[0]
    donor_rows = (donors & (ROWS - 1)).reshape(-1)
    receptor_rows = (receptor_cells & (ROWS - 1)).reshape(-1)
    near_weights, far_weights = along_grid(weights, -1)[0], along_grid(weights, -2)[0]
    table = table_of(probes)
    up, down = weight_relay(near_weights, far_weights, table)
    before_weights, after_weights = along_cell(up, 1), along_cell(down, -1)
    staged = rows_at_sides(table, donor_rows)
    up, down = side_sums(staged, donors, before_weights, after_weights)
    after, before = along_cell(up, 1), along_cell(down, -1)
    same = same_sums(table, donors, donor_rows, near_weights, far_weights)
    near, far = message_relay(before, same, after)
    near, far = along_grid(near, 1), along_grid(far, 2)
    c, l, u, *sums = forward(table, centre, lower_coef, upper_coef, before_weights, after_weights)
    tangent, far = couple(receptor_cells, receptor_rows, near, far, sums)
    far = along_grid(far, -2)
    near = along_grid(at_receptors(tangent, receptor_cells, receptor_rows), -1)
    sums = transposed(tangent, c, l, u, far)
    up, down = return_relay(near, far, tangent, l, u, sums[-1])
    before, after = along_cell(up, 1), along_cell(down, -1)
    sums = add_same(donors, donor_rows, near_weights, far_weights, near, far, sums)
    adjoint, gram = add_sides(donors, donor_rows, before_weights, after_weights, before, after, sums)
    total_cells = lax.axis_size("grid") * lax.axis_size("cell") * probes.shape[2]
    basis, factor = basis_of(total_cells, axis_sum(axis_sum(gram, "grid"), "cell"), adjoint)
    return (basis, factor)


def solution(mesh):
    in_specs = (
        P(None, "grid", "cell"),
        P("grid", "cell"),
        P("grid", "cell"),
        P("grid", "cell"),
        P("grid", None, "cell"),
        P("grid", "cell"),
        P("grid", None, "cell"),
    )
    out_specs = (P(None, "grid", "cell"), P())
    return jax.shard_map(body, mesh=mesh, in_specs=in_specs, out_specs=out_specs, check_vma=False)
```

```python
import functools

import jax
import jax.numpy as jnp
from jax import lax
from jax.experimental import pallas as pl
from jax.experimental.pallas import tpu as pltpu
from jax.sharding import PartitionSpec as P

f32 = jnp.float32
i32 = jnp.int32
bf16 = jnp.bfloat16

PROBES = 16
GROUPS = 8
ROWS = 4096
LANES = 128
PARTNERS = 6
FRINGE = 1024
HALF = 3 * FRINGE
SLOTS = PARTNERS * FRINGE
TILES = ROWS // LANES
WAYS = 8
SUMS = 4
QUARTER = SLOTS // 4
UNROLL = 8

AXES = ("grid", "cell")

VMEM = pl.BlockSpec(memory_space=pltpu.VMEM)
HBM = pl.BlockSpec(memory_space=pl.ANY)
FIXED = pl.BlockSpec(memory_space=pltpu.HBM)


def aligned(start, size):
    return pl.ds(pl.multiple_of(start, size), size)


def rows_of(start, size):
    return pl.ds(pl.multiple_of(start, 8), size)


def split(x):
    high = x.astype(bf16)
    return high, (x - high.astype(f32)).astype(bf16)


def params(limit_mib):
    return pltpu.CompilerParams(vmem_limit_bytes=limit_mib << 20)


def cost(microseconds):
    return pl.CostEstimate(flops=0, transcendentals=0, bytes_accessed=microseconds * 3_000_000)


def resident(*shape):
    return pltpu.VMEM(shape, f32)


HEAD = 128


def segments(many, partners):
    return [(m, k) for m in range(many) for k in partners]


def index_scratch(segs):
    size = len(segs) * FRINGE // WAYS
    return [pltpu.SMEM((size,), i32)] * WAYS + [pltpu.SemaphoreType.DMA((3 * WAYS,))]


def index_copies(rows_hbm, segs, parts, sem):
    size = parts[0].shape[0]
    cuts = sorted({0, HEAD, size} | set(range(0, size, FRINGE)))
    phases = [[], []]
    for c in range(len(cuts) - 1):
        low, high = cuts[c], cuts[c + 1]
        for w in range(WAYS):
            seg, offset = divmod(w * size + low, FRINGE)
            start = segs[seg][0] * SLOTS + segs[seg][1] * FRINGE + offset
            copy = pltpu.make_async_copy(
                rows_hbm.at[pl.ds(start, high - low)], parts[w].at[pl.ds(low, high - low)], sem.at[c * WAYS + w]
            )
            copy.start()
            phases[min(c, 1)].append(copy)
    return phases


def finish(copies):
    for copy in copies:
        copy.wait()


def row_steps(parts, low, high, step):
    def outer(j, carry):
        for n in range(UNROLL):
            q = low + j * UNROLL + n
            for w in range(WAYS):
                step(w, q, parts[w][q])
        return carry

    lax.fori_loop(0, (high - low) // UNROLL, outer, 0)


def gather_rows(table, parts, staged, phases):
    count = parts[0].shape[0]

    def step(w, q, row):
        staged[pl.ds(w * count + q, 1), :] = table[pl.ds(row, 1), :]

    finish(phases[0])
    row_steps(parts, 0, HEAD, step)
    finish(phases[1])
    row_steps(parts, HEAD, count, step)


def clear(sums):
    def step(j, carry):
        for total in sums:
            for n in range(4):
                total[rows_of(j * 32 + n * 8, 8), :] = jnp.zeros((8, LANES), f32)
        return carry

    lax.fori_loop(0, ROWS // 32, step, 0)


def add_rows(sums, parts, staged):
    count = parts[0].shape[0]

    def outer(j, carry):
        for n in range(UNROLL):
            q = j * UNROLL + n
            for half in range(2):
                total = sums[half + n % 2 * 2]
                lists = [2 * m + half for m in range(4)]
                rows = [parts[w][q] for w in lists]
                old = [total[pl.ds(row, 1), :] for row in rows]
                new = [value + staged[pl.ds(w * count + q, 1), :] for value, w in zip(old, lists)]
                for row, value in zip(rows, new):
                    total[pl.ds(row, 1), :] = value
        return carry

    lax.fori_loop(0, count // UNROLL, outer, 0)


def groups_of(cells, m, offset):
    return jnp.broadcast_to(cells[m : m + 1, aligned(offset, LANES)], (8, LANES)) >> 12


def identity_pair():
    row = lax.broadcasted_iota(i32, (LANES, 2 * LANES), 0)
    return jnp.where(lanes((LANES, 2 * LANES)) % LANES == row, 1.0, 0.0).astype(bf16)


def turned(block, m, pair):
    if m % 2 == 0:
        return block.T
    both = jnp.concatenate(split(block), axis=1)
    return lax.dot_general(pair, both, (((1,), (1,)), ((), ())), preferred_element_type=f32)


def each_block(many, step):
    unroll = 8 // many

    def outer(j, carry):
        for n in range(unroll):
            step(j * unroll + n, n)
        return carry

    lax.fori_loop(0, FRINGE // LANES // unroll, outer, 0)


def select_fields(staged, cells, partners, weights, out):
    many = cells.shape[0]
    pair = identity_pair()
    for n, k in enumerate(partners):

        def step(b, mark=0):
            total = [jnp.zeros((8, LANES), f32)] * 2
            for m in range(many):
                field = staged[aligned((m * len(partners) + n) * FRINGE + b * LANES, LANES), :]
                field = turned(field, m if many > 1 else mark, pair)
                group = groups_of(cells, m, k * FRINGE + b * LANES)
                scale = 1.0
                if weights is not None:
                    ref, row, column = weights[k]
                    scale = ref[row + m : row + m + 1, aligned(column + b * LANES, LANES)]
                    scale = jnp.broadcast_to(scale, (8, LANES))
                for g in range(GROUPS):
                    factor = jnp.where(group == g, scale, 0.0)
                    for h in range(2):
                        at = g * PROBES + h * 8
                        total[h] = total[h] + field[at : at + 8, :] * factor
            ref, row, column = out[k]
            for h in range(2):
                ref[row + h * 8 : row + h * 8 + 8, aligned(column + b * LANES, LANES)] = total[h]

        each_block(many, step)


def spread_group(fields, cells, outs, pair):
    group = [value >> 12 for value in cells]
    row = [value & (ROWS - 1) for value in cells]
    terms = [[jnp.where(group[m] == g, fields[m][h], 0.0) for g in range(GROUPS) for h in range(2)] for m in range(4)]
    for m in range(4):
        same = [row[m] == row[i] for i in range(m)]
        block = []
        for v in range(2 * GROUPS):
            value = terms[m][v]
            for i in range(m):
                value = value + jnp.where(same[i], terms[i][v], 0.0)
            block.append(value)
        ref, at = outs[m]
        ref[aligned(at, LANES), :] = turned(jnp.concatenate(block, axis=0), m, pair)


def block_of(ref, row, column):
    return jnp.broadcast_to(ref[row : row + 1, aligned(column, LANES)], (8, LANES))


def field_of(place, b):
    ref, row, column = place
    return [ref[row + h * 8 : row + h * 8 + 8, aligned(column + b * LANES, LANES)] for h in range(2)]


def spread_at_donors(messages, cells, partners, weights, staged):
    pair = identity_pair()
    for n, k in enumerate(partners):

        def step(b, mark=0):
            field = field_of(messages[k], b)
            ref, row, column = weights[k]
            scale = [block_of(ref, row + m, column + b * LANES) for m in range(4)]
            fields = [[part * scale[m] for part in field] for m in range(4)]
            blocks = [block_of(cells, m, k * FRINGE + b * LANES) for m in range(4)]
            outs = [(staged, (m * len(partners) + n) * FRINGE + b * LANES) for m in range(4)]
            spread_group(fields, blocks, outs, pair)

        each_block(4, step)


def spread_at_receptors(messages, cells, staged):
    pair = identity_pair()
    for part in range(3):

        def step(j, carry):
            fields, blocks, outs = [], [], []
            for m in range(4):
                k, shift = divmod(m * QUARTER + part * 4 * LANES, FRINGE)
                fields.append(field_of(messages[k], j + shift // LANES))
                at = m * QUARTER + (part * 4 + j) * LANES
                blocks.append(block_of(cells, 0, at))
                outs.append((staged, at))
            spread_group(fields, blocks, outs, pair)
            return carry

        lax.fori_loop(0, 4, step, 0, unroll=2)


def lanes(shape):
    return lax.broadcasted_iota(i32, shape, len(shape) - 1)


def fill_ends(padded, low, high):
    lane = lanes((1, LANES))
    before = pltpu.roll(padded[ROWS : ROWS + 8, :], PROBES, 1)[7:8, :]
    after = pltpu.roll(padded[8:16, :], LANES - PROBES, 1)[0:1, :]
    padded[7:8, :] = jnp.where(lane < PROBES, low, before)
    padded[ROWS + 8 : ROWS + 9, :] = jnp.where(lane >= LANES - PROBES, high, after)


def each_row_block(step):
    def outer(j, carry):
        for u in range(4):
            step(j * 32 + u * 8)
        return carry

    lax.fori_loop(0, ROWS // 32, outer, 0)


def table_kernel(probes, table, natural, sem):
    copies = [
        pltpu.make_async_copy(probes.at[p], natural.at[pl.ds(p, 1), :], sem.at[p]) for p in range(PROBES)
    ]
    for copy in copies:
        copy.start()
    finish(copies)

    def step(j, carry):
        for n in range(4):
            tile = j * 4 + n
            parts = [natural[:, aligned(g * ROWS + tile * LANES, LANES)] for g in range(GROUPS)]
            table[aligned(tile * LANES, LANES), :] = jnp.concatenate(parts, axis=0).T
        return carry

    lax.fori_loop(0, TILES // 4, step, 0)


def table_of(probes):
    return pl.pallas_call(
        table_kernel,
        out_shape=resident(ROWS, LANES),
        in_specs=[FIXED],
        out_specs=VMEM,
        scratch_shapes=[pltpu.VMEM((PROBES, GROUPS * ROWS), f32), pltpu.SemaphoreType.DMA((PROBES,))],
        compiler_params=params(60),
        cost_estimate=cost(3),
        name="table",
    )(probes)


BEFORE, SAME, AFTER = (0, 3), (1, 4), (2, 5)
SIDES = BEFORE + AFTER
NEAR, FAR = (0, 1, 2), (3, 4, 5)
EDGE = slice(FRINGE, FRINGE + LANES)


def weight_places(before, same, after):
    return {
        0: (before, 0, 0),
        3: (before, 4, 0),
        1: (same[0], 0, FRINGE),
        4: (same[1], 0, 4 * FRINGE),
        2: (after, 0, 0),
        5: (after, 4, 0),
    }


def pair_places(pair, ref):
    return {pair[0]: (ref, 0, 0), pair[1]: (ref, PROBES, 0)}


def grid_places(near, far):
    places = {k: (near, n * PROBES, 0) for n, k in enumerate(NEAR)}
    places.update({k: (far, n * PROBES, 0) for n, k in enumerate(FAR)})
    return places


def simple_call(kernel, out_shape, operands, name):
    return pl.pallas_call(
        kernel,
        out_shape=out_shape,
        in_specs=[VMEM] * len(operands),
        out_specs=[VMEM] * len(out_shape),
        compiler_params=params(8),
        cost_estimate=cost(1),
        name=name,
    )(*operands)


def weight_relay_kernel(near, far, table, up, down):
    for pair, out, rows in ((BEFORE, up, slice(ROWS - 8, ROWS)), (AFTER, down, slice(0, 8))):
        for n, ref in enumerate((near, far)):
            start = pair[n] * FRINGE
            out[n * 4 : n * 4 + 4, 0:FRINGE] = ref[:, start : start + FRINGE]
        out[:, EDGE] = table[rows, :]


def weight_relay(near, far, table):
    shape = jax.ShapeDtypeStruct((8, FRINGE + LANES), f32)
    return simple_call(weight_relay_kernel, [shape] * 2, (near, far, table), "weight_relay")


def rows_kernel(table, rows_hbm, staged, *rest):
    parts, sem = rest[:WAYS], rest[WAYS]
    gather_rows(table, parts, staged, index_copies(rows_hbm, segments(4, SIDES), parts, sem))


def rows_at_sides(table, rows):
    segs = segments(4, SIDES)
    return pl.pallas_call(
        rows_kernel,
        out_shape=resident(len(segs) * FRINGE, LANES),
        in_specs=[VMEM, HBM],
        out_specs=VMEM,
        scratch_shapes=index_scratch(segs),
        compiler_params=params(8),
        cost_estimate=cost(11),
        name="rows_at_sides",
    )(table, rows)


PAIR = jax.ShapeDtypeStruct((2 * PROBES, FRINGE), f32)
TRIPLE = jax.ShapeDtypeStruct((3 * PROBES, FRINGE), f32)


def side_sums_kernel(staged, cells, before, after, up, down):
    places = {**pair_places(AFTER, up), **pair_places(BEFORE, down)}
    select_fields(staged, cells, SIDES, weight_places(before, (None, None), after), places)


def side_sums(staged, cells, before, after):
    return simple_call(side_sums_kernel, [PAIR] * 2, (staged, cells, before, after), "side_sums")


def same_sums_kernel(table, cells, rows_hbm, near, far, out, staged, *rest):
    parts, sem = rest[:WAYS], rest[WAYS]
    gather_rows(table, parts, staged, index_copies(rows_hbm, segments(4, SAME), parts, sem))
    select_fields(staged, cells, SAME, weight_places(None, (near, far), None), pair_places(SAME, out))


def same_sums(table, cells, rows, near, far):
    segs = segments(4, SAME)
    return pl.pallas_call(
        same_sums_kernel,
        out_shape=PAIR,
        in_specs=[VMEM, VMEM, HBM, VMEM, VMEM],
        out_specs=VMEM,
        scratch_shapes=[pltpu.VMEM((len(segs) * FRINGE, LANES), f32)] + index_scratch(segs),
        compiler_params=params(8),
        cost_estimate=cost(8),
        name="same_sums",
    )(table, cells, rows, near, far)


def message_relay_kernel(before, same, after, near, far):
    for n, out in enumerate((near, far)):
        for i, ref in enumerate((before, same, after)):
            out[i * PROBES : (i + 1) * PROBES, :] = ref[n * PROBES : (n + 1) * PROBES, :]


def message_relay(before, same, after):
    return simple_call(message_relay_kernel, [TRIPLE] * 2, (before, same, after), "message_relay")


def end_flags():
    column = lax.axis_index("cell")
    return (column > 0).astype(f32), (column < lax.axis_size("cell") - 1).astype(f32)


def outer_rows(before, after):
    has_low, has_high = end_flags()
    low = pltpu.roll(before[0:8, EDGE], PROBES, 1)[7:8, :] * has_low
    high = pltpu.roll(after[0:8, EDGE], LANES - PROBES, 1)[0:1, :] * has_high
    return low, high


def forward_kernel(table, centre, lower, upper, before, after, c_out, l_out, u_out, *rest):
    sums, padded = rest[:SUMS], rest[SUMS]

    def step(j, carry):
        for n in range(2):
            tile = j * 2 + n
            at = aligned(tile * LANES, LANES)
            padded[rows_of(tile * LANES + 8, LANES), :] = table[at, :]
            for ref, out in ((centre, c_out), (lower, l_out), (upper, u_out)):
                parts = [
                    jnp.broadcast_to(ref[:, aligned(g * ROWS + tile * LANES, LANES)], (PROBES, LANES))
                    for g in range(GROUPS)
                ]
                out[at, :] = jnp.concatenate(parts, axis=0).T
        return carry

    lax.fori_loop(0, TILES // 2, step, 0)
    fill_ends(padded, *outer_rows(before, after))

    def stencil(start):
        at = rows_of(start, 8)
        sums[0][at, :] = (
            c_out[at, :] * padded[rows_of(start + 8, 8), :]
            - l_out[at, :] * padded[pl.ds(start + 7, 8), :]
            - u_out[at, :] * padded[pl.ds(start + 9, 8), :]
        )

    each_row_block(stencil)
    clear(sums[1:])


def forward(table, centre, lower, upper, before, after):
    return pl.pallas_call(
        forward_kernel,
        out_shape=[resident(ROWS, LANES)] * (3 + SUMS),
        in_specs=[VMEM] * 6,
        out_specs=[VMEM] * (3 + SUMS),
        scratch_shapes=[pltpu.VMEM((ROWS + 16, LANES), f32)],
        compiler_params=params(8),
        cost_estimate=cost(7),
        name="forward",
    )(table, centre, lower, upper, before, after)


def couple_kernel(cells, rows_hbm, near, far, *refs):
    refs = refs[SUMS:]
    tangent, out, sums = refs[0], refs[1], refs[2 : 2 + SUMS]
    staged, staged_far = refs[2 + SUMS : 4 + SUMS]
    refs = refs[4 + SUMS :]
    parts, sem, parts_far, sem_far = refs[:WAYS], refs[WAYS], refs[WAYS + 1 : 2 * WAYS + 1], refs[2 * WAYS + 1]
    every = NEAR + FAR
    phases = index_copies(rows_hbm, segments(1, every), parts, sem)
    phases_far = index_copies(rows_hbm, segments(1, FAR), parts_far, sem_far)
    spread_at_receptors(grid_places(near, far), cells, staged)
    finish(phases[0] + phases[1])
    add_rows(sums, parts, staged)

    def total(start):
        at = rows_of(start, 8)
        value = sums[0][at, :]
        for part in sums[1:]:
            value = value + part[at, :]
        tangent[at, :] = value

    each_row_block(total)
    gather_rows(tangent, parts_far, staged_far, phases_far)
    select_fields(staged_far, cells, FAR, None, grid_places(None, out))


def couple(cells, rows, near, far, sums):
    every, some = segments(1, NEAR + FAR), segments(1, FAR)
    outs = pl.pallas_call(
        couple_kernel,
        out_shape=[resident(ROWS, LANES), TRIPLE] + [resident(ROWS, LANES)] * SUMS,
        in_specs=[VMEM, HBM] + [VMEM] * (2 + SUMS),
        out_specs=[VMEM] * (2 + SUMS),
        scratch_shapes=[pltpu.VMEM((SLOTS, LANES), f32), pltpu.VMEM((SLOTS // 2, LANES), f32)]
        + index_scratch(every)
        + index_scratch(some),
        input_output_aliases={4 + w: 2 + w for w in range(SUMS)},
        compiler_params=params(8),
        cost_estimate=cost(11),
        name="couple",
    )(cells, rows, near, far, *sums)
    return outs[0], outs[1]


def receptor_kernel(tangent, cells, rows_hbm, out, staged, *rest):
    parts, sem = rest[:WAYS], rest[WAYS]
    gather_rows(tangent, parts, staged, index_copies(rows_hbm, segments(1, NEAR), parts, sem))
    select_fields(staged, cells, NEAR, None, grid_places(out, None))


def at_receptors(tangent, cells, rows):
    segs = segments(1, NEAR)
    return pl.pallas_call(
        receptor_kernel,
        out_shape=TRIPLE,
        in_specs=[VMEM, VMEM, HBM],
        out_specs=VMEM,
        scratch_shapes=[pltpu.VMEM((len(segs) * FRINGE, LANES), f32)] + index_scratch(segs),
        compiler_params=params(8),
        cost_estimate=cost(3),
        name="at_receptors",
    )(tangent, cells, rows)


def return_relay_kernel(near, far, tangent, lower, upper, ready, up, down):
    for n, ref in enumerate((near, far)):
        at = slice(n * PROBES, (n + 1) * PROBES)
        up[at, 0:FRINGE] = ref[0:PROBES, :]
        down[at, 0:FRINGE] = ref[2 * PROBES : 3 * PROBES, :]
    end = slice(ROWS - 8, ROWS)
    up[0:8, EDGE] = upper[end, :] * tangent[end, :]
    down[0:8, EDGE] = lower[0:8, :] * tangent[0:8, :]


def return_relay(near, far, tangent, lower, upper, ready):
    shape = jax.ShapeDtypeStruct((2 * PROBES, FRINGE + LANES), f32)
    return simple_call(return_relay_kernel, [shape] * 2, (near, far, tangent, lower, upper, ready), "return_relay")


def transposed_kernel(tangent, centre, lower, upper, ready, *rest):
    sums, raised, lowered = rest[:SUMS], rest[SUMS], rest[SUMS + 1]

    def products(start):
        at = rows_of(start, 8)
        value = tangent[at, :]
        raised[rows_of(start + 8, 8), :] = upper[at, :] * value
        lowered[rows_of(start + 8, 8), :] = lower[at, :] * value

    each_row_block(products)
    nothing = jnp.zeros((1, LANES), f32)
    fill_ends(raised, nothing, nothing)
    fill_ends(lowered, nothing, nothing)

    def stencil(start):
        at = rows_of(start, 8)
        sums[0][at, :] = (
            centre[at, :] * tangent[at, :] - raised[pl.ds(start + 7, 8), :] - lowered[pl.ds(start + 9, 8), :]
        )

    each_row_block(stencil)
    clear(sums[1:])


def transposed(tangent, centre, lower, upper, ready):
    return pl.pallas_call(
        transposed_kernel,
        out_shape=[resident(ROWS, LANES)] * SUMS,
        in_specs=[VMEM] * 5,
        out_specs=[VMEM] * SUMS,
        scratch_shapes=[pltpu.VMEM((ROWS + 16, LANES), f32)] * 2,
        compiler_params=params(8),
        cost_estimate=cost(1),
        name="transposed",
    )(tangent, centre, lower, upper, ready)


def donor_same_kernel(cells, rows_hbm, near_weights, far_weights, near, far, *refs):
    refs = refs[SUMS:]
    sums, staged, parts, sem = refs[:SUMS], refs[SUMS], refs[SUMS + 1 : SUMS + WAYS + 1], refs[SUMS + WAYS + 1]
    phases = index_copies(rows_hbm, segments(4, SAME), parts, sem)
    weights = weight_places(None, (near_weights, far_weights), None)
    spread_at_donors(grid_places(near, far), cells, SAME, weights, staged)
    finish(phases[0] + phases[1])
    add_rows(sums, parts, staged)


def add_same(cells, rows, near_weights, far_weights, near, far, sums):
    segs = segments(4, SAME)
    return pl.pallas_call(
        donor_same_kernel,
        out_shape=[resident(ROWS, LANES)] * SUMS,
        in_specs=[VMEM, HBM] + [VMEM] * (4 + SUMS),
        out_specs=[VMEM] * SUMS,
        scratch_shapes=[pltpu.VMEM((len(segs) * FRINGE, LANES), f32)] + index_scratch(segs),
        input_output_aliases={6 + w: w for w in range(SUMS)},
        compiler_params=params(8),
        cost_estimate=cost(9),
        name="add_same",
    )(cells, rows, near_weights, far_weights, near, far, *sums)


def sum_of_groups(value):
    for shift in (64, 32, 16):
        value = value + pltpu.roll(value, shift, 1)
    return value


def own_group():
    return lanes((8, LANES)) // PROBES == lax.broadcasted_iota(i32, (8, LANES), 0)


def donor_sides_kernel(cells, rows_hbm, before_weights, after_weights, before, after, *refs):
    refs = refs[SUMS:]
    adjoint, gram, sums, staged = refs[0], refs[1], refs[2 : 2 + SUMS], refs[2 + SUMS]
    parts, sem = refs[3 + SUMS : 3 + SUMS + WAYS], refs[3 + SUMS + WAYS]
    phases = index_copies(rows_hbm, segments(4, SIDES), parts, sem)
    weights = weight_places(before_weights, (None, None), after_weights)
    spread_at_donors({**pair_places(BEFORE, before), **pair_places(AFTER, after)}, cells, SIDES, weights, staged)
    finish(phases[0] + phases[1])
    add_rows(sums, parts, staged)
    lane = lanes((1, LANES))
    low, high = outer_rows(before, after)
    sums[0][0:1, :] = sums[0][0:1, :] - jnp.where(lane < PROBES, low, 0.0)
    end = sums[0][ROWS - 1 : ROWS, :]
    sums[0][ROWS - 1 : ROWS, :] = end - jnp.where(lane >= LANES - PROBES, high, 0.0)

    def total(start):
        at = rows_of(start, 8)
        value = sums[0][at, :]
        for part in sums[1:]:
            value = value + part[at, :]
        adjoint[at, :] = value

    each_row_block(total)

    def multiply(j, product):
        left_side, right_side = [], []
        for n in range(4):
            block = adjoint[aligned((j * 4 + n) * LANES, LANES), :]
            high, low = split(block)
            high_t, low_t = split(block.T)
            left_side += [high_t, high_t, low_t]
            right_side += [high, low, high]
        left_side = jnp.concatenate(left_side, axis=1)
        right_side = jnp.concatenate(right_side, axis=0)
        return product + jnp.dot(left_side, right_side, preferred_element_type=f32)

    product = lax.fori_loop(0, TILES // 4, multiply, jnp.zeros((LANES, LANES), f32))
    group = lanes((PROBES, LANES)) // PROBES
    folded = jnp.zeros((PROBES, LANES), f32)
    for g in range(GROUPS):
        folded = folded + jnp.where(group == g, product[g * PROBES : (g + 1) * PROBES, :], 0.0)
    folded = sum_of_groups(folded)
    for n in range(2):
        gram[n : n + 1, :] = jnp.sum(jnp.where(own_group(), folded[n * 8 : n * 8 + 8, :], 0.0), axis=0, keepdims=True)


def add_sides(cells, rows, before_weights, after_weights, before, after, sums):
    segs = segments(4, SIDES)
    outs = pl.pallas_call(
        donor_sides_kernel,
        out_shape=[resident(ROWS, LANES), jax.ShapeDtypeStruct((2, LANES), f32)]
        + [resident(ROWS, LANES)] * SUMS,
        in_specs=[VMEM, HBM] + [VMEM] * (4 + SUMS),
        out_specs=[VMEM] * (2 + SUMS),
        scratch_shapes=[pltpu.VMEM((len(segs) * FRINGE, LANES), f32)] + index_scratch(segs),
        input_output_aliases={6 + w: 2 + w for w in range(SUMS)},
        compiler_params=params(12),
        cost_estimate=cost(18),
        name="add_sides",
    )(cells, rows, before_weights, after_weights, before, after, *sums)
    return outs[0], outs[1]


def basis_kernel(total_cells, gram, adjoint, basis, factor, natural, sem):
    row = lax.broadcasted_iota(i32, (PROBES, LANES), 0)
    lane = lanes((PROBES, LANES))
    whole = jnp.concatenate(
        [sum_of_groups(jnp.where(own_group(), jnp.broadcast_to(gram[n : n + 1, :], (8, LANES)), 0.0)) for n in range(2)],
        axis=0,
    ) / f32(total_cells)
    columns = [jnp.broadcast_to(whole[:, j : j + 1], (PROBES, LANES)) for j in range(PROBES)]
    right = jnp.where(row == lane % PROBES, 1.0, 0.0)
    result = jnp.zeros((PROBES, LANES), f32)
    for j in range(PROBES):
        pivot = columns[j][j : j + 1, :]
        root = jnp.sqrt(pivot)
        ratio = jnp.where(row > j, columns[j] / pivot, 0.0)
        result = jnp.where((lane == j) & (row >= j), columns[j] / root, result)
        right_row = right[j : j + 1, :]
        right = jnp.where(row == j, right_row / root, right - ratio * right_row)
        for n in range(j + 1, PROBES):
            columns[n] = columns[n] - ratio * columns[n][j : j + 1, :]
    factor[...] = result[:, :PROBES]
    inverse = jnp.concatenate([right] * GROUPS, axis=0)
    same = lax.broadcasted_iota(i32, (LANES, LANES), 0) // PROBES == lanes((LANES, LANES)) // PROBES
    high, low = split(jnp.where(same, inverse, 0.0))
    left_side = jnp.concatenate([high, high, low], axis=1)

    def step(j, carry):
        for n in range(4):
            tile = j * 4 + n
            high, low = split(adjoint[aligned(tile * LANES, LANES), :])
            right_side = jnp.concatenate([high, low, high], axis=1)
            block = lax.dot_general(left_side, right_side, (((1,), (1,)), ((), ())), preferred_element_type=f32)
            for g in range(GROUPS):
                natural[:, aligned(g * ROWS + tile * LANES, LANES)] = block[g * PROBES : (g + 1) * PROBES, :]
        return carry

    copies = []
    for quarter in range(4):
        lax.fori_loop(quarter * TILES // 16, (quarter + 1) * TILES // 16, step, 0)
        for g in range(GROUPS):
            at = pl.ds(g * ROWS + quarter * ROWS // 4, ROWS // 4)
            copies.append(pltpu.make_async_copy(natural.at[:, at], basis.at[:, 0, at], sem.at[len(copies)]))
            copies[-1].start()
    finish(copies)


def basis_of(total_cells, gram, adjoint):
    return pl.pallas_call(
        functools.partial(basis_kernel, total_cells),
        out_shape=[
            jax.ShapeDtypeStruct((PROBES, 1, GROUPS * ROWS), f32),
            jax.ShapeDtypeStruct((PROBES, PROBES), f32),
        ],
        in_specs=[VMEM] * 2,
        out_specs=[FIXED, VMEM],
        scratch_shapes=[pltpu.VMEM((PROBES, GROUPS * ROWS), f32), pltpu.SemaphoreType.DMA((4 * GROUPS,))],
        compiler_params=params(8),
        cost_estimate=cost(6),
        name="basis",
    )(gram, adjoint)


def moved(value, place):
    grids, columns = (lax.axis_size(axis) for axis in AXES)
    route = []
    for g in range(grids):
        for c in range(columns):
            to_g, to_c = place(g, c)
            route.append((g * columns + c, (to_g % grids) * columns + to_c % columns))
    return lax.ppermute(value, AXES, route)


def along_grid(value, distance):
    return moved(value, lambda g, c: (g + distance, c))


def along_cell(value, distance):
    return moved(value, lambda g, c: (g, c + distance))


def axis_sum(value, axis):
    copies = jnp.broadcast_to(value, (lax.axis_size(axis),) + value.shape)
    return jnp.sum(lax.all_to_all(copies, axis, 0, 0), axis=0)


def body(probes, centre, lower_coef, upper_coef, donor_cells, receptor_cells, weights):
    donors = donor_cells[0]
    donor_rows = (donors & (ROWS - 1)).reshape(-1)
    receptor_rows = (receptor_cells & (ROWS - 1)).reshape(-1)
    near_weights, far_weights = along_grid(weights, -1)[0], along_grid(weights, -2)[0]
    table = table_of(probes)
    up, down = weight_relay(near_weights, far_weights, table)
    before_weights, after_weights = along_cell(up, 1), along_cell(down, -1)
    staged = rows_at_sides(table, donor_rows)
    up, down = side_sums(staged, donors, before_weights, after_weights)
    after, before = along_cell(up, 1), along_cell(down, -1)
    same = same_sums(table, donors, donor_rows, near_weights, far_weights)
    near, far = message_relay(before, same, after)
    near, far = along_grid(near, 1), along_grid(far, 2)
    c, l, u, *sums = forward(table, centre, lower_coef, upper_coef, before_weights, after_weights)
    tangent, far = couple(receptor_cells, receptor_rows, near, far, sums)
    far = along_grid(far, -2)
    near = along_grid(at_receptors(tangent, receptor_cells, receptor_rows), -1)
    sums = transposed(tangent, c, l, u, far)
    up, down = return_relay(near, far, tangent, l, u, sums[-1])
    before, after = along_cell(up, 1), along_cell(down, -1)
    sums = add_same(donors, donor_rows, near_weights, far_weights, near, far, sums)
    adjoint, gram = add_sides(donors, donor_rows, before_weights, after_weights, before, after, sums)
    total_cells = lax.axis_size("grid") * lax.axis_size("cell") * probes.shape[2]
    basis, factor = basis_of(total_cells, axis_sum(axis_sum(gram, "grid"), "cell"), adjoint)
    return (basis, factor)


def solution(mesh):
    in_specs = (
        P(None, "grid", "cell"),
        P("grid", "cell"),
        P("grid", "cell"),
        P("grid", "cell"),
        P("grid", None, "cell"),
        P("grid", "cell"),
        P("grid", None, "cell"),
    )
    out_specs = (P(None, "grid", "cell"), P())
    return jax.shard_map(body, mesh=mesh, in_specs=in_specs, out_specs=out_specs, check_vma=False)
```

```python
import functools

import jax
import jax.numpy as jnp
from jax import lax
from jax.experimental import pallas as pl
from jax.experimental.pallas import tpu as pltpu
from jax.sharding import PartitionSpec as P

f32 = jnp.float32
i32 = jnp.int32
bf16 = jnp.bfloat16

PROBES = 16
GROUPS = 8
ROWS = 4096
LANES = 128
PARTNERS = 6
FRINGE = 1024
HALF = 3 * FRINGE
SLOTS = PARTNERS * FRINGE
TILES = ROWS // LANES
WAYS = 8
SUMS = 4
QUARTER = SLOTS // 4
UNROLL = 8
ADD_UNROLL = 32

AXES = ("grid", "cell")

VMEM = pl.BlockSpec(memory_space=pltpu.VMEM)
HBM = pl.BlockSpec(memory_space=pl.ANY)
FIXED = pl.BlockSpec(memory_space=pltpu.HBM)


def aligned(start, size):
    return pl.ds(pl.multiple_of(start, size), size)


def rows_of(start, size):
    return pl.ds(pl.multiple_of(start, 8), size)


def split(x):
    high = x.astype(bf16)
    return high, (x - high.astype(f32)).astype(bf16)


def params(limit_mib):
    return pltpu.CompilerParams(vmem_limit_bytes=limit_mib << 20)


def cost(microseconds):
    return pl.CostEstimate(flops=0, transcendentals=0, bytes_accessed=microseconds * 3_000_000)


def resident(*shape):
    return pltpu.VMEM(shape, f32)


HEAD = 128


def segments(many, partners):
    return [(m, k) for m in range(many) for k in partners]


def index_scratch(segs):
    size = len(segs) * FRINGE // WAYS
    return [pltpu.SMEM((size,), i32)] * WAYS + [pltpu.SemaphoreType.DMA((3 * WAYS,))]


def index_copies(rows_hbm, segs, parts, sem):
    size = parts[0].shape[0]
    cuts = sorted({0, HEAD, size} | set(range(0, size, FRINGE)))
    phases = [[], []]
    for c in range(len(cuts) - 1):
        low, high = cuts[c], cuts[c + 1]
        for w in range(WAYS):
            seg, offset = divmod(w * size + low, FRINGE)
            start = segs[seg][0] * SLOTS + segs[seg][1] * FRINGE + offset
            copy = pltpu.make_async_copy(
                rows_hbm.at[pl.ds(start, high - low)], parts[w].at[pl.ds(low, high - low)], sem.at[c * WAYS + w]
            )
            copy.start()
            phases[min(c, 1)].append(copy)
    return phases


def finish(copies):
    for copy in copies:
        copy.wait()


def row_steps(parts, low, high, step):
    def outer(j, carry):
        for n in range(UNROLL):
            q = low + j * UNROLL + n
            for w in range(WAYS):
                step(w, q, parts[w][q])
        return carry

    lax.fori_loop(0, (high - low) // UNROLL, outer, 0)


def gather_rows(table, parts, staged, phases):
    count = parts[0].shape[0]

    def step(w, q, row):
        staged[pl.ds(w * count + q, 1), :] = table[pl.ds(row, 1), :]

    finish(phases[0])
    row_steps(parts, 0, HEAD, step)
    finish(phases[1])
    row_steps(parts, HEAD, count, step)


def clear(sums):
    def step(j, carry):
        for total in sums:
            for n in range(4):
                total[rows_of(j * 32 + n * 8, 8), :] = jnp.zeros((8, LANES), f32)
        return carry

    lax.fori_loop(0, ROWS // 32, step, 0)


def add_rows(sums, parts, staged):
    count = parts[0].shape[0]

    def outer(j, carry):
        for n in range(ADD_UNROLL):
            q = j * ADD_UNROLL + n
            for half in range(2):
                total = sums[half + n % 2 * 2]
                lists = [2 * m + half for m in range(4)]
                rows = [parts[w][q] for w in lists]
                old = [total[pl.ds(row, 1), :] for row in rows]
                new = [value + staged[pl.ds(w * count + q, 1), :] for value, w in zip(old, lists)]
                for row, value in zip(rows, new):
                    total[pl.ds(row, 1), :] = value
        return carry

    lax.fori_loop(0, count // ADD_UNROLL, outer, 0)


def groups_of(cells, m, offset):
    return jnp.broadcast_to(cells[m : m + 1, aligned(offset, LANES)], (8, LANES)) >> 12


def each_block(many, step):
    unroll = 8 // many

    def outer(j, carry):
        for n in range(unroll):
            step(j * unroll + n)
        return carry

    lax.fori_loop(0, FRINGE // LANES // unroll, outer, 0)


def select_fields(staged, cells, partners, weights, out):
    many = cells.shape[0]
    for n, k in enumerate(partners):

        def step(b):
            total = [jnp.zeros((8, LANES), f32)] * 2
            for m in range(many):
                field = staged[aligned((m * len(partners) + n) * FRINGE + b * LANES, LANES), :].T
                group = groups_of(cells, m, k * FRINGE + b * LANES)
                scale = 1.0
                if weights is not None:
                    ref, row, column = weights[k]
                    scale = ref[row + m : row + m + 1, aligned(column + b * LANES, LANES)]
                    scale = jnp.broadcast_to(scale, (8, LANES))
                for g in range(GROUPS):
                    factor = jnp.where(group == g, scale, 0.0)
                    for h in range(2):
                        at = g * PROBES + h * 8
                        total[h] = total[h] + field[at : at + 8, :] * factor
            ref, row, column = out[k]
            for h in range(2):
                ref[row + h * 8 : row + h * 8 + 8, aligned(column + b * LANES, LANES)] = total[h]

        each_block(many, step)


def spread_group(fields, cells, outs):
    group = [value >> 12 for value in cells]
    row = [value & (ROWS - 1) for value in cells]
    terms = [[jnp.where(group[m] == g, fields[m][h], 0.0) for g in range(GROUPS) for h in range(2)] for m in range(4)]
    for m in range(4):
        same = [row[m] == row[i] for i in range(m)]
        block = []
        for v in range(2 * GROUPS):
            value = terms[m][v]
            for i in range(m):
                value = value + jnp.where(same[i], terms[i][v], 0.0)
            block.append(value)
        ref, at = outs[m]
        ref[aligned(at, LANES), :] = jnp.concatenate(block, axis=0).T


def block_of(ref, row, column):
    return jnp.broadcast_to(ref[row : row + 1, aligned(column, LANES)], (8, LANES))


def field_of(place, b):
    ref, row, column = place
    return [ref[row + h * 8 : row + h * 8 + 8, aligned(column + b * LANES, LANES)] for h in range(2)]


def spread_at_donors(messages, cells, partners, weights, staged):
    for n, k in enumerate(partners):

        def step(b):
            field = field_of(messages[k], b)
            ref, row, column = weights[k]
            scale = [block_of(ref, row + m, column + b * LANES) for m in range(4)]
            fields = [[part * scale[m] for part in field] for m in range(4)]
            blocks = [block_of(cells, m, k * FRINGE + b * LANES) for m in range(4)]
            spread_group(fields, blocks, [(staged, (m * len(partners) + n) * FRINGE + b * LANES) for m in range(4)])

        each_block(4, step)


def spread_at_receptors(messages, cells, staged):
    for part in range(3):

        def step(j, carry):
            fields, blocks, outs = [], [], []
            for m in range(4):
                k, shift = divmod(m * QUARTER + part * 4 * LANES, FRINGE)
                fields.append(field_of(messages[k], j + shift // LANES))
                at = m * QUARTER + (part * 4 + j) * LANES
                blocks.append(block_of(cells, 0, at))
                outs.append((staged, at))
            spread_group(fields, blocks, outs)
            return carry

        lax.fori_loop(0, 4, step, 0, unroll=2)


def lanes(shape):
    return lax.broadcasted_iota(i32, shape, len(shape) - 1)


def fill_ends(padded, low, high):
    lane = lanes((1, LANES))
    before = pltpu.roll(padded[ROWS : ROWS + 8, :], PROBES, 1)[7:8, :]
    after = pltpu.roll(padded[8:16, :], LANES - PROBES, 1)[0:1, :]
    padded[7:8, :] = jnp.where(lane < PROBES, low, before)
    padded[ROWS + 8 : ROWS + 9, :] = jnp.where(lane >= LANES - PROBES, high, after)


def each_row_block(step):
    def outer(j, carry):
        for u in range(4):
            step(j * 32 + u * 8)
        return carry

    lax.fori_loop(0, ROWS // 32, outer, 0)


def table_kernel(probes, table, natural, sem):
    copies = [
        pltpu.make_async_copy(probes.at[p], natural.at[pl.ds(p, 1), :], sem.at[p]) for p in range(PROBES)
    ]
    for copy in copies:
        copy.start()
    finish(copies)

    def step(j, carry):
        for n in range(4):
            tile = j * 4 + n
            parts = [natural[:, aligned(g * ROWS + tile * LANES, LANES)] for g in range(GROUPS)]
            table[aligned(tile * LANES, LANES), :] = jnp.concatenate(parts, axis=0).T
        return carry

    lax.fori_loop(0, TILES // 4, step, 0)


def table_of(probes):
    return pl.pallas_call(
        table_kernel,
        out_shape=resident(ROWS, LANES),
        in_specs=[FIXED],
        out_specs=VMEM,
        scratch_shapes=[pltpu.VMEM((PROBES, GROUPS * ROWS), f32), pltpu.SemaphoreType.DMA((PROBES,))],
        compiler_params=params(60),
        cost_estimate=cost(3),
        name="table",
    )(probes)


BEFORE, SAME, AFTER = (0, 3), (1, 4), (2, 5)
SIDES = BEFORE + AFTER
NEAR, FAR = (0, 1, 2), (3, 4, 5)
EDGE = slice(FRINGE, FRINGE + LANES)


def weight_places(before, same, after):
    return {
        0: (before, 0, 0),
        3: (before, 4, 0),
        1: (same[0], 0, FRINGE),
        4: (same[1], 0, 4 * FRINGE),
        2: (after, 0, 0),
        5: (after, 4, 0),
    }


def pair_places(pair, ref):
    return {pair[0]: (ref, 0, 0), pair[1]: (ref, PROBES, 0)}


def grid_places(near, far):
    places = {k: (near, n * PROBES, 0) for n, k in enumerate(NEAR)}
    places.update({k: (far, n * PROBES, 0) for n, k in enumerate(FAR)})
    return places


def simple_call(kernel, out_shape, operands, name):
    return pl.pallas_call(
        kernel,
        out_shape=out_shape,
        in_specs=[VMEM] * len(operands),
        out_specs=[VMEM] * len(out_shape),
        compiler_params=params(8),
        cost_estimate=cost(1),
        name=name,
    )(*operands)


def weight_relay_kernel(near, far, table, up, down):
    for pair, out, rows in ((BEFORE, up, slice(ROWS - 8, ROWS)), (AFTER, down, slice(0, 8))):
        for n, ref in enumerate((near, far)):
            start = pair[n] * FRINGE
            out[n * 4 : n * 4 + 4, 0:FRINGE] = ref[:, start : start + FRINGE]
        out[:, EDGE] = table[rows, :]


def weight_relay(near, far, table):
    shape = jax.ShapeDtypeStruct((8, FRINGE + LANES), f32)
    return simple_call(weight_relay_kernel, [shape] * 2, (near, far, table), "weight_relay")


def rows_kernel(table, rows_hbm, staged, *rest):
    parts, sem = rest[:WAYS], rest[WAYS]
    gather_rows(table, parts, staged, index_copies(rows_hbm, segments(4, SIDES), parts, sem))


def rows_at_sides(table, rows):
    segs = segments(4, SIDES)
    return pl.pallas_call(
        rows_kernel,
        out_shape=resident(len(segs) * FRINGE, LANES),
        in_specs=[VMEM, HBM],
        out_specs=VMEM,
        scratch_shapes=index_scratch(segs),
        compiler_params=params(8),
        cost_estimate=cost(11),
        name="rows_at_sides",
    )(table, rows)


PAIR = jax.ShapeDtypeStruct((2 * PROBES, FRINGE), f32)
TRIPLE = jax.ShapeDtypeStruct((3 * PROBES, FRINGE), f32)


def side_sums_kernel(staged, cells, before, after, up, down):
    places = {**pair_places(AFTER, up), **pair_places(BEFORE, down)}
    select_fields(staged, cells, SIDES, weight_places(before, (None, None), after), places)


def side_sums(staged, cells, before, after):
    return simple_call(side_sums_kernel, [PAIR] * 2, (staged, cells, before, after), "side_sums")


def same_sums_kernel(table, cells, rows_hbm, near, far, out, staged, *rest):
    parts, sem = rest[:WAYS], rest[WAYS]
    gather_rows(table, parts, staged, index_copies(rows_hbm, segments(4, SAME), parts, sem))
    select_fields(staged, cells, SAME, weight_places(None, (near, far), None), pair_places(SAME, out))


def same_sums(table, cells, rows, near, far):
    segs = segments(4, SAME)
    return pl.pallas_call(
        same_sums_kernel,
        out_shape=PAIR,
        in_specs=[VMEM, VMEM, HBM, VMEM, VMEM],
        out_specs=VMEM,
        scratch_shapes=[pltpu.VMEM((len(segs) * FRINGE, LANES), f32)] + index_scratch(segs),
        compiler_params=params(8),
        cost_estimate=cost(8),
        name="same_sums",
    )(table, cells, rows, near, far)


def message_relay_kernel(before, same, after, near, far):
    for n, out in enumerate((near, far)):
        for i, ref in enumerate((before, same, after)):
            out[i * PROBES : (i + 1) * PROBES, :] = ref[n * PROBES : (n + 1) * PROBES, :]


def message_relay(before, same, after):
    return simple_call(message_relay_kernel, [TRIPLE] * 2, (before, same, after), "message_relay")


def end_flags():
    column = lax.axis_index("cell")
    return (column > 0).astype(f32), (column < lax.axis_size("cell") - 1).astype(f32)


def outer_rows(before, after):
    has_low, has_high = end_flags()
    low = pltpu.roll(before[0:8, EDGE], PROBES, 1)[7:8, :] * has_low
    high = pltpu.roll(after[0:8, EDGE], LANES - PROBES, 1)[0:1, :] * has_high
    return low, high


def forward_kernel(table, centre, lower, upper, before, after, c_out, l_out, u_out, *rest):
    sums, padded = rest[:SUMS], rest[SUMS]

    def step(j, carry):
        for n in range(2):
            tile = j * 2 + n
            at = aligned(tile * LANES, LANES)
            padded[rows_of(tile * LANES + 8, LANES), :] = table[at, :]
            for ref, out in ((centre, c_out), (lower, l_out), (upper, u_out)):
                parts = [
                    jnp.broadcast_to(ref[:, aligned(g * ROWS + tile * LANES, LANES)], (PROBES, LANES))
                    for g in range(GROUPS)
                ]
                out[at, :] = jnp.concatenate(parts, axis=0).T
        return carry

    lax.fori_loop(0, TILES // 2, step, 0)
    fill_ends(padded, *outer_rows(before, after))

    def stencil(start):
        at = rows_of(start, 8)
        sums[0][at, :] = (
            c_out[at, :] * padded[rows_of(start + 8, 8), :]
            - l_out[at, :] * padded[pl.ds(start + 7, 8), :]
            - u_out[at, :] * padded[pl.ds(start + 9, 8), :]
        )

    each_row_block(stencil)
    clear(sums[1:])


def forward(table, centre, lower, upper, before, after):
    return pl.pallas_call(
        forward_kernel,
        out_shape=[resident(ROWS, LANES)] * (3 + SUMS),
        in_specs=[VMEM] * 6,
        out_specs=[VMEM] * (3 + SUMS),
        scratch_shapes=[pltpu.VMEM((ROWS + 16, LANES), f32)],
        compiler_params=params(8),
        cost_estimate=cost(7),
        name="forward",
    )(table, centre, lower, upper, before, after)


def couple_kernel(cells, rows_hbm, near, far, *refs):
    refs = refs[SUMS:]
    tangent, out, sums = refs[0], refs[1], refs[2 : 2 + SUMS]
    staged, staged_far = refs[2 + SUMS : 4 + SUMS]
    refs = refs[4 + SUMS :]
    parts, sem, parts_far, sem_far = refs[:WAYS], refs[WAYS], refs[WAYS + 1 : 2 * WAYS + 1], refs[2 * WAYS + 1]
    every = NEAR + FAR
    phases = index_copies(rows_hbm, segments(1, every), parts, sem)
    phases_far = index_copies(rows_hbm, segments(1, FAR), parts_far, sem_far)
    spread_at_receptors(grid_places(near, far), cells, staged)
    finish(phases[0] + phases[1])
    add_rows(sums, parts, staged)

    def total(start):
        at = rows_of(start, 8)
        value = sums[0][at, :]
        for part in sums[1:]:
            value = value + part[at, :]
        tangent[at, :] = value

    each_row_block(total)
    gather_rows(tangent, parts_far, staged_far, phases_far)
    select_fields(staged_far, cells, FAR, None, grid_places(None, out))


def couple(cells, rows, near, far, sums):
    every, some = segments(1, NEAR + FAR), segments(1, FAR)
    outs = pl.pallas_call(
        couple_kernel,
        out_shape=[resident(ROWS, LANES), TRIPLE] + [resident(ROWS, LANES)] * SUMS,
        in_specs=[VMEM, HBM] + [VMEM] * (2 + SUMS),
        out_specs=[VMEM] * (2 + SUMS),
        scratch_shapes=[pltpu.VMEM((SLOTS, LANES), f32), pltpu.VMEM((SLOTS // 2, LANES), f32)]
        + index_scratch(every)
        + index_scratch(some),
        input_output_aliases={4 + w: 2 + w for w in range(SUMS)},
        compiler_params=params(8),
        cost_estimate=cost(11),
        name="couple",
    )(cells, rows, near, far, *sums)
    return outs[0], outs[1]


def receptor_kernel(tangent, cells, rows_hbm, out, staged, *rest):
    parts, sem = rest[:WAYS], rest[WAYS]
    gather_rows(tangent, parts, staged, index_copies(rows_hbm, segments(1, NEAR), parts, sem))
    select_fields(staged, cells, NEAR, None, grid_places(out, None))


def at_receptors(tangent, cells, rows):
    segs = segments(1, NEAR)
    return pl.pallas_call(
        receptor_kernel,
        out_shape=TRIPLE,
        in_specs=[VMEM, VMEM, HBM],
        out_specs=VMEM,
        scratch_shapes=[pltpu.VMEM((len(segs) * FRINGE, LANES), f32)] + index_scratch(segs),
        compiler_params=params(8),
        cost_estimate=cost(3),
        name="at_receptors",
    )(tangent, cells, rows)


def return_relay_kernel(near, far, tangent, lower, upper, ready, up, down):
    for n, ref in enumerate((near, far)):
        at = slice(n * PROBES, (n + 1) * PROBES)
        up[at, 0:FRINGE] = ref[0:PROBES, :]
        down[at, 0:FRINGE] = ref[2 * PROBES : 3 * PROBES, :]
    end = slice(ROWS - 8, ROWS)
    up[0:8, EDGE] = upper[end, :] * tangent[end, :]
    down[0:8, EDGE] = lower[0:8, :] * tangent[0:8, :]


def return_relay(near, far, tangent, lower, upper, ready):
    shape = jax.ShapeDtypeStruct((2 * PROBES, FRINGE + LANES), f32)
    return simple_call(return_relay_kernel, [shape] * 2, (near, far, tangent, lower, upper, ready), "return_relay")


def transposed_kernel(tangent, centre, lower, upper, ready, *rest):
    sums, raised, lowered = rest[:SUMS], rest[SUMS], rest[SUMS + 1]

    def products(start):
        at = rows_of(start, 8)
        value = tangent[at, :]
        raised[rows_of(start + 8, 8), :] = upper[at, :] * value
        lowered[rows_of(start + 8, 8), :] = lower[at, :] * value

    each_row_block(products)
    nothing = jnp.zeros((1, LANES), f32)
    fill_ends(raised, nothing, nothing)
    fill_ends(lowered, nothing, nothing)

    def stencil(start):
        at = rows_of(start, 8)
        sums[0][at, :] = (
            centre[at, :] * tangent[at, :] - raised[pl.ds(start + 7, 8), :] - lowered[pl.ds(start + 9, 8), :]
        )

    each_row_block(stencil)
    clear(sums[1:])


def transposed(tangent, centre, lower, upper, ready):
    return pl.pallas_call(
        transposed_kernel,
        out_shape=[resident(ROWS, LANES)] * SUMS,
        in_specs=[VMEM] * 5,
        out_specs=[VMEM] * SUMS,
        scratch_shapes=[pltpu.VMEM((ROWS + 16, LANES), f32)] * 2,
        compiler_params=params(8),
        cost_estimate=cost(1),
        name="transposed",
    )(tangent, centre, lower, upper, ready)


def donor_same_kernel(cells, rows_hbm, near_weights, far_weights, near, far, *refs):
    refs = refs[SUMS:]
    sums, staged, parts, sem = refs[:SUMS], refs[SUMS], refs[SUMS + 1 : SUMS + WAYS + 1], refs[SUMS + WAYS + 1]
    phases = index_copies(rows_hbm, segments(4, SAME), parts, sem)
    weights = weight_places(None, (near_weights, far_weights), None)
    spread_at_donors(grid_places(near, far), cells, SAME, weights, staged)
    finish(phases[0] + phases[1])
    add_rows(sums, parts, staged)


def add_same(cells, rows, near_weights, far_weights, near, far, sums):
    segs = segments(4, SAME)
    return pl.pallas_call(
        donor_same_kernel,
        out_shape=[resident(ROWS, LANES)] * SUMS,
        in_specs=[VMEM, HBM] + [VMEM] * (4 + SUMS),
        out_specs=[VMEM] * SUMS,
        scratch_shapes=[pltpu.VMEM((len(segs) * FRINGE, LANES), f32)] + index_scratch(segs),
        input_output_aliases={6 + w: w for w in range(SUMS)},
        compiler_params=params(8),
        cost_estimate=cost(9),
        name="add_same",
    )(cells, rows, near_weights, far_weights, near, far, *sums)


def sum_of_groups(value):
    for shift in (64, 32, 16):
        value = value + pltpu.roll(value, shift, 1)
    return value


def own_group():
    return lanes((8, LANES)) // PROBES == lax.broadcasted_iota(i32, (8, LANES), 0)


def donor_sides_kernel(cells, rows_hbm, before_weights, after_weights, before, after, *refs):
    refs = refs[SUMS:]
    adjoint, gram, sums, staged = refs[0], refs[1], refs[2 : 2 + SUMS], refs[2 + SUMS]
    parts, sem = refs[3 + SUMS : 3 + SUMS + WAYS], refs[3 + SUMS + WAYS]
    phases = index_copies(rows_hbm, segments(4, SIDES), parts, sem)
    weights = weight_places(before_weights, (None, None), after_weights)
    spread_at_donors({**pair_places(BEFORE, before), **pair_places(AFTER, after)}, cells, SIDES, weights, staged)
    finish(phases[0] + phases[1])
    add_rows(sums, parts, staged)
    lane = lanes((1, LANES))
    low, high = outer_rows(before, after)
    sums[0][0:1, :] = sums[0][0:1, :] - jnp.where(lane < PROBES, low, 0.0)
    end = sums[0][ROWS - 1 : ROWS, :]
    sums[0][ROWS - 1 : ROWS, :] = end - jnp.where(lane >= LANES - PROBES, high, 0.0)

    def total(start):
        at = rows_of(start, 8)
        value = sums[0][at, :]
        for part in sums[1:]:
            value = value + part[at, :]
        adjoint[at, :] = value

    each_row_block(total)

    def multiply(j, product):
        left_side, right_side = [], []
        for n in range(8):
            block = adjoint[aligned((j * 8 + n) * LANES, LANES), :]
            high, low = split(block)
            high_t, low_t = split(block.T)
            left_side += [high_t, high_t, low_t]
            right_side += [high, low, high]
        left_side = jnp.concatenate(left_side, axis=1)
        right_side = jnp.concatenate(right_side, axis=0)
        return product + jnp.dot(left_side, right_side, preferred_element_type=f32)

    product = lax.fori_loop(0, TILES // 8, multiply, jnp.zeros((LANES, LANES), f32))
    group = lanes((PROBES, LANES)) // PROBES
    folded = jnp.zeros((PROBES, LANES), f32)
    for g in range(GROUPS):
        folded = folded + jnp.where(group == g, product[g * PROBES : (g + 1) * PROBES, :], 0.0)
    folded = sum_of_groups(folded)
    for n in range(2):
        gram[n : n + 1, :] = jnp.sum(jnp.where(own_group(), folded[n * 8 : n * 8 + 8, :], 0.0), axis=0, keepdims=True)


def add_sides(cells, rows, before_weights, after_weights, before, after, sums):
    segs = segments(4, SIDES)
    outs = pl.pallas_call(
        donor_sides_kernel,
        out_shape=[resident(ROWS, LANES), jax.ShapeDtypeStruct((2, LANES), f32)]
        + [resident(ROWS, LANES)] * SUMS,
        in_specs=[VMEM, HBM] + [VMEM] * (4 + SUMS),
        out_specs=[VMEM] * (2 + SUMS),
        scratch_shapes=[pltpu.VMEM((len(segs) * FRINGE, LANES), f32)] + index_scratch(segs),
        input_output_aliases={6 + w: 2 + w for w in range(SUMS)},
        compiler_params=params(12),
        cost_estimate=cost(18),
        name="add_sides",
    )(cells, rows, before_weights, after_weights, before, after, *sums)
    return outs[0], outs[1]


def basis_kernel(total_cells, gram, adjoint, basis, factor, natural, sem):
    row = lax.broadcasted_iota(i32, (PROBES, LANES), 0)
    lane = lanes((PROBES, LANES))
    whole = jnp.concatenate(
        [sum_of_groups(jnp.where(own_group(), jnp.broadcast_to(gram[n : n + 1, :], (8, LANES)), 0.0)) for n in range(2)],
        axis=0,
    ) / f32(total_cells)
    columns = [jnp.broadcast_to(whole[:, j : j + 1], (PROBES, LANES)) for j in range(PROBES)]
    right = jnp.where(row == lane % PROBES, 1.0, 0.0)
    result = jnp.zeros((PROBES, LANES), f32)
    for j in range(PROBES):
        pivot = columns[j][j : j + 1, :]
        root = jnp.sqrt(pivot)
        ratio = jnp.where(row > j, columns[j] / pivot, 0.0)
        result = jnp.where((lane == j) & (row >= j), columns[j] / root, result)
        right_row = right[j : j + 1, :]
        right = jnp.where(row == j, right_row / root, right - ratio * right_row)
        for n in range(j + 1, PROBES):
            columns[n] = columns[n] - ratio * columns[n][j : j + 1, :]
    factor[...] = result[:, :PROBES]
    inverse = jnp.concatenate([right] * GROUPS, axis=0)
    same = lax.broadcasted_iota(i32, (LANES, LANES), 0) // PROBES == lanes((LANES, LANES)) // PROBES
    high, low = split(jnp.where(same, inverse, 0.0))
    left_side = jnp.concatenate([high, high, low], axis=1)

    def step(j, carry):
        for n in range(4):
            tile = j * 4 + n
            high, low = split(adjoint[aligned(tile * LANES, LANES), :])
            right_side = jnp.concatenate([high, low, high], axis=1)
            block = lax.dot_general(left_side, right_side, (((1,), (1,)), ((), ())), preferred_element_type=f32)
            for g in range(GROUPS):
                natural[:, aligned(g * ROWS + tile * LANES, LANES)] = block[g * PROBES : (g + 1) * PROBES, :]
        return carry

    copies = []
    for quarter in range(4):
        lax.fori_loop(quarter * TILES // 16, (quarter + 1) * TILES // 16, step, 0)
        for g in range(GROUPS):
            at = pl.ds(g * ROWS + quarter * ROWS // 4, ROWS // 4)
            copies.append(pltpu.make_async_copy(natural.at[:, at], basis.at[:, 0, at], sem.at[len(copies)]))
            copies[-1].start()
    finish(copies)


def basis_of(total_cells, gram, adjoint):
    return pl.pallas_call(
        functools.partial(basis_kernel, total_cells),
        out_shape=[
            jax.ShapeDtypeStruct((PROBES, 1, GROUPS * ROWS), f32),
            jax.ShapeDtypeStruct((PROBES, PROBES), f32),
        ],
        in_specs=[VMEM] * 2,
        out_specs=[FIXED, VMEM],
        scratch_shapes=[pltpu.VMEM((PROBES, GROUPS * ROWS), f32), pltpu.SemaphoreType.DMA((4 * GROUPS,))],
        compiler_params=params(8),
        cost_estimate=cost(6),
        name="basis",
    )(gram, adjoint)


def moved(value, place):
    grids, columns = (lax.axis_size(axis) for axis in AXES)
    route = []
    for g in range(grids):
        for c in range(columns):
            to_g, to_c = place(g, c)
            route.append((g * columns + c, (to_g % grids) * columns + to_c % columns))
    return lax.ppermute(value, AXES, route)


def along_grid(value, distance):
    return moved(value, lambda g, c: (g + distance, c))


def along_cell(value, distance):
    return moved(value, lambda g, c: (g, c + distance))


def axis_sum(value, axis):
    copies = jnp.broadcast_to(value, (lax.axis_size(axis),) + value.shape)
    return jnp.sum(lax.all_to_all(copies, axis, 0, 0), axis=0)


def body(probes, centre, lower_coef, upper_coef, donor_cells, receptor_cells, weights):
    donors = donor_cells[0]
    donor_rows = (donors & (ROWS - 1)).reshape(-1)
    receptor_rows = (receptor_cells & (ROWS - 1)).reshape(-1)
    near_weights, far_weights = along_grid(weights, -1)[0], along_grid(weights, -2)[0]
    table = table_of(probes)
    up, down = weight_relay(near_weights, far_weights, table)
    before_weights, after_weights = along_cell(up, 1), along_cell(down, -1)
    staged = rows_at_sides(table, donor_rows)
    up, down = side_sums(staged, donors, before_weights, after_weights)
    after, before = along_cell(up, 1), along_cell(down, -1)
    same = same_sums(table, donors, donor_rows, near_weights, far_weights)
    near, far = message_relay(before, same, after)
    near, far = along_grid(near, 1), along_grid(far, 2)
    c, l, u, *sums = forward(table, centre, lower_coef, upper_coef, before_weights, after_weights)
    tangent, far = couple(receptor_cells, receptor_rows, near, far, sums)
    far = along_grid(far, -2)
    near = along_grid(at_receptors(tangent, receptor_cells, receptor_rows), -1)
    sums = transposed(tangent, c, l, u, far)
    up, down = return_relay(near, far, tangent, l, u, sums[-1])
    before, after = along_cell(up, 1), along_cell(down, -1)
    sums = add_same(donors, donor_rows, near_weights, far_weights, near, far, sums)
    adjoint, gram = add_sides(donors, donor_rows, before_weights, after_weights, before, after, sums)
    total_cells = lax.axis_size("grid") * lax.axis_size("cell") * probes.shape[2]
    basis, factor = basis_of(total_cells, axis_sum(axis_sum(gram, "grid"), "cell"), adjoint)
    return (basis, factor)


def solution(mesh):
    in_specs = (
        P(None, "grid", "cell"),
        P("grid", "cell"),
        P("grid", "cell"),
        P("grid", "cell"),
        P("grid", None, "cell"),
        P("grid", "cell"),
        P("grid", None, "cell"),
    )
    out_specs = (P(None, "grid", "cell"), P())
    return jax.shard_map(body, mesh=mesh, in_specs=in_specs, out_specs=out_specs, check_vma=False)
```

```python
import functools

import jax
import jax.numpy as jnp
from jax import lax
from jax.experimental import pallas as pl
from jax.experimental.pallas import tpu as pltpu
from jax.sharding import PartitionSpec as P

f32 = jnp.float32
i32 = jnp.int32
bf16 = jnp.bfloat16

PROBES = 16
GROUPS = 8
ROWS = 4096
LANES = 128
PARTNERS = 6
FRINGE = 1024
HALF = 3 * FRINGE
SLOTS = PARTNERS * FRINGE
TILES = ROWS // LANES
WAYS = 8
SUMS = 4
QUARTER = SLOTS // 4
UNROLL = 16
ADD_UNROLL = 32

AXES = ("grid", "cell")

VMEM = pl.BlockSpec(memory_space=pltpu.VMEM)
HBM = pl.BlockSpec(memory_space=pl.ANY)
FIXED = pl.BlockSpec(memory_space=pltpu.HBM)


def aligned(start, size):
    return pl.ds(pl.multiple_of(start, size), size)


def rows_of(start, size):
    return pl.ds(pl.multiple_of(start, 8), size)


def split(x):
    high = x.astype(bf16)
    return high, (x - high.astype(f32)).astype(bf16)


def params(limit_mib):
    return pltpu.CompilerParams(vmem_limit_bytes=limit_mib << 20)


def cost(microseconds):
    return pl.CostEstimate(flops=0, transcendentals=0, bytes_accessed=microseconds * 3_000_000)


def resident(*shape):
    return pltpu.VMEM(shape, f32)


HEAD = 128


def segments(many, partners):
    return [(m, k) for m in range(many) for k in partners]


def index_scratch(segs):
    size = len(segs) * FRINGE // WAYS
    return [pltpu.SMEM((size,), i32)] * WAYS + [pltpu.SemaphoreType.DMA((3 * WAYS,))]


def index_copies(rows_hbm, segs, parts, sem):
    size = parts[0].shape[0]
    cuts = sorted({0, HEAD, size} | set(range(0, size, FRINGE)))
    phases = [[], []]
    for c in range(len(cuts) - 1):
        low, high = cuts[c], cuts[c + 1]
        for w in range(WAYS):
            seg, offset = divmod(w * size + low, FRINGE)
            start = segs[seg][0] * SLOTS + segs[seg][1] * FRINGE + offset
            copy = pltpu.make_async_copy(
                rows_hbm.at[pl.ds(start, high - low)], parts[w].at[pl.ds(low, high - low)], sem.at[c * WAYS + w]
            )
            copy.start()
            phases[min(c, 1)].append(copy)
    return phases


def finish(copies):
    for copy in copies:
        copy.wait()


def row_steps(parts, low, high, step):
    def outer(j, carry):
        for n in range(UNROLL):
            q = low + j * UNROLL + n
            for w in range(WAYS):
                step(w, q, parts[w][q])
        return carry

    lax.fori_loop(0, (high - low) // UNROLL, outer, 0)


def gather_rows(table, parts, staged, phases):
    count = parts[0].shape[0]

    def step(w, q, row):
        staged[pl.ds(w * count + q, 1), :] = table[pl.ds(row, 1), :]

    finish(phases[0])
    row_steps(parts, 0, HEAD, step)
    finish(phases[1])
    row_steps(parts, HEAD, count, step)


def clear(sums):
    def step(j, carry):
        for total in sums:
            for n in range(4):
                total[rows_of(j * 32 + n * 8, 8), :] = jnp.zeros((8, LANES), f32)
        return carry

    lax.fori_loop(0, ROWS // 32, step, 0)


def add_rows(sums, parts, staged):
    count = parts[0].shape[0]

    def outer(j, carry):
        for n in range(ADD_UNROLL):
            q = j * ADD_UNROLL + n
            for half in range(2):
                total = sums[half + n % 2 * 2]
                lists = [2 * m + half for m in range(4)]
                rows = [parts[w][q] for w in lists]
                old = [total[pl.ds(row, 1), :] for row in rows]
                new = [value + staged[pl.ds(w * count + q, 1), :] for value, w in zip(old, lists)]
                for row, value in zip(rows, new):
                    total[pl.ds(row, 1), :] = value
        return carry

    lax.fori_loop(0, count // ADD_UNROLL, outer, 0)


def groups_of(cells, m, offset):
    return jnp.broadcast_to(cells[m : m + 1, aligned(offset, LANES)], (8, LANES)) >> 12


def each_block(many, step):
    unroll = 8 // many

    def outer(j, carry):
        for n in range(unroll):
            step(j * unroll + n)
        return carry

    lax.fori_loop(0, FRINGE // LANES // unroll, outer, 0)


def select_fields(staged, cells, partners, weights, out):
    many = cells.shape[0]
    for n, k in enumerate(partners):

        def step(b):
            total = [jnp.zeros((8, LANES), f32)] * 2
            for m in range(many):
                field = staged[aligned((m * len(partners) + n) * FRINGE + b * LANES, LANES), :].T
                group = groups_of(cells, m, k * FRINGE + b * LANES)
                scale = 1.0
                if weights is not None:
                    ref, row, column = weights[k]
                    scale = ref[row + m : row + m + 1, aligned(column + b * LANES, LANES)]
                    scale = jnp.broadcast_to(scale, (8, LANES))
                for g in range(GROUPS):
                    factor = jnp.where(group == g, scale, 0.0)
                    for h in range(2):
                        at = g * PROBES + h * 8
                        total[h] = total[h] + field[at : at + 8, :] * factor
            ref, row, column = out[k]
            for h in range(2):
                ref[row + h * 8 : row + h * 8 + 8, aligned(column + b * LANES, LANES)] = total[h]

        each_block(many, step)


def spread_group(fields, cells, outs):
    group = [value >> 12 for value in cells]
    row = [value & (ROWS - 1) for value in cells]
    terms = [[jnp.where(group[m] == g, fields[m][h], 0.0) for g in range(GROUPS) for h in range(2)] for m in range(4)]
    for m in range(4):
        same = [row[m] == row[i] for i in range(m)]
        block = []
        for v in range(2 * GROUPS):
            value = terms[m][v]
            for i in range(m):
                value = value + jnp.where(same[i], terms[i][v], 0.0)
            block.append(value)
        ref, at = outs[m]
        ref[aligned(at, LANES), :] = jnp.concatenate(block, axis=0).T


def block_of(ref, row, column):
    return jnp.broadcast_to(ref[row : row + 1, aligned(column, LANES)], (8, LANES))


def field_of(place, b):
    ref, row, column = place
    return [ref[row + h * 8 : row + h * 8 + 8, aligned(column + b * LANES, LANES)] for h in range(2)]


def spread_at_donors(messages, cells, partners, weights, staged):
    for n, k in enumerate(partners):

        def step(b):
            field = field_of(messages[k], b)
            ref, row, column = weights[k]
            scale = [block_of(ref, row + m, column + b * LANES) for m in range(4)]
            fields = [[part * scale[m] for part in field] for m in range(4)]
            blocks = [block_of(cells, m, k * FRINGE + b * LANES) for m in range(4)]
            spread_group(fields, blocks, [(staged, (m * len(partners) + n) * FRINGE + b * LANES) for m in range(4)])

        each_block(4, step)


def spread_at_receptors(messages, cells, staged):
    for part in range(3):

        def step(j, carry):
            fields, blocks, outs = [], [], []
            for m in range(4):
                k, shift = divmod(m * QUARTER + part * 4 * LANES, FRINGE)
                fields.append(field_of(messages[k], j + shift // LANES))
                at = m * QUARTER + (part * 4 + j) * LANES
                blocks.append(block_of(cells, 0, at))
                outs.append((staged, at))
            spread_group(fields, blocks, outs)
            return carry

        lax.fori_loop(0, 4, step, 0, unroll=2)


def lanes(shape):
    return lax.broadcasted_iota(i32, shape, len(shape) - 1)


def fill_ends(padded, low, high):
    lane = lanes((1, LANES))
    before = pltpu.roll(padded[ROWS : ROWS + 8, :], PROBES, 1)[7:8, :]
    after = pltpu.roll(padded[8:16, :], LANES - PROBES, 1)[0:1, :]
    padded[7:8, :] = jnp.where(lane < PROBES, low, before)
    padded[ROWS + 8 : ROWS + 9, :] = jnp.where(lane >= LANES - PROBES, high, after)


def each_row_block(step):
    def outer(j, carry):
        for u in range(4):
            step(j * 32 + u * 8)
        return carry

    lax.fori_loop(0, ROWS // 32, outer, 0)


def table_kernel(probes, table, natural, sem):
    copies = [
        pltpu.make_async_copy(probes.at[p], natural.at[pl.ds(p, 1), :], sem.at[p]) for p in range(PROBES)
    ]
    for copy in copies:
        copy.start()
    finish(copies)

    def step(j, carry):
        for n in range(4):
            tile = j * 4 + n
            parts = [natural[:, aligned(g * ROWS + tile * LANES, LANES)] for g in range(GROUPS)]
            table[aligned(tile * LANES, LANES), :] = jnp.concatenate(parts, axis=0).T
        return carry

    lax.fori_loop(0, TILES // 4, step, 0)


def table_of(probes):
    return pl.pallas_call(
        table_kernel,
        out_shape=resident(ROWS, LANES),
        in_specs=[FIXED],
        out_specs=VMEM,
        scratch_shapes=[pltpu.VMEM((PROBES, GROUPS * ROWS), f32), pltpu.SemaphoreType.DMA((PROBES,))],
        compiler_params=params(60),
        cost_estimate=cost(3),
        name="table",
    )(probes)


BEFORE, SAME, AFTER = (0, 3), (1, 4), (2, 5)
SIDES = BEFORE + AFTER
NEAR, FAR = (0, 1, 2), (3, 4, 5)
EDGE = slice(FRINGE, FRINGE + LANES)


def weight_places(before, same, after):
    return {
        0: (before, 0, 0),
        3: (before, 4, 0),
        1: (same[0], 0, FRINGE),
        4: (same[1], 0, 4 * FRINGE),
        2: (after, 0, 0),
        5: (after, 4, 0),
    }


def pair_places(pair, ref):
    return {pair[0]: (ref, 0, 0), pair[1]: (ref, PROBES, 0)}


def grid_places(near, far):
    places = {k: (near, n * PROBES, 0) for n, k in enumerate(NEAR)}
    places.update({k: (far, n * PROBES, 0) for n, k in enumerate(FAR)})
    return places


def simple_call(kernel, out_shape, operands, name):
    return pl.pallas_call(
        kernel,
        out_shape=out_shape,
        in_specs=[VMEM] * len(operands),
        out_specs=[VMEM] * len(out_shape),
        compiler_params=params(8),
        cost_estimate=cost(1),
        name=name,
    )(*operands)


def weight_relay_kernel(near, far, table, up, down):
    for pair, out, rows in ((BEFORE, up, slice(ROWS - 8, ROWS)), (AFTER, down, slice(0, 8))):
        for n, ref in enumerate((near, far)):
            start = pair[n] * FRINGE
            out[n * 4 : n * 4 + 4, 0:FRINGE] = ref[:, start : start + FRINGE]
        out[:, EDGE] = table[rows, :]


def weight_relay(near, far, table):
    shape = jax.ShapeDtypeStruct((8, FRINGE + LANES), f32)
    return simple_call(weight_relay_kernel, [shape] * 2, (near, far, table), "weight_relay")


def rows_kernel(table, rows_hbm, staged, *rest):
    parts, sem = rest[:WAYS], rest[WAYS]
    gather_rows(table, parts, staged, index_copies(rows_hbm, segments(4, SIDES), parts, sem))


def rows_at_sides(table, rows):
    segs = segments(4, SIDES)
    return pl.pallas_call(
        rows_kernel,
        out_shape=resident(len(segs) * FRINGE, LANES),
        in_specs=[VMEM, HBM],
        out_specs=VMEM,
        scratch_shapes=index_scratch(segs),
        compiler_params=params(8),
        cost_estimate=cost(11),
        name="rows_at_sides",
    )(table, rows)


PAIR = jax.ShapeDtypeStruct((2 * PROBES, FRINGE), f32)
TRIPLE = jax.ShapeDtypeStruct((3 * PROBES, FRINGE), f32)


def side_sums_kernel(staged, cells, before, after, up, down):
    places = {**pair_places(AFTER, up), **pair_places(BEFORE, down)}
    select_fields(staged, cells, SIDES, weight_places(before, (None, None), after), places)


def side_sums(staged, cells, before, after):
    return simple_call(side_sums_kernel, [PAIR] * 2, (staged, cells, before, after), "side_sums")


def same_sums_kernel(table, cells, rows_hbm, near, far, out, staged, *rest):
    parts, sem = rest[:WAYS], rest[WAYS]
    gather_rows(table, parts, staged, index_copies(rows_hbm, segments(4, SAME), parts, sem))
    select_fields(staged, cells, SAME, weight_places(None, (near, far), None), pair_places(SAME, out))


def same_sums(table, cells, rows, near, far):
    segs = segments(4, SAME)
    return pl.pallas_call(
        same_sums_kernel,
        out_shape=PAIR,
        in_specs=[VMEM, VMEM, HBM, VMEM, VMEM],
        out_specs=VMEM,
        scratch_shapes=[pltpu.VMEM((len(segs) * FRINGE, LANES), f32)] + index_scratch(segs),
        compiler_params=params(8),
        cost_estimate=cost(8),
        name="same_sums",
    )(table, cells, rows, near, far)


def message_relay_kernel(before, same, after, near, far):
    for n, out in enumerate((near, far)):
        for i, ref in enumerate((before, same, after)):
            out[i * PROBES : (i + 1) * PROBES, :] = ref[n * PROBES : (n + 1) * PROBES, :]


def message_relay(before, same, after):
    return simple_call(message_relay_kernel, [TRIPLE] * 2, (before, same, after), "message_relay")


def end_flags():
    column = lax.axis_index("cell")
    return (column > 0).astype(f32), (column < lax.axis_size("cell") - 1).astype(f32)


def outer_rows(before, after):
    has_low, has_high = end_flags()
    low = pltpu.roll(before[0:8, EDGE], PROBES, 1)[7:8, :] * has_low
    high = pltpu.roll(after[0:8, EDGE], LANES - PROBES, 1)[0:1, :] * has_high
    return low, high


def forward_kernel(table, centre, lower, upper, before, after, c_out, l_out, u_out, *rest):
    sums, padded = rest[:SUMS], rest[SUMS]

    def step(j, carry):
        for n in range(2):
            tile = j * 2 + n
            at = aligned(tile * LANES, LANES)
            padded[rows_of(tile * LANES + 8, LANES), :] = table[at, :]
            for ref, out in ((centre, c_out), (lower, l_out), (upper, u_out)):
                parts = [
                    jnp.broadcast_to(ref[:, aligned(g * ROWS + tile * LANES, LANES)], (PROBES, LANES))
                    for g in range(GROUPS)
                ]
                out[at, :] = jnp.concatenate(parts, axis=0).T
        return carry

    lax.fori_loop(0, TILES // 2, step, 0)
    fill_ends(padded, *outer_rows(before, after))

    def stencil(start):
        at = rows_of(start, 8)
        sums[0][at, :] = (
            c_out[at, :] * padded[rows_of(start + 8, 8), :]
            - l_out[at, :] * padded[pl.ds(start + 7, 8), :]
            - u_out[at, :] * padded[pl.ds(start + 9, 8), :]
        )

    each_row_block(stencil)
    clear(sums[1:])


def forward(table, centre, lower, upper, before, after):
    return pl.pallas_call(
        forward_kernel,
        out_shape=[resident(ROWS, LANES)] * (3 + SUMS),
        in_specs=[VMEM] * 6,
        out_specs=[VMEM] * (3 + SUMS),
        scratch_shapes=[pltpu.VMEM((ROWS + 16, LANES), f32)],
        compiler_params=params(8),
        cost_estimate=cost(7),
        name="forward",
    )(table, centre, lower, upper, before, after)


def couple_kernel(cells, rows_hbm, near, far, *refs):
    refs = refs[SUMS:]
    tangent, out, sums = refs[0], refs[1], refs[2 : 2 + SUMS]
    staged, staged_far = refs[2 + SUMS : 4 + SUMS]
    refs = refs[4 + SUMS :]
    parts, sem, parts_far, sem_far = refs[:WAYS], refs[WAYS], refs[WAYS + 1 : 2 * WAYS + 1], refs[2 * WAYS + 1]
    every = NEAR + FAR
    phases = index_copies(rows_hbm, segments(1, every), parts, sem)
    phases_far = index_copies(rows_hbm, segments(1, FAR), parts_far, sem_far)
    spread_at_receptors(grid_places(near, far), cells, staged)
    finish(phases[0] + phases[1])
    add_rows(sums, parts, staged)

    def total(start):
        at = rows_of(start, 8)
        value = sums[0][at, :]
        for part in sums[1:]:
            value = value + part[at, :]
        tangent[at, :] = value

    each_row_block(total)
    gather_rows(tangent, parts_far, staged_far, phases_far)
    select_fields(staged_far, cells, FAR, None, grid_places(None, out))


def couple(cells, rows, near, far, sums):
    every, some = segments(1, NEAR + FAR), segments(1, FAR)
    outs = pl.pallas_call(
        couple_kernel,
        out_shape=[resident(ROWS, LANES), TRIPLE] + [resident(ROWS, LANES)] * SUMS,
        in_specs=[VMEM, HBM] + [VMEM] * (2 + SUMS),
        out_specs=[VMEM] * (2 + SUMS),
        scratch_shapes=[pltpu.VMEM((SLOTS, LANES), f32), pltpu.VMEM((SLOTS // 2, LANES), f32)]
        + index_scratch(every)
        + index_scratch(some),
        input_output_aliases={4 + w: 2 + w for w in range(SUMS)},
        compiler_params=params(8),
        cost_estimate=cost(11),
        name="couple",
    )(cells, rows, near, far, *sums)
    return outs[0], outs[1]


def receptor_kernel(tangent, cells, rows_hbm, out, staged, *rest):
    parts, sem = rest[:WAYS], rest[WAYS]
    gather_rows(tangent, parts, staged, index_copies(rows_hbm, segments(1, NEAR), parts, sem))
    select_fields(staged, cells, NEAR, None, grid_places(out, None))


def at_receptors(tangent, cells, rows):
    segs = segments(1, NEAR)
    return pl.pallas_call(
        receptor_kernel,
        out_shape=TRIPLE,
        in_specs=[VMEM, VMEM, HBM],
        out_specs=VMEM,
        scratch_shapes=[pltpu.VMEM((len(segs) * FRINGE, LANES), f32)] + index_scratch(segs),
        compiler_params=params(8),
        cost_estimate=cost(3),
        name="at_receptors",
    )(tangent, cells, rows)


def return_relay_kernel(near, far, tangent, lower, upper, ready, up, down):
    for n, ref in enumerate((near, far)):
        at = slice(n * PROBES, (n + 1) * PROBES)
        up[at, 0:FRINGE] = ref[0:PROBES, :]
        down[at, 0:FRINGE] = ref[2 * PROBES : 3 * PROBES, :]
    end = slice(ROWS - 8, ROWS)
    up[0:8, EDGE] = upper[end, :] * tangent[end, :]
    down[0:8, EDGE] = lower[0:8, :] * tangent[0:8, :]


def return_relay(near, far, tangent, lower, upper, ready):
    shape = jax.ShapeDtypeStruct((2 * PROBES, FRINGE + LANES), f32)
    return simple_call(return_relay_kernel, [shape] * 2, (near, far, tangent, lower, upper, ready), "return_relay")


def transposed_kernel(tangent, centre, lower, upper, ready, *rest):
    sums, raised, lowered = rest[:SUMS], rest[SUMS], rest[SUMS + 1]

    def products(start):
        at = rows_of(start, 8)
        value = tangent[at, :]
        raised[rows_of(start + 8, 8), :] = upper[at, :] * value
        lowered[rows_of(start + 8, 8), :] = lower[at, :] * value

    each_row_block(products)
    nothing = jnp.zeros((1, LANES), f32)
    fill_ends(raised, nothing, nothing)
    fill_ends(lowered, nothing, nothing)

    def stencil(start):
        at = rows_of(start, 8)
        sums[0][at, :] = (
            centre[at, :] * tangent[at, :] - raised[pl.ds(start + 7, 8), :] - lowered[pl.ds(start + 9, 8), :]
        )

    each_row_block(stencil)
    clear(sums[1:])


def transposed(tangent, centre, lower, upper, ready):
    return pl.pallas_call(
        transposed_kernel,
        out_shape=[resident(ROWS, LANES)] * SUMS,
        in_specs=[VMEM] * 5,
        out_specs=[VMEM] * SUMS,
        scratch_shapes=[pltpu.VMEM((ROWS + 16, LANES), f32)] * 2,
        compiler_params=params(8),
        cost_estimate=cost(1),
        name="transposed",
    )(tangent, centre, lower, upper, ready)


def donor_same_kernel(cells, rows_hbm, near_weights, far_weights, near, far, *refs):
    refs = refs[SUMS:]
    sums, staged, parts, sem = refs[:SUMS], refs[SUMS], refs[SUMS + 1 : SUMS + WAYS + 1], refs[SUMS + WAYS + 1]
    phases = index_copies(rows_hbm, segments(4, SAME), parts, sem)
    weights = weight_places(None, (near_weights, far_weights), None)
    spread_at_donors(grid_places(near, far), cells, SAME, weights, staged)
    finish(phases[0] + phases[1])
    add_rows(sums, parts, staged)


def add_same(cells, rows, near_weights, far_weights, near, far, sums):
    segs = segments(4, SAME)
    return pl.pallas_call(
        donor_same_kernel,
        out_shape=[resident(ROWS, LANES)] * SUMS,
        in_specs=[VMEM, HBM] + [VMEM] * (4 + SUMS),
        out_specs=[VMEM] * SUMS,
        scratch_shapes=[pltpu.VMEM((len(segs) * FRINGE, LANES), f32)] + index_scratch(segs),
        input_output_aliases={6 + w: w for w in range(SUMS)},
        compiler_params=params(8),
        cost_estimate=cost(9),
        name="add_same",
    )(cells, rows, near_weights, far_weights, near, far, *sums)


def sum_of_groups(value):
    for shift in (64, 32, 16):
        value = value + pltpu.roll(value, shift, 1)
    return value


def own_group():
    return lanes((8, LANES)) // PROBES == lax.broadcasted_iota(i32, (8, LANES), 0)


def donor_sides_kernel(cells, rows_hbm, before_weights, after_weights, before, after, *refs):
    refs = refs[SUMS:]
    adjoint, gram, sums, staged = refs[0], refs[1], refs[2 : 2 + SUMS], refs[2 + SUMS]
    parts, sem = refs[3 + SUMS : 3 + SUMS + WAYS], refs[3 + SUMS + WAYS]
    phases = index_copies(rows_hbm, segments(4, SIDES), parts, sem)
    weights = weight_places(before_weights, (None, None), after_weights)
    spread_at_donors({**pair_places(BEFORE, before), **pair_places(AFTER, after)}, cells, SIDES, weights, staged)
    finish(phases[0] + phases[1])
    add_rows(sums, parts, staged)
    lane = lanes((1, LANES))
    low, high = outer_rows(before, after)
    sums[0][0:1, :] = sums[0][0:1, :] - jnp.where(lane < PROBES, low, 0.0)
    end = sums[0][ROWS - 1 : ROWS, :]
    sums[0][ROWS - 1 : ROWS, :] = end - jnp.where(lane >= LANES - PROBES, high, 0.0)

    def total(start):
        at = rows_of(start, 8)
        value = sums[0][at, :]
        for part in sums[1:]:
            value = value + part[at, :]
        adjoint[at, :] = value

    each_row_block(total)

    def multiply(j, product):
        left_side, right_side = [], []
        for n in range(8):
            block = adjoint[aligned((j * 8 + n) * LANES, LANES), :]
            high, low = split(block)
            high_t, low_t = split(block.T)
            left_side += [high_t, high_t, low_t]
            right_side += [high, low, high]
        left_side = jnp.concatenate(left_side, axis=1)
        right_side = jnp.concatenate(right_side, axis=0)
        return product + jnp.dot(left_side, right_side, preferred_element_type=f32)

    product = lax.fori_loop(0, TILES // 8, multiply, jnp.zeros((LANES, LANES), f32))
    group = lanes((PROBES, LANES)) // PROBES
    folded = jnp.zeros((PROBES, LANES), f32)
    for g in range(GROUPS):
        folded = folded + jnp.where(group == g, product[g * PROBES : (g + 1) * PROBES, :], 0.0)
    folded = sum_of_groups(folded)
    for n in range(2):
        gram[n : n + 1, :] = jnp.sum(jnp.where(own_group(), folded[n * 8 : n * 8 + 8, :], 0.0), axis=0, keepdims=True)


def add_sides(cells, rows, before_weights, after_weights, before, after, sums):
    segs = segments(4, SIDES)
    outs = pl.pallas_call(
        donor_sides_kernel,
        out_shape=[resident(ROWS, LANES), jax.ShapeDtypeStruct((2, LANES), f32)]
        + [resident(ROWS, LANES)] * SUMS,
        in_specs=[VMEM, HBM] + [VMEM] * (4 + SUMS),
        out_specs=[VMEM] * (2 + SUMS),
        scratch_shapes=[pltpu.VMEM((len(segs) * FRINGE, LANES), f32)] + index_scratch(segs),
        input_output_aliases={6 + w: 2 + w for w in range(SUMS)},
        compiler_params=params(12),
        cost_estimate=cost(18),
        name="add_sides",
    )(cells, rows, before_weights, after_weights, before, after, *sums)
    return outs[0], outs[1]


def basis_kernel(total_cells, gram, adjoint, basis, factor, natural, sem):
    row = lax.broadcasted_iota(i32, (PROBES, LANES), 0)
    lane = lanes((PROBES, LANES))
    whole = jnp.concatenate(
        [sum_of_groups(jnp.where(own_group(), jnp.broadcast_to(gram[n : n + 1, :], (8, LANES)), 0.0)) for n in range(2)],
        axis=0,
    ) / f32(total_cells)
    columns = [jnp.broadcast_to(whole[:, j : j + 1], (PROBES, LANES)) for j in range(PROBES)]
    right = jnp.where(row == lane % PROBES, 1.0, 0.0)
    result = jnp.zeros((PROBES, LANES), f32)
    for j in range(PROBES):
        pivot = columns[j][j : j + 1, :]
        root = jnp.sqrt(pivot)
        ratio = jnp.where(row > j, columns[j] / pivot, 0.0)
        result = jnp.where((lane == j) & (row >= j), columns[j] / root, result)
        right_row = right[j : j + 1, :]
        right = jnp.where(row == j, right_row / root, right - ratio * right_row)
        for n in range(j + 1, PROBES):
            columns[n] = columns[n] - ratio * columns[n][j : j + 1, :]
    factor[...] = result[:, :PROBES]
    inverse = jnp.concatenate([right] * GROUPS, axis=0)
    same = lax.broadcasted_iota(i32, (LANES, LANES), 0) // PROBES == lanes((LANES, LANES)) // PROBES
    high, low = split(jnp.where(same, inverse, 0.0))
    left_side = jnp.concatenate([high, high, low], axis=1)

    def step(j, carry):
        for n in range(4):
            tile = j * 4 + n
            high, low = split(adjoint[aligned(tile * LANES, LANES), :])
            right_side = jnp.concatenate([high, low, high], axis=1)
            block = lax.dot_general(left_side, right_side, (((1,), (1,)), ((), ())), preferred_element_type=f32)
            for g in range(GROUPS):
                natural[:, aligned(g * ROWS + tile * LANES, LANES)] = block[g * PROBES : (g + 1) * PROBES, :]
        return carry

    copies = []
    for quarter in range(4):
        lax.fori_loop(quarter * TILES // 16, (quarter + 1) * TILES // 16, step, 0)
        for g in range(GROUPS):
            at = pl.ds(g * ROWS + quarter * ROWS // 4, ROWS // 4)
            copies.append(pltpu.make_async_copy(natural.at[:, at], basis.at[:, 0, at], sem.at[len(copies)]))
            copies[-1].start()
    finish(copies)


def basis_of(total_cells, gram, adjoint):
    return pl.pallas_call(
        functools.partial(basis_kernel, total_cells),
        out_shape=[
            jax.ShapeDtypeStruct((PROBES, 1, GROUPS * ROWS), f32),
            jax.ShapeDtypeStruct((PROBES, PROBES), f32),
        ],
        in_specs=[VMEM] * 2,
        out_specs=[FIXED, VMEM],
        scratch_shapes=[pltpu.VMEM((PROBES, GROUPS * ROWS), f32), pltpu.SemaphoreType.DMA((4 * GROUPS,))],
        compiler_params=params(8),
        cost_estimate=cost(6),
        name="basis",
    )(gram, adjoint)


def moved(value, place):
    grids, columns = (lax.axis_size(axis) for axis in AXES)
    route = []
    for g in range(grids):
        for c in range(columns):
            to_g, to_c = place(g, c)
            route.append((g * columns + c, (to_g % grids) * columns + to_c % columns))
    return lax.ppermute(value, AXES, route)


def along_grid(value, distance):
    return moved(value, lambda g, c: (g + distance, c))


def along_cell(value, distance):
    return moved(value, lambda g, c: (g, c + distance))


def axis_sum(value, axis):
    copies = jnp.broadcast_to(value, (lax.axis_size(axis),) + value.shape)
    return jnp.sum(lax.all_to_all(copies, axis, 0, 0), axis=0)


def body(probes, centre, lower_coef, upper_coef, donor_cells, receptor_cells, weights):
    donors = donor_cells[0]
    donor_rows = (donors & (ROWS - 1)).reshape(-1)
    receptor_rows = (receptor_cells & (ROWS - 1)).reshape(-1)
    near_weights, far_weights = along_grid(weights, -1)[0], along_grid(weights, -2)[0]
    table = table_of(probes)
    up, down = weight_relay(near_weights, far_weights, table)
    before_weights, after_weights = along_cell(up, 1), along_cell(down, -1)
    staged = rows_at_sides(table, donor_rows)
    up, down = side_sums(staged, donors, before_weights, after_weights)
    after, before = along_cell(up, 1), along_cell(down, -1)
    same = same_sums(table, donors, donor_rows, near_weights, far_weights)
    near, far = message_relay(before, same, after)
    near, far = along_grid(near, 1), along_grid(far, 2)
    c, l, u, *sums = forward(table, centre, lower_coef, upper_coef, before_weights, after_weights)
    tangent, far = couple(receptor_cells, receptor_rows, near, far, sums)
    far = along_grid(far, -2)
    near = along_grid(at_receptors(tangent, receptor_cells, receptor_rows), -1)
    sums = transposed(tangent, c, l, u, far)
    up, down = return_relay(near, far, tangent, l, u, sums[-1])
    before, after = along_cell(up, 1), along_cell(down, -1)
    sums = add_same(donors, donor_rows, near_weights, far_weights, near, far, sums)
    adjoint, gram = add_sides(donors, donor_rows, before_weights, after_weights, before, after, sums)
    total_cells = lax.axis_size("grid") * lax.axis_size("cell") * probes.shape[2]
    basis, factor = basis_of(total_cells, axis_sum(axis_sum(gram, "grid"), "cell"), adjoint)
    return (basis, factor)


def solution(mesh):
    in_specs = (
        P(None, "grid", "cell"),
        P("grid", "cell"),
        P("grid", "cell"),
        P("grid", "cell"),
        P("grid", None, "cell"),
        P("grid", "cell"),
        P("grid", None, "cell"),
    )
    out_specs = (P(None, "grid", "cell"), P())
    return jax.shard_map(body, mesh=mesh, in_specs=in_specs, out_specs=out_specs, check_vma=False)
```

```python
import functools

import jax
import jax.numpy as jnp
from jax import lax
from jax.experimental import pallas as pl
from jax.experimental.pallas import tpu as pltpu
from jax.sharding import PartitionSpec as P

f32 = jnp.float32
i32 = jnp.int32
bf16 = jnp.bfloat16

PROBES = 16
GROUPS = 8
ROWS = 4096
LANES = 128
PARTNERS = 6
FRINGE = 1024
HALF = 3 * FRINGE
SLOTS = PARTNERS * FRINGE
TILES = ROWS // LANES
WAYS = 8
SUMS = 4
QUARTER = SLOTS // 4
UNROLL = 32
ADD_UNROLL = 32

AXES = ("grid", "cell")

VMEM = pl.BlockSpec(memory_space=pltpu.VMEM)
HBM = pl.BlockSpec(memory_space=pl.ANY)
FIXED = pl.BlockSpec(memory_space=pltpu.HBM)


def aligned(start, size):
    return pl.ds(pl.multiple_of(start, size), size)


def rows_of(start, size):
    return pl.ds(pl.multiple_of(start, 8), size)


def split(x):
    high = x.astype(bf16)
    return high, (x - high.astype(f32)).astype(bf16)


def params(limit_mib):
    return pltpu.CompilerParams(vmem_limit_bytes=limit_mib << 20)


def cost(microseconds):
    return pl.CostEstimate(flops=0, transcendentals=0, bytes_accessed=microseconds * 3_000_000)


def resident(*shape):
    return pltpu.VMEM(shape, f32)


HEAD = 128


def segments(many, partners):
    return [(m, k) for m in range(many) for k in partners]


def index_scratch(segs):
    size = len(segs) * FRINGE // WAYS
    return [pltpu.SMEM((size,), i32)] * WAYS + [pltpu.SemaphoreType.DMA((3 * WAYS,))]


def index_copies(rows_hbm, segs, parts, sem):
    size = parts[0].shape[0]
    cuts = sorted({0, HEAD, size} | set(range(0, size, FRINGE)))
    phases = [[], []]
    for c in range(len(cuts) - 1):
        low, high = cuts[c], cuts[c + 1]
        for w in range(WAYS):
            seg, offset = divmod(w * size + low, FRINGE)
            start = segs[seg][0] * SLOTS + segs[seg][1] * FRINGE + offset
            copy = pltpu.make_async_copy(
                rows_hbm.at[pl.ds(start, high - low)], parts[w].at[pl.ds(low, high - low)], sem.at[c * WAYS + w]
            )
            copy.start()
            phases[min(c, 1)].append(copy)
    return phases


def finish(copies):
    for copy in copies:
        copy.wait()


def row_steps(parts, low, high, step):
    def outer(j, carry):
        for n in range(UNROLL):
            q = low + j * UNROLL + n
            for w in range(WAYS):
                step(w, q, parts[w][q])
        return carry

    lax.fori_loop(0, (high - low) // UNROLL, outer, 0)


def gather_rows(table, parts, staged, phases):
    count = parts[0].shape[0]

    def step(w, q, row):
        staged[pl.ds(w * count + q, 1), :] = table[pl.ds(row, 1), :]

    finish(phases[0])
    row_steps(parts, 0, HEAD, step)
    finish(phases[1])
    row_steps(parts, HEAD, count, step)


def clear(sums):
    def step(j, carry):
        for total in sums:
            for n in range(4):
                total[rows_of(j * 32 + n * 8, 8), :] = jnp.zeros((8, LANES), f32)
        return carry

    lax.fori_loop(0, ROWS // 32, step, 0)


def add_rows(sums, parts, staged):
    count = parts[0].shape[0]

    def outer(j, carry):
        for n in range(ADD_UNROLL):
            q = j * ADD_UNROLL + n
            for half in range(2):
                total = sums[half + n % 2 * 2]
                lists = [2 * m + half for m in range(4)]
                rows = [parts[w][q] for w in lists]
                old = [total[pl.ds(row, 1), :] for row in rows]
                new = [value + staged[pl.ds(w * count + q, 1), :] for value, w in zip(old, lists)]
                for row, value in zip(rows, new):
                    total[pl.ds(row, 1), :] = value
        return carry

    lax.fori_loop(0, count // ADD_UNROLL, outer, 0)


def groups_of(cells, m, offset):
    return jnp.broadcast_to(cells[m : m + 1, aligned(offset, LANES)], (8, LANES)) >> 12


def each_block(many, step):
    unroll = 8 // many

    def outer(j, carry):
        for n in range(unroll):
            step(j * unroll + n)
        return carry

    lax.fori_loop(0, FRINGE // LANES // unroll, outer, 0)


def select_fields(staged, cells, partners, weights, out):
    many = cells.shape[0]
    for n, k in enumerate(partners):

        def step(b):
            total = [jnp.zeros((8, LANES), f32)] * 2
            for m in range(many):
                field = staged[aligned((m * len(partners) + n) * FRINGE + b * LANES, LANES), :].T
                group = groups_of(cells, m, k * FRINGE + b * LANES)
                scale = 1.0
                if weights is not None:
                    ref, row, column = weights[k]
                    scale = ref[row + m : row + m + 1, aligned(column + b * LANES, LANES)]
                    scale = jnp.broadcast_to(scale, (8, LANES))
                for g in range(GROUPS):
                    factor = jnp.where(group == g, scale, 0.0)
                    for h in range(2):
                        at = g * PROBES + h * 8
                        total[h] = total[h] + field[at : at + 8, :] * factor
            ref, row, column = out[k]
            for h in range(2):
                ref[row + h * 8 : row + h * 8 + 8, aligned(column + b * LANES, LANES)] = total[h]

        each_block(many, step)


def spread_group(fields, cells, outs):
    group = [value >> 12 for value in cells]
    row = [value & (ROWS - 1) for value in cells]
    terms = [[jnp.where(group[m] == g, fields[m][h], 0.0) for g in range(GROUPS) for h in range(2)] for m in range(4)]
    for m in range(4):
        same = [row[m] == row[i] for i in range(m)]
        block = []
        for v in range(2 * GROUPS):
            value = terms[m][v]
            for i in range(m):
                value = value + jnp.where(same[i], terms[i][v], 0.0)
            block.append(value)
        ref, at = outs[m]
        ref[aligned(at, LANES), :] = jnp.concatenate(block, axis=0).T


def block_of(ref, row, column):
    return jnp.broadcast_to(ref[row : row + 1, aligned(column, LANES)], (8, LANES))


def field_of(place, b):
    ref, row, column = place
    return [ref[row + h * 8 : row + h * 8 + 8, aligned(column + b * LANES, LANES)] for h in range(2)]


def spread_at_donors(messages, cells, partners, weights, staged):
    for n, k in enumerate(partners):

        def step(b):
            field = field_of(messages[k], b)
            ref, row, column = weights[k]
            scale = [block_of(ref, row + m, column + b * LANES) for m in range(4)]
            fields = [[part * scale[m] for part in field] for m in range(4)]
            blocks = [block_of(cells, m, k * FRINGE + b * LANES) for m in range(4)]
            spread_group(fields, blocks, [(staged, (m * len(partners) + n) * FRINGE + b * LANES) for m in range(4)])

        each_block(4, step)


def spread_at_receptors(messages, cells, staged):
    for part in range(3):

        def step(j, carry):
            fields, blocks, outs = [], [], []
            for m in range(4):
                k, shift = divmod(m * QUARTER + part * 4 * LANES, FRINGE)
                fields.append(field_of(messages[k], j + shift // LANES))
                at = m * QUARTER + (part * 4 + j) * LANES
                blocks.append(block_of(cells, 0, at))
                outs.append((staged, at))
            spread_group(fields, blocks, outs)
            return carry

        lax.fori_loop(0, 4, step, 0, unroll=2)


def lanes(shape):
    return lax.broadcasted_iota(i32, shape, len(shape) - 1)


def fill_ends(padded, low, high):
    lane = lanes((1, LANES))
    before = pltpu.roll(padded[ROWS : ROWS + 8, :], PROBES, 1)[7:8, :]
    after = pltpu.roll(padded[8:16, :], LANES - PROBES, 1)[0:1, :]
    padded[7:8, :] = jnp.where(lane < PROBES, low, before)
    padded[ROWS + 8 : ROWS + 9, :] = jnp.where(lane >= LANES - PROBES, high, after)


def each_row_block(step):
    def outer(j, carry):
        for u in range(4):
            step(j * 32 + u * 8)
        return carry

    lax.fori_loop(0, ROWS // 32, outer, 0)


def table_kernel(probes, table, natural, sem):
    copies = [
        pltpu.make_async_copy(probes.at[p], natural.at[pl.ds(p, 1), :], sem.at[p]) for p in range(PROBES)
    ]
    for copy in copies:
        copy.start()
    finish(copies)

    def step(j, carry):
        for n in range(4):
            tile = j * 4 + n
            parts = [natural[:, aligned(g * ROWS + tile * LANES, LANES)] for g in range(GROUPS)]
            table[aligned(tile * LANES, LANES), :] = jnp.concatenate(parts, axis=0).T
        return carry

    lax.fori_loop(0, TILES // 4, step, 0)


def table_of(probes):
    return pl.pallas_call(
        table_kernel,
        out_shape=resident(ROWS, LANES),
        in_specs=[FIXED],
        out_specs=VMEM,
        scratch_shapes=[pltpu.VMEM((PROBES, GROUPS * ROWS), f32), pltpu.SemaphoreType.DMA((PROBES,))],
        compiler_params=params(60),
        cost_estimate=cost(3),
        name="table",
    )(probes)


BEFORE, SAME, AFTER = (0, 3), (1, 4), (2, 5)
SIDES = BEFORE + AFTER
NEAR, FAR = (0, 1, 2), (3, 4, 5)
EDGE = slice(FRINGE, FRINGE + LANES)


def weight_places(before, same, after):
    return {
        0: (before, 0, 0),
        3: (before, 4, 0),
        1: (same[0], 0, FRINGE),
        4: (same[1], 0, 4 * FRINGE),
        2: (after, 0, 0),
        5: (after, 4, 0),
    }


def pair_places(pair, ref):
    return {pair[0]: (ref, 0, 0), pair[1]: (ref, PROBES, 0)}


def grid_places(near, far):
    places = {k: (near, n * PROBES, 0) for n, k in enumerate(NEAR)}
    places.update({k: (far, n * PROBES, 0) for n, k in enumerate(FAR)})
    return places


def simple_call(kernel, out_shape, operands, name):
    return pl.pallas_call(
        kernel,
        out_shape=out_shape,
        in_specs=[VMEM] * len(operands),
        out_specs=[VMEM] * len(out_shape),
        compiler_params=params(8),
        cost_estimate=cost(1),
        name=name,
    )(*operands)


def weight_relay_kernel(near, far, table, up, down):
    for pair, out, rows in ((BEFORE, up, slice(ROWS - 8, ROWS)), (AFTER, down, slice(0, 8))):
        for n, ref in enumerate((near, far)):
            start = pair[n] * FRINGE
            out[n * 4 : n * 4 + 4, 0:FRINGE] = ref[:, start : start + FRINGE]
        out[:, EDGE] = table[rows, :]


def weight_relay(near, far, table):
    shape = jax.ShapeDtypeStruct((8, FRINGE + LANES), f32)
    return simple_call(weight_relay_kernel, [shape] * 2, (near, far, table), "weight_relay")


def rows_kernel(table, rows_hbm, staged, *rest):
    parts, sem = rest[:WAYS], rest[WAYS]
    gather_rows(table, parts, staged, index_copies(rows_hbm, segments(4, SIDES), parts, sem))


def rows_at_sides(table, rows):
    segs = segments(4, SIDES)
    return pl.pallas_call(
        rows_kernel,
        out_shape=resident(len(segs) * FRINGE, LANES),
        in_specs=[VMEM, HBM],
        out_specs=VMEM,
        scratch_shapes=index_scratch(segs),
        compiler_params=params(8),
        cost_estimate=cost(11),
        name="rows_at_sides",
    )(table, rows)


PAIR = jax.ShapeDtypeStruct((2 * PROBES, FRINGE), f32)
TRIPLE = jax.ShapeDtypeStruct((3 * PROBES, FRINGE), f32)


def side_sums_kernel(staged, cells, before, after, up, down):
    places = {**pair_places(AFTER, up), **pair_places(BEFORE, down)}
    select_fields(staged, cells, SIDES, weight_places(before, (None, None), after), places)


def side_sums(staged, cells, before, after):
    return simple_call(side_sums_kernel, [PAIR] * 2, (staged, cells, before, after), "side_sums")


def same_sums_kernel(table, cells, rows_hbm, near, far, out, staged, *rest):
    parts, sem = rest[:WAYS], rest[WAYS]
    gather_rows(table, parts, staged, index_copies(rows_hbm, segments(4, SAME), parts, sem))
    select_fields(staged, cells, SAME, weight_places(None, (near, far), None), pair_places(SAME, out))


def same_sums(table, cells, rows, near, far):
    segs = segments(4, SAME)
    return pl.pallas_call(
        same_sums_kernel,
        out_shape=PAIR,
        in_specs=[VMEM, VMEM, HBM, VMEM, VMEM],
        out_specs=VMEM,
        scratch_shapes=[pltpu.VMEM((len(segs) * FRINGE, LANES), f32)] + index_scratch(segs),
        compiler_params=params(8),
        cost_estimate=cost(8),
        name="same_sums",
    )(table, cells, rows, near, far)


def message_relay_kernel(before, same, after, near, far):
    for n, out in enumerate((near, far)):
        for i, ref in enumerate((before, same, after)):
            out[i * PROBES : (i + 1) * PROBES, :] = ref[n * PROBES : (n + 1) * PROBES, :]


def message_relay(before, same, after):
    return simple_call(message_relay_kernel, [TRIPLE] * 2, (before, same, after), "message_relay")


def end_flags():
    column = lax.axis_index("cell")
    return (column > 0).astype(f32), (column < lax.axis_size("cell") - 1).astype(f32)


def outer_rows(before, after):
    has_low, has_high = end_flags()
    low = pltpu.roll(before[0:8, EDGE], PROBES, 1)[7:8, :] * has_low
    high = pltpu.roll(after[0:8, EDGE], LANES - PROBES, 1)[0:1, :] * has_high
    return low, high


def forward_kernel(table, centre, lower, upper, before, after, c_out, l_out, u_out, *rest):
    sums, padded = rest[:SUMS], rest[SUMS]

    def step(j, carry):
        for n in range(2):
            tile = j * 2 + n
            at = aligned(tile * LANES, LANES)
            padded[rows_of(tile * LANES + 8, LANES), :] = table[at, :]
            for ref, out in ((centre, c_out), (lower, l_out), (upper, u_out)):
                parts = [
                    jnp.broadcast_to(ref[:, aligned(g * ROWS + tile * LANES, LANES)], (PROBES, LANES))
                    for g in range(GROUPS)
                ]
                out[at, :] = jnp.concatenate(parts, axis=0).T
        return carry

    lax.fori_loop(0, TILES // 2, step, 0)
    fill_ends(padded, *outer_rows(before, after))

    def stencil(start):
        at = rows_of(start, 8)
        sums[0][at, :] = (
            c_out[at, :] * padded[rows_of(start + 8, 8), :]
            - l_out[at, :] * padded[pl.ds(start + 7, 8), :]
            - u_out[at, :] * padded[pl.ds(start + 9, 8), :]
        )

    each_row_block(stencil)
    clear(sums[1:])


def forward(table, centre, lower, upper, before, after):
    return pl.pallas_call(
        forward_kernel,
        out_shape=[resident(ROWS, LANES)] * (3 + SUMS),
        in_specs=[VMEM] * 6,
        out_specs=[VMEM] * (3 + SUMS),
        scratch_shapes=[pltpu.VMEM((ROWS + 16, LANES), f32)],
        compiler_params=params(8),
        cost_estimate=cost(7),
        name="forward",
    )(table, centre, lower, upper, before, after)


def couple_kernel(cells, rows_hbm, near, far, *refs):
    refs = refs[SUMS:]
    tangent, out, sums = refs[0], refs[1], refs[2 : 2 + SUMS]
    staged, staged_far = refs[2 + SUMS : 4 + SUMS]
    refs = refs[4 + SUMS :]
    parts, sem, parts_far, sem_far = refs[:WAYS], refs[WAYS], refs[WAYS + 1 : 2 * WAYS + 1], refs[2 * WAYS + 1]
    every = NEAR + FAR
    phases = index_copies(rows_hbm, segments(1, every), parts, sem)
    phases_far = index_copies(rows_hbm, segments(1, FAR), parts_far, sem_far)
    spread_at_receptors(grid_places(near, far), cells, staged)
    finish(phases[0] + phases[1])
    add_rows(sums, parts, staged)

    def total(start):
        at = rows_of(start, 8)
        value = sums[0][at, :]
        for part in sums[1:]:
            value = value + part[at, :]
        tangent[at, :] = value

    each_row_block(total)
    gather_rows(tangent, parts_far, staged_far, phases_far)
    select_fields(staged_far, cells, FAR, None, grid_places(None, out))


def couple(cells, rows, near, far, sums):
    every, some = segments(1, NEAR + FAR), segments(1, FAR)
    outs = pl.pallas_call(
        couple_kernel,
        out_shape=[resident(ROWS, LANES), TRIPLE] + [resident(ROWS, LANES)] * SUMS,
        in_specs=[VMEM, HBM] + [VMEM] * (2 + SUMS),
        out_specs=[VMEM] * (2 + SUMS),
        scratch_shapes=[pltpu.VMEM((SLOTS, LANES), f32), pltpu.VMEM((SLOTS // 2, LANES), f32)]
        + index_scratch(every)
        + index_scratch(some),
        input_output_aliases={4 + w: 2 + w for w in range(SUMS)},
        compiler_params=params(8),
        cost_estimate=cost(11),
        name="couple",
    )(cells, rows, near, far, *sums)
    return outs[0], outs[1]


def receptor_kernel(tangent, cells, rows_hbm, out, staged, *rest):
    parts, sem = rest[:WAYS], rest[WAYS]
    gather_rows(tangent, parts, staged, index_copies(rows_hbm, segments(1, NEAR), parts, sem))
    select_fields(staged, cells, NEAR, None, grid_places(out, None))


def at_receptors(tangent, cells, rows):
    segs = segments(1, NEAR)
    return pl.pallas_call(
        receptor_kernel,
        out_shape=TRIPLE,
        in_specs=[VMEM, VMEM, HBM],
        out_specs=VMEM,
        scratch_shapes=[pltpu.VMEM((len(segs) * FRINGE, LANES), f32)] + index_scratch(segs),
        compiler_params=params(8),
        cost_estimate=cost(3),
        name="at_receptors",
    )(tangent, cells, rows)


def return_relay_kernel(near, far, tangent, lower, upper, ready, up, down):
    for n, ref in enumerate((near, far)):
        at = slice(n * PROBES, (n + 1) * PROBES)
        up[at, 0:FRINGE] = ref[0:PROBES, :]
        down[at, 0:FRINGE] = ref[2 * PROBES : 3 * PROBES, :]
    end = slice(ROWS - 8, ROWS)
    up[0:8, EDGE] = upper[end, :] * tangent[end, :]
    down[0:8, EDGE] = lower[0:8, :] * tangent[0:8, :]


def return_relay(near, far, tangent, lower, upper, ready):
    shape = jax.ShapeDtypeStruct((2 * PROBES, FRINGE + LANES), f32)
    return simple_call(return_relay_kernel, [shape] * 2, (near, far, tangent, lower, upper, ready), "return_relay")


def transposed_kernel(tangent, centre, lower, upper, ready, *rest):
    sums, raised, lowered = rest[:SUMS], rest[SUMS], rest[SUMS + 1]

    def products(start):
        at = rows_of(start, 8)
        value = tangent[at, :]
        raised[rows_of(start + 8, 8), :] = upper[at, :] * value
        lowered[rows_of(start + 8, 8), :] = lower[at, :] * value

    each_row_block(products)
    nothing = jnp.zeros((1, LANES), f32)
    fill_ends(raised, nothing, nothing)
    fill_ends(lowered, nothing, nothing)

    def stencil(start):
        at = rows_of(start, 8)
        sums[0][at, :] = (
            centre[at, :] * tangent[at, :] - raised[pl.ds(start + 7, 8), :] - lowered[pl.ds(start + 9, 8), :]
        )

    each_row_block(stencil)
    clear(sums[1:])


def transposed(tangent, centre, lower, upper, ready):
    return pl.pallas_call(
        transposed_kernel,
        out_shape=[resident(ROWS, LANES)] * SUMS,
        in_specs=[VMEM] * 5,
        out_specs=[VMEM] * SUMS,
        scratch_shapes=[pltpu.VMEM((ROWS + 16, LANES), f32)] * 2,
        compiler_params=params(8),
        cost_estimate=cost(1),
        name="transposed",
    )(tangent, centre, lower, upper, ready)


def donor_same_kernel(cells, rows_hbm, near_weights, far_weights, near, far, *refs):
    refs = refs[SUMS:]
    sums, staged, parts, sem = refs[:SUMS], refs[SUMS], refs[SUMS + 1 : SUMS + WAYS + 1], refs[SUMS + WAYS + 1]
    phases = index_copies(rows_hbm, segments(4, SAME), parts, sem)
    weights = weight_places(None, (near_weights, far_weights), None)
    spread_at_donors(grid_places(near, far), cells, SAME, weights, staged)
    finish(phases[0] + phases[1])
    add_rows(sums, parts, staged)


def add_same(cells, rows, near_weights, far_weights, near, far, sums):
    segs = segments(4, SAME)
    return pl.pallas_call(
        donor_same_kernel,
        out_shape=[resident(ROWS, LANES)] * SUMS,
        in_specs=[VMEM, HBM] + [VMEM] * (4 + SUMS),
        out_specs=[VMEM] * SUMS,
        scratch_shapes=[pltpu.VMEM((len(segs) * FRINGE, LANES), f32)] + index_scratch(segs),
        input_output_aliases={6 + w: w for w in range(SUMS)},
        compiler_params=params(8),
        cost_estimate=cost(9),
        name="add_same",
    )(cells, rows, near_weights, far_weights, near, far, *sums)


def sum_of_groups(value):
    for shift in (64, 32, 16):
        value = value + pltpu.roll(value, shift, 1)
    return value


def own_group():
    return lanes((8, LANES)) // PROBES == lax.broadcasted_iota(i32, (8, LANES), 0)


def donor_sides_kernel(cells, rows_hbm, before_weights, after_weights, before, after, *refs):
    refs = refs[SUMS:]
    adjoint, gram, sums, staged = refs[0], refs[1], refs[2 : 2 + SUMS], refs[2 + SUMS]
    parts, sem = refs[3 + SUMS : 3 + SUMS + WAYS], refs[3 + SUMS + WAYS]
    phases = index_copies(rows_hbm, segments(4, SIDES), parts, sem)
    weights = weight_places(before_weights, (None, None), after_weights)
    spread_at_donors({**pair_places(BEFORE, before), **pair_places(AFTER, after)}, cells, SIDES, weights, staged)
    finish(phases[0] + phases[1])
    add_rows(sums, parts, staged)
    lane = lanes((1, LANES))
    low, high = outer_rows(before, after)
    sums[0][0:1, :] = sums[0][0:1, :] - jnp.where(lane < PROBES, low, 0.0)
    end = sums[0][ROWS - 1 : ROWS, :]
    sums[0][ROWS - 1 : ROWS, :] = end - jnp.where(lane >= LANES - PROBES, high, 0.0)

    def total(start):
        at = rows_of(start, 8)
        value = sums[0][at, :]
        for part in sums[1:]:
            value = value + part[at, :]
        adjoint[at, :] = value

    each_row_block(total)

    def multiply(j, product):
        left_side, right_side = [], []
        for n in range(8):
            block = adjoint[aligned((j * 8 + n) * LANES, LANES), :]
            high, low = split(block)
            high_t, low_t = split(block.T)
            left_side += [high_t, high_t, low_t]
            right_side += [high, low, high]
        left_side = jnp.concatenate(left_side, axis=1)
        right_side = jnp.concatenate(right_side, axis=0)
        return product + jnp.dot(left_side, right_side, preferred_element_type=f32)

    product = lax.fori_loop(0, TILES // 8, multiply, jnp.zeros((LANES, LANES), f32))
    group = lanes((PROBES, LANES)) // PROBES
    folded = jnp.zeros((PROBES, LANES), f32)
    for g in range(GROUPS):
        folded = folded + jnp.where(group == g, product[g * PROBES : (g + 1) * PROBES, :], 0.0)
    folded = sum_of_groups(folded)
    for n in range(2):
        gram[n : n + 1, :] = jnp.sum(jnp.where(own_group(), folded[n * 8 : n * 8 + 8, :], 0.0), axis=0, keepdims=True)


def add_sides(cells, rows, before_weights, after_weights, before, after, sums):
    segs = segments(4, SIDES)
    outs = pl.pallas_call(
        donor_sides_kernel,
        out_shape=[resident(ROWS, LANES), jax.ShapeDtypeStruct((2, LANES), f32)]
        + [resident(ROWS, LANES)] * SUMS,
        in_specs=[VMEM, HBM] + [VMEM] * (4 + SUMS),
        out_specs=[VMEM] * (2 + SUMS),
        scratch_shapes=[pltpu.VMEM((len(segs) * FRINGE, LANES), f32)] + index_scratch(segs),
        input_output_aliases={6 + w: 2 + w for w in range(SUMS)},
        compiler_params=params(12),
        cost_estimate=cost(18),
        name="add_sides",
    )(cells, rows, before_weights, after_weights, before, after, *sums)
    return outs[0], outs[1]


def basis_kernel(total_cells, gram, adjoint, basis, factor, natural, sem):
    row = lax.broadcasted_iota(i32, (PROBES, LANES), 0)
    lane = lanes((PROBES, LANES))
    whole = jnp.concatenate(
        [sum_of_groups(jnp.where(own_group(), jnp.broadcast_to(gram[n : n + 1, :], (8, LANES)), 0.0)) for n in range(2)],
        axis=0,
    ) / f32(total_cells)
    columns = [jnp.broadcast_to(whole[:, j : j + 1], (PROBES, LANES)) for j in range(PROBES)]
    right = jnp.where(row == lane % PROBES, 1.0, 0.0)
    result = jnp.zeros((PROBES, LANES), f32)
    for j in range(PROBES):
        pivot = columns[j][j : j + 1, :]
        root = jnp.sqrt(pivot)
        ratio = jnp.where(row > j, columns[j] / pivot, 0.0)
        result = jnp.where((lane == j) & (row >= j), columns[j] / root, result)
        right_row = right[j : j + 1, :]
        right = jnp.where(row == j, right_row / root, right - ratio * right_row)
        for n in range(j + 1, PROBES):
            columns[n] = columns[n] - ratio * columns[n][j : j + 1, :]
    factor[...] = result[:, :PROBES]
    inverse = jnp.concatenate([right] * GROUPS, axis=0)
    same = lax.broadcasted_iota(i32, (LANES, LANES), 0) // PROBES == lanes((LANES, LANES)) // PROBES
    high, low = split(jnp.where(same, inverse, 0.0))
    left_side = jnp.concatenate([high, high, low], axis=1)

    def step(j, carry):
        for n in range(4):
            tile = j * 4 + n
            high, low = split(adjoint[aligned(tile * LANES, LANES), :])
            right_side = jnp.concatenate([high, low, high], axis=1)
            block = lax.dot_general(left_side, right_side, (((1,), (1,)), ((), ())), preferred_element_type=f32)
            for g in range(GROUPS):
                natural[:, aligned(g * ROWS + tile * LANES, LANES)] = block[g * PROBES : (g + 1) * PROBES, :]
        return carry

    copies = []
    for quarter in range(4):
        lax.fori_loop(quarter * TILES // 16, (quarter + 1) * TILES // 16, step, 0)
        for g in range(GROUPS):
            at = pl.ds(g * ROWS + quarter * ROWS // 4, ROWS // 4)
            copies.append(pltpu.make_async_copy(natural.at[:, at], basis.at[:, 0, at], sem.at[len(copies)]))
            copies[-1].start()
    finish(copies)


def basis_of(total_cells, gram, adjoint):
    return pl.pallas_call(
        functools.partial(basis_kernel, total_cells),
        out_shape=[
            jax.ShapeDtypeStruct((PROBES, 1, GROUPS * ROWS), f32),
            jax.ShapeDtypeStruct((PROBES, PROBES), f32),
        ],
        in_specs=[VMEM] * 2,
        out_specs=[FIXED, VMEM],
        scratch_shapes=[pltpu.VMEM((PROBES, GROUPS * ROWS), f32), pltpu.SemaphoreType.DMA((4 * GROUPS,))],
        compiler_params=params(8),
        cost_estimate=cost(6),
        name="basis",
    )(gram, adjoint)


def moved(value, place):
    grids, columns = (lax.axis_size(axis) for axis in AXES)
    route = []
    for g in range(grids):
        for c in range(columns):
            to_g, to_c = place(g, c)
            route.append((g * columns + c, (to_g % grids) * columns + to_c % columns))
    return lax.ppermute(value, AXES, route)


def along_grid(value, distance):
    return moved(value, lambda g, c: (g + distance, c))


def along_cell(value, distance):
    return moved(value, lambda g, c: (g, c + distance))


def axis_sum(value, axis):
    copies = jnp.broadcast_to(value, (lax.axis_size(axis),) + value.shape)
    return jnp.sum(lax.all_to_all(copies, axis, 0, 0), axis=0)


def body(probes, centre, lower_coef, upper_coef, donor_cells, receptor_cells, weights):
    donors = donor_cells[0]
    donor_rows = (donors & (ROWS - 1)).reshape(-1)
    receptor_rows = (receptor_cells & (ROWS - 1)).reshape(-1)
    near_weights, far_weights = along_grid(weights, -1)[0], along_grid(weights, -2)[0]
    table = table_of(probes)
    up, down = weight_relay(near_weights, far_weights, table)
    before_weights, after_weights = along_cell(up, 1), along_cell(down, -1)
    staged = rows_at_sides(table, donor_rows)
    up, down = side_sums(staged, donors, before_weights, after_weights)
    after, before = along_cell(up, 1), along_cell(down, -1)
    same = same_sums(table, donors, donor_rows, near_weights, far_weights)
    near, far = message_relay(before, same, after)
    near, far = along_grid(near, 1), along_grid(far, 2)
    c, l, u, *sums = forward(table, centre, lower_coef, upper_coef, before_weights, after_weights)
    tangent, far = couple(receptor_cells, receptor_rows, near, far, sums)
    far = along_grid(far, -2)
    near = along_grid(at_receptors(tangent, receptor_cells, receptor_rows), -1)
    sums = transposed(tangent, c, l, u, far)
    up, down = return_relay(near, far, tangent, l, u, sums[-1])
    before, after = along_cell(up, 1), along_cell(down, -1)
    sums = add_same(donors, donor_rows, near_weights, far_weights, near, far, sums)
    adjoint, gram = add_sides(donors, donor_rows, before_weights, after_weights, before, after, sums)
    total_cells = lax.axis_size("grid") * lax.axis_size("cell") * probes.shape[2]
    basis, factor = basis_of(total_cells, axis_sum(axis_sum(gram, "grid"), "cell"), adjoint)
    return (basis, factor)


def solution(mesh):
    in_specs = (
        P(None, "grid", "cell"),
        P("grid", "cell"),
        P("grid", "cell"),
        P("grid", "cell"),
        P("grid", None, "cell"),
        P("grid", "cell"),
        P("grid", None, "cell"),
    )
    out_specs = (P(None, "grid", "cell"), P())
    return jax.shard_map(body, mesh=mesh, in_specs=in_specs, out_specs=out_specs, check_vma=False)
```

```python
import functools

import jax
import jax.numpy as jnp
from jax import lax
from jax.experimental import pallas as pl
from jax.experimental.pallas import tpu as pltpu
from jax.sharding import PartitionSpec as P

f32 = jnp.float32
i32 = jnp.int32
bf16 = jnp.bfloat16

PROBES = 16
GROUPS = 8
ROWS = 4096
LANES = 128
PARTNERS = 6
FRINGE = 1024
HALF = 3 * FRINGE
SLOTS = PARTNERS * FRINGE
TILES = ROWS // LANES
WAYS = 8
SUMS = 4
QUARTER = SLOTS // 4
UNROLL = 16
ADD_UNROLL = 32

AXES = ("grid", "cell")

VMEM = pl.BlockSpec(memory_space=pltpu.VMEM)
HBM = pl.BlockSpec(memory_space=pl.ANY)
FIXED = pl.BlockSpec(memory_space=pltpu.HBM)


def aligned(start, size):
    return pl.ds(pl.multiple_of(start, size), size)


def rows_of(start, size):
    return pl.ds(pl.multiple_of(start, 8), size)


def split(x):
    high = x.astype(bf16)
    return high, (x - high.astype(f32)).astype(bf16)


def params(limit_mib):
    return pltpu.CompilerParams(vmem_limit_bytes=limit_mib << 20)


def cost(microseconds):
    return pl.CostEstimate(flops=0, transcendentals=0, bytes_accessed=microseconds * 3_000_000)


def resident(*shape):
    return pltpu.VMEM(shape, f32)


HEAD = 128


def segments(many, partners):
    return [(m, k) for m in range(many) for k in partners]


def index_scratch(segs):
    size = len(segs) * FRINGE // WAYS
    return [pltpu.SMEM((size,), i32)] * WAYS + [pltpu.SemaphoreType.DMA((3 * WAYS,))]


def index_copies(rows_hbm, segs, parts, sem):
    size = parts[0].shape[0]
    cuts = sorted({0, HEAD, size} | set(range(0, size, FRINGE)))
    phases = [[], []]
    for c in range(len(cuts) - 1):
        low, high = cuts[c], cuts[c + 1]
        for w in range(WAYS):
            seg, offset = divmod(w * size + low, FRINGE)
            start = segs[seg][0] * SLOTS + segs[seg][1] * FRINGE + offset
            copy = pltpu.make_async_copy(
                rows_hbm.at[pl.ds(start, high - low)], parts[w].at[pl.ds(low, high - low)], sem.at[c * WAYS + w]
            )
            copy.start()
            phases[min(c, 1)].append(copy)
    return phases


def finish(copies):
    for copy in copies:
        copy.wait()


def row_steps(parts, low, high, step):
    def outer(j, carry):
        for n in range(UNROLL):
            q = low + j * UNROLL + n
            for w in range(WAYS):
                step(w, q, parts[w][q])
        return carry

    lax.fori_loop(0, (high - low) // UNROLL, outer, 0)


def gather_rows(table, parts, staged, phases):
    count = parts[0].shape[0]

    def step(w, q, row):
        staged[pl.ds(w * count + q, 1), :] = table[pl.ds(row, 1), :]

    finish(phases[0])
    row_steps(parts, 0, HEAD, step)
    finish(phases[1])
    row_steps(parts, HEAD, count, step)


def clear(sums):
    def step(j, carry):
        for total in sums:
            for n in range(4):
                total[rows_of(j * 32 + n * 8, 8), :] = jnp.zeros((8, LANES), f32)
        return carry

    lax.fori_loop(0, ROWS // 32, step, 0)


def add_rows(sums, parts, staged):
    count = parts[0].shape[0]

    def outer(j, carry):
        for n in range(ADD_UNROLL):
            q = j * ADD_UNROLL + n
            for half in range(2):
                total = sums[half + n % 2 * 2]
                lists = [2 * m + half for m in range(4)]
                rows = [parts[w][q] for w in lists]
                old = [total[pl.ds(row, 1), :] for row in rows]
                new = [value + staged[pl.ds(w * count + q, 1), :] for value, w in zip(old, lists)]
                for row, value in zip(rows, new):
                    total[pl.ds(row, 1), :] = value
        return carry

    lax.fori_loop(0, count // ADD_UNROLL, outer, 0)


def groups_of(cells, m, offset):
    return jnp.broadcast_to(cells[m : m + 1, aligned(offset, LANES)], (8, LANES)) >> 12


def each_block(many, step):
    unroll = 8 // many

    def outer(j, carry):
        for n in range(unroll):
            step(j * unroll + n)
        return carry

    lax.fori_loop(0, FRINGE // LANES // unroll, outer, 0)


def select_fields(staged, cells, partners, weights, out):
    many = cells.shape[0]
    for n, k in enumerate(partners):

        def step(b):
            total = [jnp.zeros((8, LANES), f32)] * 2
            for m in range(many):
                field = staged[aligned((m * len(partners) + n) * FRINGE + b * LANES, LANES), :].T
                group = groups_of(cells, m, k * FRINGE + b * LANES)
                scale = 1.0
                if weights is not None:
                    ref, row, column = weights[k]
                    scale = ref[row + m : row + m + 1, aligned(column + b * LANES, LANES)]
                    scale = jnp.broadcast_to(scale, (8, LANES))
                for g in range(GROUPS):
                    factor = jnp.where(group == g, scale, 0.0)
                    for h in range(2):
                        at = g * PROBES + h * 8
                        total[h] = total[h] + field[at : at + 8, :] * factor
            ref, row, column = out[k]
            for h in range(2):
                ref[row + h * 8 : row + h * 8 + 8, aligned(column + b * LANES, LANES)] = total[h]

        each_block(many, step)


def spread_group(fields, cells, outs):
    group = [value >> 12 for value in cells]
    row = [value & (ROWS - 1) for value in cells]
    terms = [[jnp.where(group[m] == g, fields[m][h], 0.0) for g in range(GROUPS) for h in range(2)] for m in range(4)]
    for m in range(4):
        same = [row[m] == row[i] for i in range(m)]
        block = []
        for v in range(2 * GROUPS):
            value = terms[m][v]
            for i in range(m):
                value = value + jnp.where(same[i], terms[i][v], 0.0)
            block.append(value)
        ref, at = outs[m]
        ref[aligned(at, LANES), :] = jnp.concatenate(block, axis=0).T


def block_of(ref, row, column):
    return jnp.broadcast_to(ref[row : row + 1, aligned(column, LANES)], (8, LANES))


def field_of(place, b):
    ref, row, column = place
    return [ref[row + h * 8 : row + h * 8 + 8, aligned(column + b * LANES, LANES)] for h in range(2)]


def spread_at_donors(messages, cells, partners, weights, staged):
    for n, k in enumerate(partners):

        def step(b):
            field = field_of(messages[k], b)
            ref, row, column = weights[k]
            scale = [block_of(ref, row + m, column + b * LANES) for m in range(4)]
            fields = [[part * scale[m] for part in field] for m in range(4)]
            blocks = [block_of(cells, m, k * FRINGE + b * LANES) for m in range(4)]
            spread_group(fields, blocks, [(staged, (m * len(partners) + n) * FRINGE + b * LANES) for m in range(4)])

        each_block(4, step)


def spread_at_receptors(messages, cells, staged):
    for part in range(3):

        def step(j, carry):
            fields, blocks, outs = [], [], []
            for m in range(4):
                k, shift = divmod(m * QUARTER + part * 4 * LANES, FRINGE)
                fields.append(field_of(messages[k], j + shift // LANES))
                at = m * QUARTER + (part * 4 + j) * LANES
                blocks.append(block_of(cells, 0, at))
                outs.append((staged, at))
            spread_group(fields, blocks, outs)
            return carry

        lax.fori_loop(0, 4, step, 0, unroll=2)


def lanes(shape):
    return lax.broadcasted_iota(i32, shape, len(shape) - 1)


def fill_ends(padded, low, high):
    lane = lanes((1, LANES))
    before = pltpu.roll(padded[ROWS : ROWS + 8, :], PROBES, 1)[7:8, :]
    after = pltpu.roll(padded[8:16, :], LANES - PROBES, 1)[0:1, :]
    padded[7:8, :] = jnp.where(lane < PROBES, low, before)
    padded[ROWS + 8 : ROWS + 9, :] = jnp.where(lane >= LANES - PROBES, high, after)


def each_row_block(step):
    def outer(j, carry):
        for u in range(4):
            step(j * 32 + u * 8)
        return carry

    lax.fori_loop(0, ROWS // 32, outer, 0)


def table_kernel(probes, table, natural, sem):
    copies = [
        pltpu.make_async_copy(probes.at[p], natural.at[pl.ds(p, 1), :], sem.at[p]) for p in range(PROBES)
    ]
    for copy in copies:
        copy.start()
    finish(copies)

    def step(j, carry):
        for n in range(4):
            tile = j * 4 + n
            parts = [natural[:, aligned(g * ROWS + tile * LANES, LANES)] for g in range(GROUPS)]
            table[aligned(tile * LANES, LANES), :] = jnp.concatenate(parts, axis=0).T
        return carry

    lax.fori_loop(0, TILES // 4, step, 0)


def table_of(probes):
    return pl.pallas_call(
        table_kernel,
        out_shape=resident(ROWS, LANES),
        in_specs=[FIXED],
        out_specs=VMEM,
        scratch_shapes=[pltpu.VMEM((PROBES, GROUPS * ROWS), f32), pltpu.SemaphoreType.DMA((PROBES,))],
        compiler_params=params(60),
        cost_estimate=cost(3),
        name="table",
    )(probes)


BEFORE, SAME, AFTER = (0, 3), (1, 4), (2, 5)
SIDES = BEFORE + AFTER
NEAR, FAR = (0, 1, 2), (3, 4, 5)
EDGE = slice(FRINGE, FRINGE + LANES)


def weight_places(before, same, after):
    return {
        0: (before, 0, 0),
        3: (before, 4, 0),
        1: (same[0], 0, FRINGE),
        4: (same[1], 0, 4 * FRINGE),
        2: (after, 0, 0),
        5: (after, 4, 0),
    }


def pair_places(pair, ref):
    return {pair[0]: (ref, 0, 0), pair[1]: (ref, PROBES, 0)}


def grid_places(near, far):
    places = {k: (near, n * PROBES, 0) for n, k in enumerate(NEAR)}
    places.update({k: (far, n * PROBES, 0) for n, k in enumerate(FAR)})
    return places


def simple_call(kernel, out_shape, operands, name):
    return pl.pallas_call(
        kernel,
        out_shape=out_shape,
        in_specs=[VMEM] * len(operands),
        out_specs=[VMEM] * len(out_shape),
        compiler_params=params(8),
        cost_estimate=cost(1),
        name=name,
    )(*operands)


def weight_relay_kernel(near, far, table, up, down):
    for pair, out, rows in ((BEFORE, up, slice(ROWS - 8, ROWS)), (AFTER, down, slice(0, 8))):
        for n, ref in enumerate((near, far)):
            start = pair[n] * FRINGE
            out[n * 4 : n * 4 + 4, 0:FRINGE] = ref[:, start : start + FRINGE]
        out[:, EDGE] = table[rows, :]


def weight_relay(near, far, table):
    shape = jax.ShapeDtypeStruct((8, FRINGE + LANES), f32)
    return simple_call(weight_relay_kernel, [shape] * 2, (near, far, table), "weight_relay")


def rows_kernel(table, rows_hbm, staged, *rest):
    parts, sem = rest[:WAYS], rest[WAYS]
    gather_rows(table, parts, staged, index_copies(rows_hbm, segments(4, SIDES), parts, sem))


def rows_at_sides(table, rows):
    segs = segments(4, SIDES)
    return pl.pallas_call(
        rows_kernel,
        out_shape=resident(len(segs) * FRINGE, LANES),
        in_specs=[VMEM, HBM],
        out_specs=VMEM,
        scratch_shapes=index_scratch(segs),
        compiler_params=params(8),
        cost_estimate=cost(11),
        name="rows_at_sides",
    )(table, rows)


PAIR = jax.ShapeDtypeStruct((2 * PROBES, FRINGE), f32)
TRIPLE = jax.ShapeDtypeStruct((3 * PROBES, FRINGE), f32)


def side_sums_kernel(staged, cells, before, after, up, down):
    places = {**pair_places(AFTER, up), **pair_places(BEFORE, down)}
    select_fields(staged, cells, SIDES, weight_places(before, (None, None), after), places)


def side_sums(staged, cells, before, after):
    return simple_call(side_sums_kernel, [PAIR] * 2, (staged, cells, before, after), "side_sums")


def same_sums_kernel(table, cells, rows_hbm, near, far, out, staged, *rest):
    parts, sem = rest[:WAYS], rest[WAYS]
    gather_rows(table, parts, staged, index_copies(rows_hbm, segments(4, SAME), parts, sem))
    select_fields(staged, cells, SAME, weight_places(None, (near, far), None), pair_places(SAME, out))


def same_sums(table, cells, rows, near, far):
    segs = segments(4, SAME)
    return pl.pallas_call(
        same_sums_kernel,
        out_shape=PAIR,
        in_specs=[VMEM, VMEM, HBM, VMEM, VMEM],
        out_specs=VMEM,
        scratch_shapes=[pltpu.VMEM((len(segs) * FRINGE, LANES), f32)] + index_scratch(segs),
        compiler_params=params(8),
        cost_estimate=cost(8),
        name="same_sums",
    )(table, cells, rows, near, far)


def message_relay_kernel(before, same, after, near, far):
    for n, out in enumerate((near, far)):
        for i, ref in enumerate((before, same, after)):
            out[i * PROBES : (i + 1) * PROBES, :] = ref[n * PROBES : (n + 1) * PROBES, :]


def message_relay(before, same, after):
    return simple_call(message_relay_kernel, [TRIPLE] * 2, (before, same, after), "message_relay")


def end_flags():
    column = lax.axis_index("cell")
    return (column > 0).astype(f32), (column < lax.axis_size("cell") - 1).astype(f32)


def outer_rows(before, after):
    has_low, has_high = end_flags()
    low = pltpu.roll(before[0:8, EDGE], PROBES, 1)[7:8, :] * has_low
    high = pltpu.roll(after[0:8, EDGE], LANES - PROBES, 1)[0:1, :] * has_high
    return low, high


def forward_kernel(table, centre, lower, upper, before, after, c_out, l_out, u_out, *rest):
    sums, padded = rest[:SUMS], rest[SUMS]

    def step(j, carry):
        for n in range(2):
            tile = j * 2 + n
            at = aligned(tile * LANES, LANES)
            padded[rows_of(tile * LANES + 8, LANES), :] = table[at, :]
            for ref, out in ((centre, c_out), (lower, l_out), (upper, u_out)):
                parts = [
                    jnp.broadcast_to(ref[:, aligned(g * ROWS + tile * LANES, LANES)], (PROBES, LANES))
                    for g in range(GROUPS)
                ]
                out[at, :] = jnp.concatenate(parts, axis=0).T
        return carry

    lax.fori_loop(0, TILES // 2, step, 0)
    fill_ends(padded, *outer_rows(before, after))

    def stencil(start):
        at = rows_of(start, 8)
        sums[0][at, :] = (
            c_out[at, :] * padded[rows_of(start + 8, 8), :]
            - l_out[at, :] * padded[pl.ds(start + 7, 8), :]
            - u_out[at, :] * padded[pl.ds(start + 9, 8), :]
        )

    each_row_block(stencil)
    clear(sums[1:])


def forward(table, centre, lower, upper, before, after):
    return pl.pallas_call(
        forward_kernel,
        out_shape=[resident(ROWS, LANES)] * (3 + SUMS),
        in_specs=[VMEM] * 6,
        out_specs=[VMEM] * (3 + SUMS),
        scratch_shapes=[pltpu.VMEM((ROWS + 16, LANES), f32)],
        compiler_params=params(8),
        cost_estimate=cost(7),
        name="forward",
    )(table, centre, lower, upper, before, after)


def couple_kernel(cells, rows_hbm, near, far, *refs):
    refs = refs[SUMS:]
    tangent, out, sums = refs[0], refs[1], refs[2 : 2 + SUMS]
    staged, staged_far = refs[2 + SUMS : 4 + SUMS]
    refs = refs[4 + SUMS :]
    parts, sem, parts_far, sem_far = refs[:WAYS], refs[WAYS], refs[WAYS + 1 : 2 * WAYS + 1], refs[2 * WAYS + 1]
    every = NEAR + FAR
    phases = index_copies(rows_hbm, segments(1, every), parts, sem)
    phases_far = index_copies(rows_hbm, segments(1, FAR), parts_far, sem_far)
    spread_at_receptors(grid_places(near, far), cells, staged)
    finish(phases[0] + phases[1])
    add_rows(sums, parts, staged)

    def total(start):
        at = rows_of(start, 8)
        value = sums[0][at, :]
        for part in sums[1:]:
            value = value + part[at, :]
        tangent[at, :] = value

    each_row_block(total)
    gather_rows(tangent, parts_far, staged_far, phases_far)
    select_fields(staged_far, cells, FAR, None, grid_places(None, out))


def couple(cells, rows, near, far, sums):
    every, some = segments(1, NEAR + FAR), segments(1, FAR)
    outs = pl.pallas_call(
        couple_kernel,
        out_shape=[resident(ROWS, LANES), TRIPLE] + [resident(ROWS, LANES)] * SUMS,
        in_specs=[VMEM, HBM] + [VMEM] * (2 + SUMS),
        out_specs=[VMEM] * (2 + SUMS),
        scratch_shapes=[pltpu.VMEM((SLOTS, LANES), f32), pltpu.VMEM((SLOTS // 2, LANES), f32)]
        + index_scratch(every)
        + index_scratch(some),
        input_output_aliases={4 + w: 2 + w for w in range(SUMS)},
        compiler_params=params(8),
        cost_estimate=cost(11),
        name="couple",
    )(cells, rows, near, far, *sums)
    return outs[0], outs[1]


def receptor_kernel(tangent, cells, rows_hbm, out, staged, *rest):
    parts, sem = rest[:WAYS], rest[WAYS]
    gather_rows(tangent, parts, staged, index_copies(rows_hbm, segments(1, NEAR), parts, sem))
    select_fields(staged, cells, NEAR, None, grid_places(out, None))


def at_receptors(tangent, cells, rows):
    segs = segments(1, NEAR)
    return pl.pallas_call(
        receptor_kernel,
        out_shape=TRIPLE,
        in_specs=[VMEM, VMEM, HBM],
        out_specs=VMEM,
        scratch_shapes=[pltpu.VMEM((len(segs) * FRINGE, LANES), f32)] + index_scratch(segs),
        compiler_params=params(8),
        cost_estimate=cost(3),
        name="at_receptors",
    )(tangent, cells, rows)


def return_relay_kernel(near, far, tangent, lower, upper, ready, up, down):
    for n, ref in enumerate((near, far)):
        at = slice(n * PROBES, (n + 1) * PROBES)
        up[at, 0:FRINGE] = ref[0:PROBES, :]
        down[at, 0:FRINGE] = ref[2 * PROBES : 3 * PROBES, :]
    end = slice(ROWS - 8, ROWS)
    up[0:8, EDGE] = upper[end, :] * tangent[end, :]
    down[0:8, EDGE] = lower[0:8, :] * tangent[0:8, :]


def return_relay(near, far, tangent, lower, upper, ready):
    shape = jax.ShapeDtypeStruct((2 * PROBES, FRINGE + LANES), f32)
    return simple_call(return_relay_kernel, [shape] * 2, (near, far, tangent, lower, upper, ready), "return_relay")


def transposed_kernel(tangent, centre, lower, upper, ready, *rest):
    sums, raised, lowered = rest[:SUMS], rest[SUMS], rest[SUMS + 1]

    def products(start):
        at = rows_of(start, 8)
        value = tangent[at, :]
        raised[rows_of(start + 8, 8), :] = upper[at, :] * value
        lowered[rows_of(start + 8, 8), :] = lower[at, :] * value

    each_row_block(products)
    nothing = jnp.zeros((1, LANES), f32)
    fill_ends(raised, nothing, nothing)
    fill_ends(lowered, nothing, nothing)

    def stencil(start):
        at = rows_of(start, 8)
        sums[0][at, :] = (
            centre[at, :] * tangent[at, :] - raised[pl.ds(start + 7, 8), :] - lowered[pl.ds(start + 9, 8), :]
        )

    each_row_block(stencil)
    clear(sums[1:])


def transposed(tangent, centre, lower, upper, ready):
    return pl.pallas_call(
        transposed_kernel,
        out_shape=[resident(ROWS, LANES)] * SUMS,
        in_specs=[VMEM] * 5,
        out_specs=[VMEM] * SUMS,
        scratch_shapes=[pltpu.VMEM((ROWS + 16, LANES), f32)] * 2,
        compiler_params=params(8),
        cost_estimate=cost(1),
        name="transposed",
    )(tangent, centre, lower, upper, ready)


def donor_same_kernel(cells, rows_hbm, near_weights, far_weights, near, far, *refs):
    refs = refs[SUMS:]
    sums, staged, parts, sem = refs[:SUMS], refs[SUMS], refs[SUMS + 1 : SUMS + WAYS + 1], refs[SUMS + WAYS + 1]
    phases = index_copies(rows_hbm, segments(4, SAME), parts, sem)
    weights = weight_places(None, (near_weights, far_weights), None)
    spread_at_donors(grid_places(near, far), cells, SAME, weights, staged)
    finish(phases[0] + phases[1])
    add_rows(sums, parts, staged)


def add_same(cells, rows, near_weights, far_weights, near, far, sums):
    segs = segments(4, SAME)
    return pl.pallas_call(
        donor_same_kernel,
        out_shape=[resident(ROWS, LANES)] * SUMS,
        in_specs=[VMEM, HBM] + [VMEM] * (4 + SUMS),
        out_specs=[VMEM] * SUMS,
        scratch_shapes=[pltpu.VMEM((len(segs) * FRINGE, LANES), f32)] + index_scratch(segs),
        input_output_aliases={6 + w: w for w in range(SUMS)},
        compiler_params=params(8),
        cost_estimate=cost(9),
        name="add_same",
    )(cells, rows, near_weights, far_weights, near, far, *sums)


def sum_of_groups(value):
    for shift in (64, 32, 16):
        value = value + pltpu.roll(value, shift, 1)
    return value


def own_group():
    return lanes((8, LANES)) // PROBES == lax.broadcasted_iota(i32, (8, LANES), 0)


def donor_sides_kernel(cells, rows_hbm, before_weights, after_weights, before, after, *refs):
    refs = refs[SUMS:]
    adjoint, gram, sums, staged = refs[0], refs[1], refs[2 : 2 + SUMS], refs[2 + SUMS]
    parts, sem = refs[3 + SUMS : 3 + SUMS + WAYS], refs[3 + SUMS + WAYS]
    phases = index_copies(rows_hbm, segments(4, SIDES), parts, sem)
    weights = weight_places(before_weights, (None, None), after_weights)
    spread_at_donors({**pair_places(BEFORE, before), **pair_places(AFTER, after)}, cells, SIDES, weights, staged)
    finish(phases[0] + phases[1])
    add_rows(sums, parts, staged)
    lane = lanes((1, LANES))
    low, high = outer_rows(before, after)
    sums[0][0:1, :] = sums[0][0:1, :] - jnp.where(lane < PROBES, low, 0.0)
    end = sums[0][ROWS - 1 : ROWS, :]
    sums[0][ROWS - 1 : ROWS, :] = end - jnp.where(lane >= LANES - PROBES, high, 0.0)

    def total(start):
        at = rows_of(start, 8)
        value = sums[0][at, :]
        for part in sums[1:]:
            value = value + part[at, :]
        adjoint[at, :] = value

    each_row_block(total)

    def multiply(j, product):
        left_side, right_side = [], []
        for n in range(8):
            block = adjoint[aligned((j * 8 + n) * LANES, LANES), :]
            high, low = split(block)
            high_t, low_t = split(block.T)
            left_side += [high_t, high_t, low_t]
            right_side += [high, low, high]
        left_side = jnp.concatenate(left_side, axis=1)
        right_side = jnp.concatenate(right_side, axis=0)
        return product + jnp.dot(left_side, right_side, preferred_element_type=f32)

    product = lax.fori_loop(0, TILES // 8, multiply, jnp.zeros((LANES, LANES), f32))
    group = lanes((PROBES, LANES)) // PROBES
    folded = jnp.zeros((PROBES, LANES), f32)
    for g in range(GROUPS):
        folded = folded + jnp.where(group == g, product[g * PROBES : (g + 1) * PROBES, :], 0.0)
    folded = sum_of_groups(folded)
    for n in range(2):
        gram[:, n * LANES : (n + 1) * LANES] = jnp.sum(jnp.where(own_group(), folded[n * 8 : n * 8 + 8, :], 0.0), axis=0, keepdims=True)


def add_sides(cells, rows, before_weights, after_weights, before, after, sums):
    segs = segments(4, SIDES)
    outs = pl.pallas_call(
        donor_sides_kernel,
        out_shape=[resident(ROWS, LANES), jax.ShapeDtypeStruct((1, 2 * LANES), f32)]
        + [resident(ROWS, LANES)] * SUMS,
        in_specs=[VMEM, HBM] + [VMEM] * (4 + SUMS),
        out_specs=[VMEM] * (2 + SUMS),
        scratch_shapes=[pltpu.VMEM((len(segs) * FRINGE, LANES), f32)] + index_scratch(segs),
        input_output_aliases={6 + w: 2 + w for w in range(SUMS)},
        compiler_params=params(12),
        cost_estimate=cost(18),
        name="add_sides",
    )(cells, rows, before_weights, after_weights, before, after, *sums)
    return outs[0], outs[1]


def basis_kernel(total_cells, gram, adjoint, basis, factor, natural, sem):
    row = lax.broadcasted_iota(i32, (PROBES, LANES), 0)
    lane = lanes((PROBES, LANES))
    whole = jnp.concatenate(
        [sum_of_groups(jnp.where(own_group(), jnp.broadcast_to(gram[:, n * LANES : (n + 1) * LANES], (8, LANES)), 0.0)) for n in range(2)],
        axis=0,
    ) / f32(total_cells)
    columns = [jnp.broadcast_to(whole[:, j : j + 1], (PROBES, LANES)) for j in range(PROBES)]
    right = jnp.where(row == lane % PROBES, 1.0, 0.0)
    result = jnp.zeros((PROBES, LANES), f32)
    for j in range(PROBES):
        pivot = columns[j][j : j + 1, :]
        root = jnp.sqrt(pivot)
        ratio = jnp.where(row > j, columns[j] / pivot, 0.0)
        result = jnp.where((lane == j) & (row >= j), columns[j] / root, result)
        right_row = right[j : j + 1, :]
        right = jnp.where(row == j, right_row / root, right - ratio * right_row)
        for n in range(j + 1, PROBES):
            columns[n] = columns[n] - ratio * columns[n][j : j + 1, :]
    factor[...] = result[:, :PROBES]
    inverse = jnp.concatenate([right] * GROUPS, axis=0)
    same = lax.broadcasted_iota(i32, (LANES, LANES), 0) // PROBES == lanes((LANES, LANES)) // PROBES
    high, low = split(jnp.where(same, inverse, 0.0))
    left_side = jnp.concatenate([high, high, low], axis=1)

    def step(j, carry):
        for n in range(4):
            tile = j * 4 + n
            high, low = split(adjoint[aligned(tile * LANES, LANES), :])
            right_side = jnp.concatenate([high, low, high], axis=1)
            block = lax.dot_general(left_side, right_side, (((1,), (1,)), ((), ())), preferred_element_type=f32)
            for g in range(GROUPS):
                natural[:, aligned(g * ROWS + tile * LANES, LANES)] = block[g * PROBES : (g + 1) * PROBES, :]
        return carry

    copies = []
    for quarter in range(4):
        lax.fori_loop(quarter * TILES // 16, (quarter + 1) * TILES // 16, step, 0)
        for g in range(GROUPS):
            at = pl.ds(g * ROWS + quarter * ROWS // 4, ROWS // 4)
            copies.append(pltpu.make_async_copy(natural.at[:, at], basis.at[:, 0, at], sem.at[len(copies)]))
            copies[-1].start()
    finish(copies)


def basis_of(total_cells, gram, adjoint):
    return pl.pallas_call(
        functools.partial(basis_kernel, total_cells),
        out_shape=[
            jax.ShapeDtypeStruct((PROBES, 1, GROUPS * ROWS), f32),
            jax.ShapeDtypeStruct((PROBES, PROBES), f32),
        ],
        in_specs=[VMEM] * 2,
        out_specs=[FIXED, VMEM],
        scratch_shapes=[pltpu.VMEM((PROBES, GROUPS * ROWS), f32), pltpu.SemaphoreType.DMA((4 * GROUPS,))],
        compiler_params=params(8),
        cost_estimate=cost(6),
        name="basis",
    )(gram, adjoint)


def moved(value, place):
    grids, columns = (lax.axis_size(axis) for axis in AXES)
    route = []
    for g in range(grids):
        for c in range(columns):
            to_g, to_c = place(g, c)
            route.append((g * columns + c, (to_g % grids) * columns + to_c % columns))
    return lax.ppermute(value, AXES, route)


def along_grid(value, distance):
    return moved(value, lambda g, c: (g + distance, c))


def along_cell(value, distance):
    return moved(value, lambda g, c: (g, c + distance))


def summed(value):
    devices = lax.axis_size(AXES)
    copies = jnp.broadcast_to(value, (devices,) + value.shape)
    return jnp.sum(lax.all_to_all(copies, AXES, 0, 0), axis=0)


def body(probes, centre, lower_coef, upper_coef, donor_cells, receptor_cells, weights):
    donors = donor_cells[0]
    donor_rows = (donors & (ROWS - 1)).reshape(-1)
    receptor_rows = (receptor_cells & (ROWS - 1)).reshape(-1)
    near_weights, far_weights = along_grid(weights, -1)[0], along_grid(weights, -2)[0]
    table = table_of(probes)
    up, down = weight_relay(near_weights, far_weights, table)
    before_weights, after_weights = along_cell(up, 1), along_cell(down, -1)
    staged = rows_at_sides(table, donor_rows)
    up, down = side_sums(staged, donors, before_weights, after_weights)
    after, before = along_cell(up, 1), along_cell(down, -1)
    same = same_sums(table, donors, donor_rows, near_weights, far_weights)
    near, far = message_relay(before, same, after)
    near, far = along_grid(near, 1), along_grid(far, 2)
    c, l, u, *sums = forward(table, centre, lower_coef, upper_coef, before_weights, after_weights)
    tangent, far = couple(receptor_cells, receptor_rows, near, far, sums)
    far = along_grid(far, -2)
    near = along_grid(at_receptors(tangent, receptor_cells, receptor_rows), -1)
    sums = transposed(tangent, c, l, u, far)
    up, down = return_relay(near, far, tangent, l, u, sums[-1])
    before, after = along_cell(up, 1), along_cell(down, -1)
    sums = add_same(donors, donor_rows, near_weights, far_weights, near, far, sums)
    adjoint, gram = add_sides(donors, donor_rows, before_weights, after_weights, before, after, sums)
    total_cells = lax.axis_size("grid") * lax.axis_size("cell") * probes.shape[2]
    basis, factor = basis_of(total_cells, summed(gram), adjoint)
    return (basis, factor)


def solution(mesh):
    in_specs = (
        P(None, "grid", "cell"),
        P("grid", "cell"),
        P("grid", "cell"),
        P("grid", "cell"),
        P("grid", None, "cell"),
        P("grid", "cell"),
        P("grid", None, "cell"),
    )
    out_specs = (P(None, "grid", "cell"), P())
    return jax.shard_map(body, mesh=mesh, in_specs=in_specs, out_specs=out_specs, check_vma=False)
```

```python
import functools

import jax
import jax.numpy as jnp
from jax import lax
from jax.experimental import pallas as pl
from jax.experimental.pallas import tpu as pltpu
from jax.sharding import PartitionSpec as P

f32 = jnp.float32
i32 = jnp.int32
bf16 = jnp.bfloat16

PROBES = 16
GROUPS = 8
ROWS = 4096
LANES = 128
PARTNERS = 6
FRINGE = 1024
HALF = 3 * FRINGE
SLOTS = PARTNERS * FRINGE
TILES = ROWS // LANES
WAYS = 8
SUMS = 4
QUARTER = SLOTS // 4
UNROLL = 16
ADD_UNROLL = 32

AXES = ("grid", "cell")

VMEM = pl.BlockSpec(memory_space=pltpu.VMEM)
HBM = pl.BlockSpec(memory_space=pl.ANY)
FIXED = pl.BlockSpec(memory_space=pltpu.HBM)


def aligned(start, size):
    return pl.ds(pl.multiple_of(start, size), size)


def rows_of(start, size):
    return pl.ds(pl.multiple_of(start, 8), size)


def split(x):
    high = x.astype(bf16)
    return high, (x - high.astype(f32)).astype(bf16)


def params(limit_mib):
    return pltpu.CompilerParams(vmem_limit_bytes=limit_mib << 20)


def cost(microseconds):
    return pl.CostEstimate(flops=0, transcendentals=0, bytes_accessed=microseconds * 3_000_000)


def resident(*shape):
    return pltpu.VMEM(shape, f32)


HEAD = 128


def segments(many, partners):
    return [(m, k) for m in range(many) for k in partners]


def index_scratch(segs):
    size = len(segs) * FRINGE // WAYS
    return [pltpu.SMEM((size,), i32)] * WAYS + [pltpu.SemaphoreType.DMA((3 * WAYS,))]


def index_copies(rows_hbm, segs, parts, sem):
    size = parts[0].shape[0]
    cuts = sorted({0, HEAD, size} | set(range(0, size, FRINGE)))
    phases = [[], []]
    for c in range(len(cuts) - 1):
        low, high = cuts[c], cuts[c + 1]
        for w in range(WAYS):
            seg, offset = divmod(w * size + low, FRINGE)
            start = segs[seg][0] * SLOTS + segs[seg][1] * FRINGE + offset
            copy = pltpu.make_async_copy(
                rows_hbm.at[pl.ds(start, high - low)], parts[w].at[pl.ds(low, high - low)], sem.at[c * WAYS + w]
            )
            copy.start()
            phases[min(c, 1)].append(copy)
    return phases


def finish(copies):
    for copy in copies:
        copy.wait()


def row_steps(parts, low, high, step):
    def outer(j, carry):
        for n in range(UNROLL):
            q = low + j * UNROLL + n
            for w in range(WAYS):
                step(w, q, parts[w][q])
        return carry

    lax.fori_loop(0, (high - low) // UNROLL, outer, 0)


def gather_rows(table, parts, staged, phases):
    count = parts[0].shape[0]

    def step(w, q, row):
        staged[pl.ds(w * count + q, 1), :] = table[pl.ds(row, 1), :]

    finish(phases[0])
    row_steps(parts, 0, HEAD, step)
    finish(phases[1])
    row_steps(parts, HEAD, count, step)


def clear(sums):
    def step(j, carry):
        for total in sums:
            for n in range(4):
                total[rows_of(j * 32 + n * 8, 8), :] = jnp.zeros((8, LANES), f32)
        return carry

    lax.fori_loop(0, ROWS // 32, step, 0)


def add_rows(sums, parts, staged):
    count = parts[0].shape[0]

    def outer(j, carry):
        for n in range(ADD_UNROLL):
            q = j * ADD_UNROLL + n
            for half in range(2):
                total = sums[half + n % 2 * 2]
                lists = [2 * m + half for m in range(4)]
                rows = [parts[w][q] for w in lists]
                old = [total[pl.ds(row, 1), :] for row in rows]
                new = [value + staged[pl.ds(w * count + q, 1), :] for value, w in zip(old, lists)]
                for row, value in zip(rows, new):
                    total[pl.ds(row, 1), :] = value
        return carry

    lax.fori_loop(0, count // ADD_UNROLL, outer, 0)


def groups_of(cells, m, offset):
    return jnp.broadcast_to(cells[m : m + 1, aligned(offset, LANES)], (8, LANES)) >> 12


def each_block(many, step):
    unroll = 8 // many

    def outer(j, carry):
        for n in range(unroll):
            step(j * unroll + n)
        return carry

    lax.fori_loop(0, FRINGE // LANES // unroll, outer, 0)


def select_fields(staged, cells, partners, weights, out):
    many = cells.shape[0]
    for n, k in enumerate(partners):

        def step(b):
            total = [jnp.zeros((8, LANES), f32)] * 2
            for m in range(many):
                field = staged[aligned((m * len(partners) + n) * FRINGE + b * LANES, LANES), :].T
                group = groups_of(cells, m, k * FRINGE + b * LANES)
                scale = 1.0
                if weights is not None:
                    ref, row, column = weights[k]
                    scale = ref[row + m : row + m + 1, aligned(column + b * LANES, LANES)]
                    scale = jnp.broadcast_to(scale, (8, LANES))
                for g in range(GROUPS):
                    factor = jnp.where(group == g, scale, 0.0)
                    for h in range(2):
                        at = g * PROBES + h * 8
                        total[h] = total[h] + field[at : at + 8, :] * factor
            ref, row, column = out[k]
            for h in range(2):
                ref[row + h * 8 : row + h * 8 + 8, aligned(column + b * LANES, LANES)] = total[h]

        each_block(many, step)


def spread_group(fields, cells, outs):
    group = [value >> 12 for value in cells]
    row = [value & (ROWS - 1) for value in cells]
    terms = [[jnp.where(group[m] == g, fields[m][h], 0.0) for g in range(GROUPS) for h in range(2)] for m in range(4)]
    for m in range(4):
        same = [row[m] == row[i] for i in range(m)]
        block = []
        for v in range(2 * GROUPS):
            value = terms[m][v]
            for i in range(m):
                value = value + jnp.where(same[i], terms[i][v], 0.0)
            block.append(value)
        ref, at = outs[m]
        ref[aligned(at, LANES), :] = jnp.concatenate(block, axis=0).T


def block_of(ref, row, column):
    return jnp.broadcast_to(ref[row : row + 1, aligned(column, LANES)], (8, LANES))


def field_of(place, b):
    ref, row, column = place
    return [ref[row + h * 8 : row + h * 8 + 8, aligned(column + b * LANES, LANES)] for h in range(2)]


def spread_at_donors(messages, cells, partners, weights, staged):
    for n, k in enumerate(partners):

        def step(b):
            field = field_of(messages[k], b)
            ref, row, column = weights[k]
            scale = [block_of(ref, row + m, column + b * LANES) for m in range(4)]
            fields = [[part * scale[m] for part in field] for m in range(4)]
            blocks = [block_of(cells, m, k * FRINGE + b * LANES) for m in range(4)]
            spread_group(fields, blocks, [(staged, (m * len(partners) + n) * FRINGE + b * LANES) for m in range(4)])

        each_block(4, step)


def spread_at_receptors(messages, cells, staged):
    for part in range(3):

        def step(j, carry):
            fields, blocks, outs = [], [], []
            for m in range(4):
                k, shift = divmod(m * QUARTER + part * 4 * LANES, FRINGE)
                fields.append(field_of(messages[k], j + shift // LANES))
                at = m * QUARTER + (part * 4 + j) * LANES
                blocks.append(block_of(cells, 0, at))
                outs.append((staged, at))
            spread_group(fields, blocks, outs)
            return carry

        lax.fori_loop(0, 4, step, 0, unroll=2)


def lanes(shape):
    return lax.broadcasted_iota(i32, shape, len(shape) - 1)


def fill_ends(padded, low, high):
    lane = lanes((1, LANES))
    before = pltpu.roll(padded[ROWS : ROWS + 8, :], PROBES, 1)[7:8, :]
    after = pltpu.roll(padded[8:16, :], LANES - PROBES, 1)[0:1, :]
    padded[7:8, :] = jnp.where(lane < PROBES, low, before)
    padded[ROWS + 8 : ROWS + 9, :] = jnp.where(lane >= LANES - PROBES, high, after)


def each_row_block(step):
    def outer(j, carry):
        for u in range(4):
            step(j * 32 + u * 8)
        return carry

    lax.fori_loop(0, ROWS // 32, outer, 0)


def table_kernel(probes, table, natural, sem):
    copies = [
        pltpu.make_async_copy(probes.at[p], natural.at[pl.ds(p, 1), :], sem.at[p]) for p in range(PROBES)
    ]
    for copy in copies:
        copy.start()
    finish(copies)

    def step(j, carry):
        for n in range(4):
            tile = j * 4 + n
            parts = [natural[:, aligned(g * ROWS + tile * LANES, LANES)] for g in range(GROUPS)]
            table[aligned(tile * LANES, LANES), :] = jnp.concatenate(parts, axis=0).T
        return carry

    lax.fori_loop(0, TILES // 4, step, 0)


def table_of(probes):
    return pl.pallas_call(
        table_kernel,
        out_shape=resident(ROWS, LANES),
        in_specs=[FIXED],
        out_specs=VMEM,
        scratch_shapes=[pltpu.VMEM((PROBES, GROUPS * ROWS), f32), pltpu.SemaphoreType.DMA((PROBES,))],
        compiler_params=params(60),
        cost_estimate=cost(3),
        name="table",
    )(probes)


BEFORE, SAME, AFTER = (0, 3), (1, 4), (2, 5)
SIDES = BEFORE + AFTER
NEAR, FAR = (0, 1, 2), (3, 4, 5)
EDGE = slice(FRINGE, FRINGE + LANES)


def weight_places(before, same, after):
    return {
        0: (before, 0, 0),
        3: (before, 4, 0),
        1: (same[0], 0, FRINGE),
        4: (same[1], 0, FRINGE),
        2: (after, 0, 0),
        5: (after, 4, 0),
    }


def pair_places(pair, ref):
    return {pair[0]: (ref, 0, 0), pair[1]: (ref, PROBES, 0)}


def grid_places(near, far):
    places = {k: (near, n * PROBES, 0) for n, k in enumerate(NEAR)}
    places.update({k: (far, n * PROBES, 0) for n, k in enumerate(FAR)})
    return places


def simple_call(kernel, out_shape, operands, name):
    return pl.pallas_call(
        kernel,
        out_shape=out_shape,
        in_specs=[VMEM] * len(operands),
        out_specs=[VMEM] * len(out_shape),
        compiler_params=params(8),
        cost_estimate=cost(1),
        name=name,
    )(*operands)


def weight_relay_kernel(near, far, table, up, down):
    for pair, out, rows in ((BEFORE, up, slice(ROWS - 8, ROWS)), (AFTER, down, slice(0, 8))):
        for n, ref in enumerate((near, far)):
            start = pair[0] * FRINGE
            out[n * 4 : n * 4 + 4, 0:FRINGE] = ref[:, start : start + FRINGE]
        out[:, EDGE] = table[rows, :]


def weight_relay(near, far, table):
    shape = jax.ShapeDtypeStruct((8, FRINGE + LANES), f32)
    return simple_call(weight_relay_kernel, [shape] * 2, (near, far, table), "weight_relay")


def rows_kernel(table, rows_hbm, staged, *rest):
    parts, sem = rest[:WAYS], rest[WAYS]
    gather_rows(table, parts, staged, index_copies(rows_hbm, segments(4, SIDES), parts, sem))


def rows_at_sides(table, rows):
    segs = segments(4, SIDES)
    return pl.pallas_call(
        rows_kernel,
        out_shape=resident(len(segs) * FRINGE, LANES),
        in_specs=[VMEM, HBM],
        out_specs=VMEM,
        scratch_shapes=index_scratch(segs),
        compiler_params=params(8),
        cost_estimate=cost(11),
        name="rows_at_sides",
    )(table, rows)


PAIR = jax.ShapeDtypeStruct((2 * PROBES, FRINGE), f32)
TRIPLE = jax.ShapeDtypeStruct((3 * PROBES, FRINGE), f32)


def side_sums_kernel(staged, cells, before, after, up, down):
    places = {**pair_places(AFTER, up), **pair_places(BEFORE, down)}
    select_fields(staged, cells, SIDES, weight_places(before, (None, None), after), places)


def side_sums(staged, cells, before, after):
    return simple_call(side_sums_kernel, [PAIR] * 2, (staged, cells, before, after), "side_sums")


def same_sums_kernel(table, cells, rows_hbm, near, far, out, staged, *rest):
    parts, sem = rest[:WAYS], rest[WAYS]
    gather_rows(table, parts, staged, index_copies(rows_hbm, segments(4, SAME), parts, sem))
    select_fields(staged, cells, SAME, weight_places(None, (near, far), None), pair_places(SAME, out))


def same_sums(table, cells, rows, near, far):
    segs = segments(4, SAME)
    return pl.pallas_call(
        same_sums_kernel,
        out_shape=PAIR,
        in_specs=[VMEM, VMEM, HBM, VMEM, VMEM],
        out_specs=VMEM,
        scratch_shapes=[pltpu.VMEM((len(segs) * FRINGE, LANES), f32)] + index_scratch(segs),
        compiler_params=params(8),
        cost_estimate=cost(8),
        name="same_sums",
    )(table, cells, rows, near, far)


def message_relay_kernel(before, same, after, near, far):
    for n, out in enumerate((near, far)):
        for i, ref in enumerate((before, same, after)):
            out[i * PROBES : (i + 1) * PROBES, :] = ref[n * PROBES : (n + 1) * PROBES, :]


def message_relay(before, same, after):
    return simple_call(message_relay_kernel, [TRIPLE] * 2, (before, same, after), "message_relay")


def end_flags():
    column = lax.axis_index("cell")
    return (column > 0).astype(f32), (column < lax.axis_size("cell") - 1).astype(f32)


def outer_rows(before, after):
    has_low, has_high = end_flags()
    low = pltpu.roll(before[0:8, EDGE], PROBES, 1)[7:8, :] * has_low
    high = pltpu.roll(after[0:8, EDGE], LANES - PROBES, 1)[0:1, :] * has_high
    return low, high


def forward_kernel(table, centre, lower, upper, before, after, c_out, l_out, u_out, *rest):
    sums, padded = rest[:SUMS], rest[SUMS]

    def step(j, carry):
        for n in range(2):
            tile = j * 2 + n
            at = aligned(tile * LANES, LANES)
            padded[rows_of(tile * LANES + 8, LANES), :] = table[at, :]
            for ref, out in ((centre, c_out), (lower, l_out), (upper, u_out)):
                parts = [
                    jnp.broadcast_to(ref[:, aligned(g * ROWS + tile * LANES, LANES)], (PROBES, LANES))
                    for g in range(GROUPS)
                ]
                out[at, :] = jnp.concatenate(parts, axis=0).T
        return carry

    lax.fori_loop(0, TILES // 2, step, 0)
    fill_ends(padded, *outer_rows(before, after))

    def stencil(start):
        at = rows_of(start, 8)
        sums[0][at, :] = (
            c_out[at, :] * padded[rows_of(start + 8, 8), :]
            - l_out[at, :] * padded[pl.ds(start + 7, 8), :]
            - u_out[at, :] * padded[pl.ds(start + 9, 8), :]
        )

    each_row_block(stencil)
    clear(sums[1:])


def forward(table, centre, lower, upper, before, after):
    return pl.pallas_call(
        forward_kernel,
        out_shape=[resident(ROWS, LANES)] * (3 + SUMS),
        in_specs=[VMEM] * 6,
        out_specs=[VMEM] * (3 + SUMS),
        scratch_shapes=[pltpu.VMEM((ROWS + 16, LANES), f32)],
        compiler_params=params(8),
        cost_estimate=cost(7),
        name="forward",
    )(table, centre, lower, upper, before, after)


def couple_kernel(cells, rows_hbm, near, far, *refs):
    refs = refs[SUMS:]
    tangent, out, sums = refs[0], refs[1], refs[2 : 2 + SUMS]
    staged, staged_far = refs[2 + SUMS : 4 + SUMS]
    refs = refs[4 + SUMS :]
    parts, sem, parts_far, sem_far = refs[:WAYS], refs[WAYS], refs[WAYS + 1 : 2 * WAYS + 1], refs[2 * WAYS + 1]
    every = NEAR + FAR
    phases = index_copies(rows_hbm, segments(1, every), parts, sem)
    phases_far = index_copies(rows_hbm, segments(1, FAR), parts_far, sem_far)
    spread_at_receptors(grid_places(near, far), cells, staged)
    finish(phases[0] + phases[1])
    add_rows(sums, parts, staged)

    def total(start):
        at = rows_of(start, 8)
        value = sums[0][at, :]
        for part in sums[1:]:
            value = value + part[at, :]
        tangent[at, :] = value

    each_row_block(total)
    gather_rows(tangent, parts_far, staged_far, phases_far)
    select_fields(staged_far, cells, FAR, None, grid_places(None, out))


def couple(cells, rows, near, far, sums):
    every, some = segments(1, NEAR + FAR), segments(1, FAR)
    outs = pl.pallas_call(
        couple_kernel,
        out_shape=[resident(ROWS, LANES), TRIPLE] + [resident(ROWS, LANES)] * SUMS,
        in_specs=[VMEM, HBM] + [VMEM] * (2 + SUMS),
        out_specs=[VMEM] * (2 + SUMS),
        scratch_shapes=[pltpu.VMEM((SLOTS, LANES), f32), pltpu.VMEM((SLOTS // 2, LANES), f32)]
        + index_scratch(every)
        + index_scratch(some),
        input_output_aliases={4 + w: 2 + w for w in range(SUMS)},
        compiler_params=params(8),
        cost_estimate=cost(11),
        name="couple",
    )(cells, rows, near, far, *sums)
    return outs[0], outs[1]


def receptor_kernel(tangent, cells, rows_hbm, out, staged, *rest):
    parts, sem = rest[:WAYS], rest[WAYS]
    gather_rows(tangent, parts, staged, index_copies(rows_hbm, segments(1, NEAR), parts, sem))
    select_fields(staged, cells, NEAR, None, grid_places(out, None))


def at_receptors(tangent, cells, rows):
    segs = segments(1, NEAR)
    return pl.pallas_call(
        receptor_kernel,
        out_shape=TRIPLE,
        in_specs=[VMEM, VMEM, HBM],
        out_specs=VMEM,
        scratch_shapes=[pltpu.VMEM((len(segs) * FRINGE, LANES), f32)] + index_scratch(segs),
        compiler_params=params(8),
        cost_estimate=cost(3),
        name="at_receptors",
    )(tangent, cells, rows)


def return_relay_kernel(near, far, tangent, lower, upper, ready, up, down):
    for n, ref in enumerate((near, far)):
        at = slice(n * PROBES, (n + 1) * PROBES)
        up[at, 0:FRINGE] = ref[0:PROBES, :]
        down[at, 0:FRINGE] = ref[2 * PROBES : 3 * PROBES, :]
    end = slice(ROWS - 8, ROWS)
    up[0:8, EDGE] = upper[end, :] * tangent[end, :]
    down[0:8, EDGE] = lower[0:8, :] * tangent[0:8, :]


def return_relay(near, far, tangent, lower, upper, ready):
    shape = jax.ShapeDtypeStruct((2 * PROBES, FRINGE + LANES), f32)
    return simple_call(return_relay_kernel, [shape] * 2, (near, far, tangent, lower, upper, ready), "return_relay")


def transposed_kernel(tangent, centre, lower, upper, ready, *rest):
    sums, raised, lowered = rest[:SUMS], rest[SUMS], rest[SUMS + 1]

    def products(start):
        at = rows_of(start, 8)
        value = tangent[at, :]
        raised[rows_of(start + 8, 8), :] = upper[at, :] * value
        lowered[rows_of(start + 8, 8), :] = lower[at, :] * value

    each_row_block(products)
    nothing = jnp.zeros((1, LANES), f32)
    fill_ends(raised, nothing, nothing)
    fill_ends(lowered, nothing, nothing)

    def stencil(start):
        at = rows_of(start, 8)
        sums[0][at, :] = (
            centre[at, :] * tangent[at, :] - raised[pl.ds(start + 7, 8), :] - lowered[pl.ds(start + 9, 8), :]
        )

    each_row_block(stencil)
    clear(sums[1:])


def transposed(tangent, centre, lower, upper, ready):
    return pl.pallas_call(
        transposed_kernel,
        out_shape=[resident(ROWS, LANES)] * SUMS,
        in_specs=[VMEM] * 5,
        out_specs=[VMEM] * SUMS,
        scratch_shapes=[pltpu.VMEM((ROWS + 16, LANES), f32)] * 2,
        compiler_params=params(8),
        cost_estimate=cost(1),
        name="transposed",
    )(tangent, centre, lower, upper, ready)


def donor_same_kernel(cells, rows_hbm, near_weights, far_weights, near, far, *refs):
    refs = refs[SUMS:]
    sums, staged, parts, sem = refs[:SUMS], refs[SUMS], refs[SUMS + 1 : SUMS + WAYS + 1], refs[SUMS + WAYS + 1]
    phases = index_copies(rows_hbm, segments(4, SAME), parts, sem)
    weights = weight_places(None, (near_weights, far_weights), None)
    spread_at_donors(grid_places(near, far), cells, SAME, weights, staged)
    finish(phases[0] + phases[1])
    add_rows(sums, parts, staged)


def add_same(cells, rows, near_weights, far_weights, near, far, sums):
    segs = segments(4, SAME)
    return pl.pallas_call(
        donor_same_kernel,
        out_shape=[resident(ROWS, LANES)] * SUMS,
        in_specs=[VMEM, HBM] + [VMEM] * (4 + SUMS),
        out_specs=[VMEM] * SUMS,
        scratch_shapes=[pltpu.VMEM((len(segs) * FRINGE, LANES), f32)] + index_scratch(segs),
        input_output_aliases={6 + w: w for w in range(SUMS)},
        compiler_params=params(8),
        cost_estimate=cost(9),
        name="add_same",
    )(cells, rows, near_weights, far_weights, near, far, *sums)


def sum_of_groups(value):
    for shift in (64, 32, 16):
        value = value + pltpu.roll(value, shift, 1)
    return value


def own_group():
    return lanes((8, LANES)) // PROBES == lax.broadcasted_iota(i32, (8, LANES), 0)


def donor_sides_kernel(cells, rows_hbm, before_weights, after_weights, before, after, *refs):
    refs = refs[SUMS:]
    adjoint, gram, sums, staged = refs[0], refs[1], refs[2 : 2 + SUMS], refs[2 + SUMS]
    parts, sem = refs[3 + SUMS : 3 + SUMS + WAYS], refs[3 + SUMS + WAYS]
    phases = index_copies(rows_hbm, segments(4, SIDES), parts, sem)
    weights = weight_places(before_weights, (None, None), after_weights)
    spread_at_donors({**pair_places(BEFORE, before), **pair_places(AFTER, after)}, cells, SIDES, weights, staged)
    finish(phases[0] + phases[1])
    add_rows(sums, parts, staged)
    lane = lanes((1, LANES))
    low, high = outer_rows(before, after)
    sums[0][0:1, :] = sums[0][0:1, :] - jnp.where(lane < PROBES, low, 0.0)
    end = sums[0][ROWS - 1 : ROWS, :]
    sums[0][ROWS - 1 : ROWS, :] = end - jnp.where(lane >= LANES - PROBES, high, 0.0)

    def total(start):
        at = rows_of(start, 8)
        value = sums[0][at, :]
        for part in sums[1:]:
            value = value + part[at, :]
        adjoint[at, :] = value

    each_row_block(total)

    def multiply(j, product):
        left_side, right_side = [], []
        for n in range(8):
            block = adjoint[aligned((j * 8 + n) * LANES, LANES), :]
            high, low = split(block)
            high_t, low_t = split(block.T)
            left_side += [high_t, high_t, low_t]
            right_side += [high, low, high]
        left_side = jnp.concatenate(left_side, axis=1)
        right_side = jnp.concatenate(right_side, axis=0)
        return product + jnp.dot(left_side, right_side, preferred_element_type=f32)

    product = lax.fori_loop(0, TILES // 8, multiply, jnp.zeros((LANES, LANES), f32))
    group = lanes((PROBES, LANES)) // PROBES
    folded = jnp.zeros((PROBES, LANES), f32)
    for g in range(GROUPS):
        folded = folded + jnp.where(group == g, product[g * PROBES : (g + 1) * PROBES, :], 0.0)
    folded = sum_of_groups(folded)
    for n in range(2):
        gram[:, n * LANES : (n + 1) * LANES] = jnp.sum(jnp.where(own_group(), folded[n * 8 : n * 8 + 8, :], 0.0), axis=0, keepdims=True)


def add_sides(cells, rows, before_weights, after_weights, before, after, sums):
    segs = segments(4, SIDES)
    outs = pl.pallas_call(
        donor_sides_kernel,
        out_shape=[resident(ROWS, LANES), jax.ShapeDtypeStruct((1, 2 * LANES), f32)]
        + [resident(ROWS, LANES)] * SUMS,
        in_specs=[VMEM, HBM] + [VMEM] * (4 + SUMS),
        out_specs=[VMEM] * (2 + SUMS),
        scratch_shapes=[pltpu.VMEM((len(segs) * FRINGE, LANES), f32)] + index_scratch(segs),
        input_output_aliases={6 + w: 2 + w for w in range(SUMS)},
        compiler_params=params(12),
        cost_estimate=cost(18),
        name="add_sides",
    )(cells, rows, before_weights, after_weights, before, after, *sums)
    return outs[0], outs[1]


def basis_kernel(total_cells, gram, adjoint, basis, factor, natural, sem):
    row = lax.broadcasted_iota(i32, (PROBES, LANES), 0)
    lane = lanes((PROBES, LANES))
    whole = jnp.concatenate(
        [sum_of_groups(jnp.where(own_group(), jnp.broadcast_to(gram[:, n * LANES : (n + 1) * LANES], (8, LANES)), 0.0)) for n in range(2)],
        axis=0,
    ) / f32(total_cells)
    columns = [jnp.broadcast_to(whole[:, j : j + 1], (PROBES, LANES)) for j in range(PROBES)]
    right = jnp.where(row == lane % PROBES, 1.0, 0.0)
    result = jnp.zeros((PROBES, LANES), f32)
    for j in range(PROBES):
        pivot = columns[j][j : j + 1, :]
        root = jnp.sqrt(pivot)
        ratio = jnp.where(row > j, columns[j] / pivot, 0.0)
        result = jnp.where((lane == j) & (row >= j), columns[j] / root, result)
        right_row = right[j : j + 1, :]
        right = jnp.where(row == j, right_row / root, right - ratio * right_row)
        for n in range(j + 1, PROBES):
            columns[n] = columns[n] - ratio * columns[n][j : j + 1, :]
    factor[...] = result[:, :PROBES]
    inverse = jnp.concatenate([right] * GROUPS, axis=0)
    same = lax.broadcasted_iota(i32, (LANES, LANES), 0) // PROBES == lanes((LANES, LANES)) // PROBES
    high, low = split(jnp.where(same, inverse, 0.0))
    left_side = jnp.concatenate([high, high, low], axis=1)

    def step(j, carry):
        for n in range(4):
            tile = j * 4 + n
            high, low = split(adjoint[aligned(tile * LANES, LANES), :])
            right_side = jnp.concatenate([high, low, high], axis=1)
            block = lax.dot_general(left_side, right_side, (((1,), (1,)), ((), ())), preferred_element_type=f32)
            for g in range(GROUPS):
                natural[:, aligned(g * ROWS + tile * LANES, LANES)] = block[g * PROBES : (g + 1) * PROBES, :]
        return carry

    copies = []
    for quarter in range(4):
        lax.fori_loop(quarter * TILES // 16, (quarter + 1) * TILES // 16, step, 0)
        for g in range(GROUPS):
            at = pl.ds(g * ROWS + quarter * ROWS // 4, ROWS // 4)
            copies.append(pltpu.make_async_copy(natural.at[:, at], basis.at[:, 0, at], sem.at[len(copies)]))
            copies[-1].start()
    finish(copies)


def basis_of(total_cells, gram, adjoint):
    return pl.pallas_call(
        functools.partial(basis_kernel, total_cells),
        out_shape=[
            jax.ShapeDtypeStruct((PROBES, 1, GROUPS * ROWS), f32),
            jax.ShapeDtypeStruct((PROBES, PROBES), f32),
        ],
        in_specs=[VMEM] * 2,
        out_specs=[FIXED, VMEM],
        scratch_shapes=[pltpu.VMEM((PROBES, GROUPS * ROWS), f32), pltpu.SemaphoreType.DMA((4 * GROUPS,))],
        compiler_params=params(8),
        cost_estimate=cost(6),
        name="basis",
    )(gram, adjoint)


def moved(value, place):
    grids, columns = (lax.axis_size(axis) for axis in AXES)
    route = []
    for g in range(grids):
        for c in range(columns):
            to_g, to_c = place(g, c)
            route.append((g * columns + c, (to_g % grids) * columns + to_c % columns))
    return lax.ppermute(value, AXES, route)


def along_grid(value, distance):
    return moved(value, lambda g, c: (g + distance, c))


def along_cell(value, distance):
    return moved(value, lambda g, c: (g, c + distance))


def summed(value):
    devices = lax.axis_size(AXES)
    copies = jnp.broadcast_to(value, (devices,) + value.shape)
    return jnp.sum(lax.all_to_all(copies, AXES, 0, 0), axis=0)


def body(probes, centre, lower_coef, upper_coef, donor_cells, receptor_cells, weights):
    donors = donor_cells[0]
    donor_rows = (donors & (ROWS - 1)).reshape(-1)
    receptor_rows = (receptor_cells & (ROWS - 1)).reshape(-1)
    half = SLOTS // 2
    near_weights, far_weights = along_grid(weights[0, :, :half], -1), along_grid(weights[0, :, half:], -2)
    table = table_of(probes)
    up, down = weight_relay(near_weights, far_weights, table)
    before_weights, after_weights = along_cell(up, 1), along_cell(down, -1)
    staged = rows_at_sides(table, donor_rows)
    up, down = side_sums(staged, donors, before_weights, after_weights)
    after, before = along_cell(up, 1), along_cell(down, -1)
    same = same_sums(table, donors, donor_rows, near_weights, far_weights)
    near, far = message_relay(before, same, after)
    near, far = along_grid(near, 1), along_grid(far, 2)
    c, l, u, *sums = forward(table, centre, lower_coef, upper_coef, before_weights, after_weights)
    tangent, far = couple(receptor_cells, receptor_rows, near, far, sums)
    far = along_grid(far, -2)
    near = along_grid(at_receptors(tangent, receptor_cells, receptor_rows), -1)
    sums = transposed(tangent, c, l, u, far)
    up, down = return_relay(near, far, tangent, l, u, sums[-1])
    before, after = along_cell(up, 1), along_cell(down, -1)
    sums = add_same(donors, donor_rows, near_weights, far_weights, near, far, sums)
    adjoint, gram = add_sides(donors, donor_rows, before_weights, after_weights, before, after, sums)
    total_cells = lax.axis_size("grid") * lax.axis_size("cell") * probes.shape[2]
    basis, factor = basis_of(total_cells, summed(gram), adjoint)
    return (basis, factor)


def solution(mesh):
    in_specs = (
        P(None, "grid", "cell"),
        P("grid", "cell"),
        P("grid", "cell"),
        P("grid", "cell"),
        P("grid", None, "cell"),
        P("grid", "cell"),
        P("grid", None, "cell"),
    )
    out_specs = (P(None, "grid", "cell"), P())
    return jax.shard_map(body, mesh=mesh, in_specs=in_specs, out_specs=out_specs, check_vma=False)
```
